32 devices in a mesh: groups: 2 (over x), user: 2 (over core), hist: 8 (over z, y).
Axes of the slice: x: 2, y: 2, z: 4, core: 2. Of those that a mesh axis runs over, the one named last changes fastest.
Arguments:
- item_table: bfloat16 [512, 1024], P('hist')
- item_ids: int32 [4, 512], P(('groups', 'user'), 'hist'), parts along dimension 0, may hold values from 0 to 511
- candidate_counts: int32 [4], P(('groups', 'user')), parts along dimension 0, may hold values from 256 to 512, as said below
- domain_ids: int32 [4, 512], P(('groups', 'user'), 'hist'), parts along dimension 0, may hold values from 0 to 1, as said below
- history_lengths: int32 [4], P(('groups', 'user')), parts along dimension 0, may hold values from 2048 to 4096, as said below
- history_keys: bfloat16 [4, 4096, 1024], P(('groups', 'user'), 'hist'), parts along dimension 0, may hold values from -9 to 9
- history_values: bfloat16 [4, 4096, 1024], P(('groups', 'user'), 'hist'), parts along dimension 0
- w_query: bfloat16 [1024, 1024], replicated, may hold values from -0.1875 to 0.1875
- w_gate: bfloat16 [1024, 1024], replicated, may hold values from -0.1875 to 0.1875
- w_out: bfloat16 [1024, 1024], replicated, may hold values from -0.1875 to 0.1875
- attn_gain: float32 [1024], replicated, may hold values from 0.1 to 1.9
- expert_weights: bfloat16 [2, 2, 1024, 1024], P('user'), may hold values from -0.1875 to 0.1875
Outputs:
- candidate_states: bfloat16 [4, 512, 1024], P(('groups', 'user'), 'hist'), parts along dimension 0
The draws below stay inside these ranges and needn't reach their ends.
There are 2 independent parts, one for each index of `groups`. The reference program is written for one: setup_inputs(seed, part) draws one part's arguments, and reference() takes and returns one part's arrays. A program takes and returns all parts, laid end to end along the dimension named above; an argument that names none is the same for every part. Nothing has to cross between parts.
Inputs may be any that keep to these rules, and one draw needn't show every extreme that they name: `candidate_counts`: slots at or past a user's count are padding; some user has 512. `history_lengths`: positions at or past a user's length are not attended; some user has 4096. `domain_ids`: in each aligned block of 64 slots of a user, at most 48 slots name one domain; in the first block of every user exactly 48 name the same domain.
All inputs are finite; a program needn't handle non-finite values.
Results may differ from the reference program's by a relative error of at most 0.0059.
Values may be sent and summed in bfloat16 or wider, within the bound.
No kernel may reach another device: no remote copies, remote signals or barrier semaphores. Data moves between devices by JAX's collectives and lax.ppermute only.
A program may use at most 64 MiB of HBM per device.

```python
import math
import jax
import jax.numpy as jnp
import numpy as np
from jax import lax

D = 1024
H = 8
HIST_DEV = 512
SLOT_DEV = 64
LAYERS = 2
CAP = 48
USERS = 2
EXPERTS = 2
HIST = 4096
SLOTS = 512
ITEMS = 512
N_HIST = 8


def scaled_pattern(key, shape, row_lo, row_hi, col_lo, col_hi):
    key_base, key_rows, key_cols = jax.random.split(key, 3)
    row_shape = shape[:-1] + (1,)
    col_shape = (1,) * (len(shape) - 1) + (shape[-1],)
    row_scale = jnp.exp(jax.random.uniform(key_rows, row_shape, jnp.float32, math.log(row_lo), math.log(row_hi)))
    col_scale = jnp.exp(jax.random.uniform(key_cols, col_shape, jnp.float32, math.log(col_lo), math.log(col_hi)))
    pattern = jax.random.normal(key_base, shape, jnp.float32)
    return pattern * row_scale * col_scale


def draw_item_table(key, part):
    return scaled_pattern(key, (ITEMS, D), 0.5, 2.0, 0.4, 4.0).astype(jnp.bfloat16)


def draw_history_values(key, part):
    return scaled_pattern(key, (USERS, HIST, D), 0.5, 2.0, 0.4, 4.0).astype(jnp.bfloat16)


def draw_candidate_counts(key, part):
    key_level, key_full = jax.random.split(key)
    counts = jax.random.randint(key_level, (USERS,), SLOTS // 2, SLOTS + 1)
    full_user = jax.random.randint(key_full, (), 0, USERS)
    return jnp.where(jnp.arange(USERS) == full_user, SLOTS, counts).astype(jnp.int32)


def draw_history_lengths(key, part):
    key_level, key_full = jax.random.split(key)
    lengths = jax.random.randint(key_level, (USERS,), HIST // 2, HIST + 1)
    full_user = jax.random.randint(key_full, (), 0, USERS)
    return jnp.where(jnp.arange(USERS) == full_user, HIST, lengths).astype(jnp.int32)


def draw_domain_ids(key, part):
    blocks = SLOTS // SLOT_DEV
    key_share, key_order, key_heavy = jax.random.split(key, 3)
    light_share = SLOT_DEV - CAP
    first_share = jax.random.randint(key_share, (USERS, blocks, 1), light_share, CAP + 1)
    heavy_domain = jax.random.randint(key_heavy, (), 0, 2)
    heavy_share = jnp.where(heavy_domain == 0, CAP, light_share)
    first_block = (jnp.arange(blocks, dtype=jnp.int32) == 0)[None, :, None]
    first_share = jnp.where(first_block, heavy_share, first_share)
    random_keys = jax.random.randint(key_order, (USERS, blocks, SLOT_DEV), 0, 1 << 20)
    distinct = random_keys * SLOT_DEV + jnp.arange(SLOT_DEV, dtype=jnp.int32)
    ordering = jnp.argsort(distinct, axis=-1, stable=True)
    position = jnp.argsort(ordering, axis=-1, stable=True)
    labels = jnp.where(position < first_share, 0, 1)
    return labels.reshape(USERS, SLOTS).astype(jnp.int32)


def touch_ends(array, own_key, smallest, top_value):
    spot = [jax.random.randint(jax.random.fold_in(own_key, axis), (), 0, length) for axis, length in enumerate(array.shape)]
    longest = array.shape.index(max(array.shape))
    beside = spot[:longest] + [(spot[longest] + 1) % array.shape[longest]] + spot[longest + 1:]
    return array.at[tuple(spot)].set(smallest).at[tuple(beside)].set(top_value)


def block_levels(rng, shape, cuts, smallest, high):
    loudness = 1.0
    for axis_at, blocks in cuts:
        steps = jax.random.uniform(jax.random.fold_in(jax.random.fold_in(rng, 6), axis_at), (blocks,), jnp.float32, smallest / len(cuts), high / len(cuts))
        loudness = loudness * jnp.repeat(jnp.exp(steps), shape[axis_at] // blocks).reshape((-1,) + (1,) * (len(shape) - 1 - axis_at))
    return loudness


def cumulative_ranks(count, slope):
    loads = [(1 << 20) // math.isqrt(standing ** slope) + 1 for standing in range(1, count + 1)]
    scale = 1 + sum(loads) // (1 << 30)
    return np.cumsum(np.array([max(1, weight // scale) for weight in loads]))


def skewed_ids(stream_key, dims, count, slope):
    listing = cumulative_ranks(count, slope)
    lot = jax.random.randint(jax.random.fold_in(stream_key, 1), dims, 0, int(listing[count - 1]))
    rank = jnp.searchsorted(jnp.asarray(listing, jnp.int32), lot, side="right")
    return jax.random.permutation(jax.random.fold_in(stream_key, 2), count)[rank].astype(jnp.int32)


def bell_draw(rng, extent, spread, limit, cuts=(), kind=jnp.bfloat16):
    values = spread * jax.random.normal(rng, extent, jnp.float32)
    if cuts:
        values = values * block_levels(rng, extent, cuts, -0.22, 0.18)
    return jnp.clip(values, -limit, limit).astype(kind)


def setup_inputs(seed: int = 0, part: int = 0) -> dict:
    key_of = jax.random.split(jax.random.key(seed), 13)
    part_splits = jax.random.split(jax.random.fold_in(key_of[12], part), 13)
    return {
        "item_table": draw_item_table(jax.random.fold_in(key_of[12], 71), part),
        "item_ids": touch_ends(skewed_ids(part_splits[1], (USERS, SLOTS), ITEMS, 2), jax.random.fold_in(part_splits[1], 3), 0, ITEMS - 1).astype(jnp.int32),
        "candidate_counts": draw_candidate_counts(jax.random.fold_in(jax.random.fold_in(key_of[12], part), 71), part),
        "domain_ids": draw_domain_ids(jax.random.fold_in(jax.random.fold_in(key_of[12], part), 71), part),
        "history_lengths": draw_history_lengths(jax.random.fold_in(jax.random.fold_in(key_of[12], part), 71), part),
        "history_keys": bell_draw(part_splits[5], (USERS, HIST, D), 1.5, 9.0, ((0, 2), (1, 8))),
        "history_values": draw_history_values(jax.random.fold_in(jax.random.fold_in(key_of[12], part), 71), part),
        "w_query": bell_draw(key_of[7], (D, D), D ** -0.5, 0.1875),
        "w_gate": bell_draw(key_of[8], (D, D), D ** -0.5, 0.1875),
        "w_out": bell_draw(key_of[9], (D, D), D ** -0.5, 0.1875),
        "attn_gain": jnp.clip(1.0 + 0.18 * jax.random.normal(key_of[10], (D,), jnp.float32), 0.1, 1.9),
        "expert_weights": bell_draw(key_of[11], (EXPERTS, LAYERS, D, D), D ** -0.5, 0.1875, ((0, 2),)),
    }


norm_eps = 1e-05

def rms_scale(matrix):
    return matrix * lax.rsqrt(lax.optimization_barrier(jnp.mean(matrix * matrix, axis=-1, keepdims=True)) + norm_eps)

def attend_local(query_rows, key_rows, value_rows, key_live):
    row_count = query_rows.shape[0]
    feat_width = query_rows.shape[1]
    head_size = feat_width // H
    query_heads = query_rows.astype(jnp.float32).reshape(row_count, H, head_size)
    key_heads = key_rows.astype(jnp.float32).reshape(key_rows.shape[0], H, head_size)
    value_heads = value_rows.astype(jnp.float32).reshape(value_rows.shape[0], H, head_size)
    scores = jnp.einsum('rhd,khd->hrk', query_heads, key_heads)
    weights = jnp.where(key_live[None, None, :], jax.nn.silu(scores * head_size ** (-0.5)), 0.0).astype(jnp.bfloat16)
    mixed_rows = jnp.einsum('hrk,khd->rhd', weights.astype(jnp.float32), value_heads)
    return mixed_rows.reshape(row_count, feat_width)

def reference(item_table, item_ids, candidate_counts, domain_ids, history_lengths, history_keys, history_values, w_query, w_gate, w_out, attn_gain, expert_weights):
    flat_ids = item_ids.reshape(-1).astype(jnp.int32)
    embedded = jnp.take(item_table, flat_ids, axis=0)
    embed_float = embedded.astype(jnp.float32)
    normed = rms_scale(embed_float).astype(jnp.bfloat16)
    queries = jnp.dot(normed, w_query, preferred_element_type=jnp.float32).astype(jnp.bfloat16)
    gating = jax.nn.silu(jnp.dot(normed, w_gate, preferred_element_type=jnp.float32))
    user_queries = queries.reshape(USERS, SLOTS, D)

    def user_attention(packed):
        query_rows, key_rows, value_rows, length = packed
        key_blocks = key_rows.reshape(N_HIST, HIST_DEV, D)
        value_blocks = value_rows.reshape(N_HIST, HIST_DEV, D)
        offsets = jnp.arange(N_HIST, dtype=jnp.int32) * HIST_DEV

        def add_block(running, block):
            key_block, value_block, offset = block
            key_live = offset + jnp.arange(HIST_DEV, dtype=jnp.int32) < length
            return (running + attend_local(query_rows, key_block, value_block, key_live), None)
        attended, leftover = lax.scan(add_block, jnp.zeros((SLOTS, D), jnp.float32), (key_blocks, value_blocks, offsets))
        return attended
    attended = lax.map(user_attention, (user_queries, history_keys, history_values, history_lengths)).reshape(USERS * SLOTS, D)
    gated_rows = (rms_scale(attended) * attn_gain * gating).astype(jnp.bfloat16)
    item_state = (embed_float + jnp.dot(gated_rows, w_out, preferred_element_type=jnp.float32)).astype(jnp.bfloat16)

    def expert_chain(layer_set):
        current = item_state
        for layer_index in range(LAYERS):
            lifted = jnp.dot(current, layer_set[layer_index], preferred_element_type=jnp.float32)
            current = (current.astype(jnp.float32) + jax.nn.silu(lifted)).astype(jnp.bfloat16)
        return current
    expert_outputs = lax.map(expert_chain, expert_weights)
    flat_domains = domain_ids.reshape(-1).astype(jnp.int32)
    picked = expert_outputs[flat_domains, jnp.arange(USERS * SLOTS, dtype=jnp.int32)]
    live = (jnp.arange(SLOTS, dtype=jnp.int32)[None, :] < candidate_counts[:, None]).reshape(-1)
    result = jnp.where(live[:, None], picked, jnp.zeros_like(picked))
    return result.reshape(USERS, SLOTS, D)
```

```python
import functools

import jax
import jax.numpy as jnp
from jax import lax
from jax.experimental import pallas as pl
from jax.experimental.pallas import tpu as pltpu
from jax.sharding import PartitionSpec as P

H = 8
LAYERS = 2
ID_ROWS = 16
ID_BASE = 128

norm_eps = 1e-05
F32 = jnp.float32
BF16 = jnp.bfloat16


def rms_scale(matrix):
    return matrix * lax.rsqrt(jnp.mean(matrix * matrix, axis=-1, keepdims=True) + norm_eps)


def swapped(value, flip):
    count = lax.axis_size("hist")
    return lax.ppermute(value, "hist", [(i, i ^ flip) for i in range(count)])


def swapped_by_user(value, flips):
    count = lax.axis_size("hist")
    pairs = [
        (u * count + i, u * count + (i ^ flip)) for u, flip in enumerate(flips) for i in range(count)
    ]
    return lax.ppermute(value, ("user", "hist"), pairs)


def from_user(value, steps):
    count = lax.axis_size("user")
    return lax.ppermute(value, "user", [((i + steps) % count, i) for i in range(count)])


def silu_half(half_scores):
    return half_scores + half_scores * jnp.tanh(half_scores)


def attend_kernel(live_ref, rows_ref, w_query_ref, keys_ref, values_ref, sums_ref):
    feat_width = rows_ref.shape[1]
    head_size = feat_width // H
    normed = rms_scale(rows_ref[...].astype(F32)).astype(BF16)
    queries = jnp.dot(normed, w_query_ref[...], preferred_element_type=F32).astype(BF16)
    place = lax.broadcasted_iota(jnp.int32, (values_ref.shape[1], head_size), 0)
    live = place < live_ref[0]
    for head in range(H):
        cut = slice(head * head_size, (head + 1) * head_size)
        scores = lax.dot_general(
            queries[:, cut], keys_ref[0, :, cut], (((1,), (1,)), ((), ())), preferred_element_type=F32
        )
        weights = silu_half(scores * (0.5 * head_size ** (-0.5))).astype(BF16)
        values = jnp.where(live, values_ref[0, :, cut].astype(F32), 0.0).astype(BF16)
        sums_ref[:, cut] = jnp.dot(weights, values, preferred_element_type=F32).astype(BF16)


def attend(rows, live_count, w_query, keys, values):
    return pl.pallas_call(
        attend_kernel,
        out_shape=jax.ShapeDtypeStruct(rows.shape, BF16),
        in_specs=[pl.BlockSpec(memory_space=pltpu.SMEM)] + [pl.BlockSpec(memory_space=pltpu.VMEM)] * 4,
        out_specs=pl.BlockSpec(memory_space=pltpu.VMEM),
        compiler_params=pltpu.CompilerParams(vmem_limit_bytes=48 * 1024 * 1024),
        cost_estimate=pl.CostEstimate(
            flops=2 * rows.shape[0] * rows.shape[1] * (rows.shape[1] + 2 * keys.shape[1]),
            bytes_accessed=2 * (keys.size + values.size + w_query.size + 2 * rows.size),
            transcendentals=rows.shape[0] * keys.shape[1] * H,
        ),
        name="attend",
    )(live_count, rows, w_query, keys, values)


def chosen(ids, items, table):
    onehot = (ids[:, None] == items[None, :]).astype(BF16)
    return jnp.dot(onehot, table, preferred_element_type=F32)


def on_device(
    item_table,
    item_ids,
    candidate_counts,
    domain_ids,
    history_lengths,
    history_keys,
    history_values,
    w_query,
    w_gate,
    w_out,
    attn_gain,
    expert_weights,
):
    slot_count = item_ids.shape[1]
    shard_rows, feat_width = item_table.shape
    hist_devices = lax.axis_size("hist")
    users = lax.axis_size("user")
    hist_index = lax.axis_index("hist")
    user_index = lax.axis_index("user")
    bits = hist_devices.bit_length() - 1

    expert_sets = [expert_weights[0]] + [from_user(expert_weights[0], s) for s in range(1, users)]

    own_ids = item_ids[0]
    digits = jnp.concatenate([own_ids // ID_BASE, own_ids % ID_BASE]).astype(BF16)
    by_turn = [digits] + [from_user(digits, s) for s in range(1, users)]
    by_turn = jnp.stack(by_turn)
    by_user = by_turn[(jnp.arange(users) - user_index) % users].reshape(1, -1)
    id_block = jnp.pad(by_user, ((0, ID_ROWS - 1), (0, feat_width - by_user.shape[1])))
    payload = jnp.concatenate([item_table, id_block], axis=0)

    whole = (hist_devices - 1) // users
    groups = [tuple(1 + users * g + u for u in range(users)) for g in range(whole)]
    rest = list(range(1 + users * whole, hist_devices))
    pieces = []
    for group in groups:
        pieces.append(swapped_by_user(payload, group))
    part_rows = shard_rows // users
    if rest:
        part = lax.dynamic_slice_in_dim(item_table, user_index * part_rows, part_rows, 0)
        part = jnp.concatenate([part, id_block], axis=0)
        for flip in rest:
            pieces.append(swapped(part, flip))
    fetched = jnp.concatenate(pieces, axis=0)
    traded = [fetched] + [from_user(fetched, s) for s in range(1, users)]

    row_sets = [item_table]
    item_sets = [hist_index * shard_rows + jnp.arange(shard_rows, dtype=jnp.int32)]
    ids_of = [[None] * users for _ in range(hist_devices)]
    ids_of[0] = [by_user[0]] * users
    for s, block in enumerate(traded):
        owner = (user_index + s) % users
        at = 0
        for group in groups:
            flip = 1 + users * (group[0] // users) + owner
            row_sets.append(block[at : at + shard_rows])
            item_sets.append((hist_index ^ flip) * shard_rows + jnp.arange(shard_rows, dtype=jnp.int32))
            for u in range(users):
                ids_of[group[u]][s] = (owner == u, block[at + shard_rows])
            at += shard_rows + ID_ROWS
        for flip in rest:
            row_sets.append(block[at : at + part_rows])
            item_sets.append(
                (hist_index ^ flip) * shard_rows + owner * part_rows + jnp.arange(part_rows, dtype=jnp.int32)
            )
            ids_of[flip][s] = (owner == 0, block[at + part_rows])
            at += part_rows + ID_ROWS
    table = jnp.concatenate(row_sets, axis=0)
    items = jnp.concatenate(item_sets)

    def ids_at(flip):
        if flip == 0:
            return own_ids
        row = ids_of[flip][0][1]
        for mine, other in ids_of[flip][1:]:
            row = jnp.where(mine, other, row)
        pair = lax.dynamic_slice_in_dim(row, user_index * 2 * slot_count, 2 * slot_count)
        pair = pair.astype(jnp.int32)
        return pair[:slot_count] * ID_BASE + pair[slot_count:]

    all_ids = jnp.stack([ids_at(flip) for flip in range(hist_devices)])

    live_count = jnp.clip(history_lengths - hist_index * history_keys.shape[1], 0, history_keys.shape[1])
    sums = attend(table, live_count.astype(jnp.int32), w_query, history_keys, history_values)

    orders = [list(range(bits)), list(range(bits))]
    if bits > 1:
        orders[1][:2] = [1, 0]
    width = feat_width // 2
    held = []
    for side, order in enumerate(orders):
        flips = [sum(((r >> (bits - 1 - t)) & 1) << bit for t, bit in enumerate(order)) for r in range(hist_devices)]
        ids = all_ids[jnp.array(flips)].reshape(-1)
        picked = chosen(ids, items, sums[:, side * width : (side + 1) * width]).astype(BF16)
        held.append(picked)

    def halved(kept, sent, flip):
        return kept.astype(F32) + swapped(sent, flip).astype(F32)

    for turn in range(bits - 1):
        for side, order in enumerate(orders):
            half = held[side].shape[0] // 2
            held[side] = halved(held[side][:half], held[side][half:].astype(BF16), 1 << order[turn])
    final = jnp.concatenate(held, axis=1)
    if bits:
        half = final.shape[0] // 2
        final = halved(final[:half], final[half:].astype(BF16), 1 << (bits - 1))
    attended = final.astype(F32)

    embed_float = chosen(own_ids, items, table)
    normed = rms_scale(embed_float).astype(BF16)
    gating = jax.nn.silu(jnp.dot(normed, w_gate, preferred_element_type=F32))
    gated_rows = (rms_scale(attended) * attn_gain * gating).astype(BF16)
    item_state = (embed_float + jnp.dot(gated_rows, w_out, preferred_element_type=F32)).astype(BF16)

    domains = domain_ids[0]
    slot_index = hist_index * slot_count + jnp.arange(slot_count, dtype=jnp.int32)
    cand_live = slot_index < candidate_counts[0]
    result = jnp.zeros(item_state.shape, BF16)
    for s, layer_weights in enumerate(expert_sets):
        current = item_state
        for layer_index in range(LAYERS):
            lifted = jnp.dot(current, layer_weights[layer_index], preferred_element_type=F32)
            current = (current.astype(F32) + jax.nn.silu(lifted)).astype(BF16)
        wanted = (domains == (user_index + s) % users) & cand_live
        result = jnp.where(wanted[:, None], current, result)
    return result[None]


def solution(mesh):
    in_specs = (
        P("hist", None),
        P(("groups", "user"), "hist"),
        P(("groups", "user")),
        P(("groups", "user"), "hist"),
        P(("groups", "user")),
        P(("groups", "user"), "hist", None),
        P(("groups", "user"), "hist", None),
        P(),
        P(),
        P(),
        P(),
        P("user", None, None, None),
    )
    out_specs = P(("groups", "user"), "hist", None)
    return jax.shard_map(
        on_device, mesh=mesh, in_specs=in_specs, out_specs=out_specs, check_vma=False
    )
```

```python
import functools

import jax
import jax.numpy as jnp
from jax import lax
from jax.experimental import pallas as pl
from jax.experimental.pallas import tpu as pltpu
from jax.sharding import PartitionSpec as P

H = 8
LAYERS = 2
VMEM_LIMIT = 24 * 1024 * 1024

norm_eps = 1e-05
F32 = jnp.float32
BF16 = jnp.bfloat16
ANY = pl.BlockSpec(memory_space=pl.ANY)
VMEM = pl.BlockSpec(memory_space=pltpu.VMEM)
SMEM = pl.BlockSpec(memory_space=pltpu.SMEM)


def rms_scale(matrix):
    return matrix * lax.rsqrt(jnp.mean(matrix * matrix, axis=-1, keepdims=True) + norm_eps)


def silu(value):
    half = 0.5 * value
    return half + half * jnp.tanh(half)


def swapped(value, flip):
    count = lax.axis_size("hist")
    return lax.ppermute(value, "hist", [(i, i ^ flip) for i in range(count)])


def swapped_by_user(value, flips):
    count = lax.axis_size("hist")
    pairs = [
        (u * count + i, u * count + (i ^ flip)) for u, flip in enumerate(flips) for i in range(count)
    ]
    return lax.ppermute(value, ("user", "hist"), pairs)


def from_user(value, steps):
    count = lax.axis_size("user")
    return lax.ppermute(value, "user", [((i + steps) % count, i) for i in range(count)])


def kernel_call(body, name, out_shapes, in_specs, scratch=(), flops=0, moved=0):
    return pl.pallas_call(
        body,
        out_shape=out_shapes,
        in_specs=in_specs,
        out_specs=[VMEM] * len(out_shapes),
        scratch_shapes=scratch,
        compiler_params=pltpu.CompilerParams(vmem_limit_bytes=VMEM_LIMIT),
        cost_estimate=pl.CostEstimate(flops=flops, bytes_accessed=moved, transcendentals=0),
        name=name,
    )


def attend_rows(row_refs, w_query_ref, keys_ref, values_ref, sums_ref):
    width = sums_ref.shape[1]
    head_size = width // H
    rows = jnp.concatenate([ref[...] for ref in row_refs], axis=0)
    normed = rms_scale(rows.astype(F32)).astype(BF16)
    queries = jnp.dot(normed, w_query_ref[...], preferred_element_type=F32).astype(BF16)
    for head in range(H):
        cut = slice(head * head_size, (head + 1) * head_size)
        scores = lax.dot_general(
            queries[:, cut], keys_ref[:, cut], (((1,), (1,)), ((), ())), preferred_element_type=F32
        )
        half = scores * (0.5 * head_size ** (-0.5))
        weights = (half + half * jnp.tanh(half)).astype(BF16)
        sums_ref[:, cut] = jnp.dot(weights, values_ref[:, cut], preferred_element_type=F32).astype(BF16)


def first_kernel(pieces, live_ref, w_query_hbm, keys_hbm, values_hbm, *refs):
    row_refs = refs[:pieces]
    sums_ref, w_query_ref, keys_ref, values_ref, sems = refs[pieces:]
    copies = [
        pltpu.make_async_copy(w_query_hbm, w_query_ref, sems.at[0]),
        pltpu.make_async_copy(keys_hbm.at[0], keys_ref, sems.at[1]),
        pltpu.make_async_copy(values_hbm.at[0], values_ref, sems.at[2]),
    ]
    for copy in copies:
        copy.start()
    for copy in copies:
        copy.wait()
    place = lax.broadcasted_iota(jnp.int32, values_ref.shape, 0)
    values_ref[...] = jnp.where(place < live_ref[0], values_ref[...].astype(F32), 0.0).astype(BF16)
    attend_rows(row_refs, w_query_ref, keys_ref, values_ref, sums_ref)


def next_kernel(pieces, w_query_ref, keys_ref, values_ref, *refs):
    attend_rows(refs[:pieces], w_query_ref, keys_ref, values_ref, refs[pieces])


def row_count(pieces):
    return sum(piece.shape[0] for piece in pieces)


def attend_cost(rows, width, history):
    return 2 * rows * width * (width + 2 * history)


def attend_first(pieces, live_count, w_query, keys, values):
    rows, width = row_count(pieces), w_query.shape[0]
    history = keys.shape[1]
    body = functools.partial(first_kernel, len(pieces))
    shapes = [(rows, width), w_query.shape, keys.shape[1:], values.shape[1:]]
    return kernel_call(
        body,
        "attend_first",
        [jax.ShapeDtypeStruct(shape, BF16) for shape in shapes],
        [SMEM, ANY, ANY, ANY] + [VMEM] * len(pieces),
        scratch=[pltpu.SemaphoreType.DMA((3,))],
        flops=attend_cost(rows, width, history),
        moved=4 * (w_query.size + keys.size + values.size),
    )(live_count, w_query, keys, values, *pieces)


def attend_next(pieces, w_query, keys, values):
    rows, width = row_count(pieces), w_query.shape[0]
    return kernel_call(
        functools.partial(next_kernel, len(pieces)),
        "attend_next",
        [jax.ShapeDtypeStruct((rows, width), BF16)],
        [VMEM] * (3 + len(pieces)),
        flops=attend_cost(rows, width, keys.shape[0]),
    )(w_query, keys, values, *pieces)[0]


def matches(layout, ids_row, hist_index, user_index, shard_rows):
    blocks = []
    for rows, steps, flips, split in layout:
        users = len(flips)
        owner = lax.rem(user_index + steps, users)
        flip = sum(jnp.where(owner == u, flip, 0) for u, flip in enumerate(flips))
        base = (hist_index ^ flip) * shard_rows + (owner * rows if split else 0)
        item = lax.broadcasted_iota(jnp.int32, (rows, ids_row.shape[1]), 0) + base
        blocks.append((item == ids_row).astype(F32).astype(BF16))
    return jnp.concatenate(blocks, axis=0)


TRANSPOSED = (((0,), (0,)), ((), ()))


def place_kernel(layout, orders, shard_rows, hist_axis, user_axis, ids_ref, first_ref, next_ref, *outs):
    slots = ids_ref.shape[1]
    ids_row = jnp.concatenate([ids_ref[flip : flip + 1, :] for flip in orders[0]], axis=1)
    onehot = matches(layout, ids_row, lax.axis_index(hist_axis), lax.axis_index(user_axis), shard_rows)
    width = first_ref.shape[1] // 2
    cut = first_ref.shape[0]
    for side, order in enumerate(orders):
        columns = slice(side * width, (side + 1) * width)
        sums = jnp.concatenate([first_ref[:, columns], next_ref[:, columns]], axis=0)
        placed = lax.dot_general(onehot, sums, TRANSPOSED, preferred_element_type=F32).astype(BF16)
        half = len(order) // 2
        for at, flip in enumerate(order):
            block = orders[0].index(flip)
            target = outs[2 * side + at // half]
            target[at % half * slots : (at % half + 1) * slots, :] = placed[block * slots : (block + 1) * slots, :]


def place(layout, orders, shard_rows, all_ids, first, following):
    devices, slots = all_ids.shape
    items = first.shape[0] + following.shape[0]
    width = first.shape[1]
    out = jax.ShapeDtypeStruct((devices * slots // 2, width // 2), BF16)
    body = functools.partial(place_kernel, layout, orders, shard_rows, "hist", "user")
    return kernel_call(
        body, "place", [out] * 4, [VMEM] * 3, flops=2 * items * devices * slots * width
    )(all_ids, first, following)


def prepare_kernel(pieces, layout, shard_rows, after_ref, ids_ref, w_gate_hbm, w_out_hbm, *refs):
    del after_ref
    users = len(layout[0][2])
    expert_hbm = refs[:users]
    row_refs = refs[users : users + pieces]
    refs = refs[users + pieces :]
    embed_ref, gating_ref, w_out_ref = refs[:3]
    expert_refs = refs[3 : 3 + users]
    w_gate_ref, sems = refs[3 + users :]
    copies = [
        pltpu.make_async_copy(source, target, sems.at[at])
        for at, (source, target) in enumerate(
            zip((w_gate_hbm, w_out_hbm) + expert_hbm, (w_gate_ref, w_out_ref) + expert_refs)
        )
    ]
    for copy in copies:
        copy.start()
    onehot = matches(layout, ids_ref[...], lax.axis_index("hist"), lax.axis_index("user"), shard_rows)
    table = jnp.concatenate([ref[...] for ref in row_refs], axis=0)
    embedded = lax.dot_general(onehot, table, TRANSPOSED, preferred_element_type=F32)
    embed_ref[...] = embedded
    normed = rms_scale(embedded).astype(BF16)
    copies[0].wait()
    gating_ref[...] = silu(jnp.dot(normed, w_gate_ref[...], preferred_element_type=F32))
    for copy in copies[1:]:
        copy.wait()


def prepare(layout, shard_rows, after, ids, w_gate, w_out, experts, pieces):
    slots, width = ids.shape[1], w_gate.shape[0]
    rows = jax.ShapeDtypeStruct((slots, width), F32)
    staged = [jax.ShapeDtypeStruct(part.shape, BF16) for part in (w_out, *experts)]
    moved = 2 * (w_gate.size + 2 * w_out.size + 2 * sum(part.size for part in experts))
    return kernel_call(
        functools.partial(prepare_kernel, len(pieces), layout, shard_rows),
        "prepare",
        [rows, rows, *staged],
        [ANY, VMEM, ANY, ANY] + [ANY] * len(experts) + [VMEM] * len(pieces),
        scratch=[pltpu.VMEM(w_gate.shape, BF16), pltpu.SemaphoreType.DMA((2 + len(experts),))],
        flops=2 * slots * width * (width + row_count(pieces)),
        moved=moved,
    )(after, ids, w_gate, w_out, *experts, *pieces)


def finish_kernel(users, kept_ref, come_ref, embed_ref, gating_ref, gain_ref, owner_ref, w_out_ref, *refs):
    expert_refs, out_ref = refs[:users], refs[users]
    attended = kept_ref[...] + come_ref[...].astype(F32)
    gated = (rms_scale(attended) * gain_ref[...] * gating_ref[...]).astype(BF16)
    mixed = jnp.dot(gated, w_out_ref[...], preferred_element_type=F32)
    state = (embed_ref[...] + mixed).astype(BF16)
    result = jnp.zeros(state.shape, F32)
    for steps, layers in enumerate(expert_refs):
        current = state
        for layer in range(LAYERS):
            lifted = jnp.dot(current, layers[layer], preferred_element_type=F32)
            current = (current.astype(F32) + silu(lifted)).astype(BF16)
        result = jnp.where(owner_ref[...] == steps, current.astype(F32), result)
    out_ref[0] = result.astype(BF16)


def finish(kept, come, embed, gating, gain, owner, w_out, experts):
    slots, width = kept.shape
    return kernel_call(
        functools.partial(finish_kernel, len(experts)),
        "finish",
        [jax.ShapeDtypeStruct((1, slots, width), BF16)],
        [VMEM] * (7 + len(experts)),
        flops=2 * slots * width * width * (1 + LAYERS * len(experts)),
    )(kept, come, embed, gating, gain, owner, w_out, *experts)[0]


def on_device(
    item_table,
    item_ids,
    candidate_counts,
    domain_ids,
    history_lengths,
    history_keys,
    history_values,
    w_query,
    w_gate,
    w_out,
    attn_gain,
    expert_weights,
):
    slot_count = item_ids.shape[1]
    shard_rows, feat_width = item_table.shape
    hist_devices = lax.axis_size("hist")
    users = lax.axis_size("user")
    hist_index = lax.axis_index("hist")
    user_index = lax.axis_index("user")
    bits = hist_devices.bit_length() - 1

    whole = (hist_devices - 1) // users
    flip_groups = [tuple(1 + users * g + u for u in range(users)) for g in range(whole)]
    flip_groups += [(flip,) * users for flip in range(1 + users * whole, hist_devices)]
    part_rows = shard_rows // users
    part = lax.dynamic_slice_in_dim(item_table, user_index * part_rows, part_rows, 0)
    pieces = [item_table]
    layout = [(shard_rows, 0, (0,) * users, False)]
    for flips in flip_groups:
        split = flips[0] == flips[-1]
        fetched = swapped_by_user(part if split else item_table, flips)
        for steps in range(users):
            pieces.append(from_user(fetched, steps) if steps else fetched)
            layout.append((fetched.shape[0], steps, flips, split))
    all_ids = item_ids
    for bit in range(bits):
        all_ids = jnp.concatenate([all_ids, swapped(all_ids, 1 << bit)], axis=0)

    own_layers = expert_weights[0]
    experts = [own_layers] + [from_user(own_layers, steps) for steps in range(1, users)]

    history = history_keys.shape[1]
    live_count = jnp.clip(history_lengths - hist_index * history, 0, history).astype(jnp.int32)
    early = 1 + users * (len(flip_groups) // 2)
    first, staged_query, staged_keys, staged_values = attend_first(
        pieces[:early], live_count, w_query, history_keys, history_values
    )
    following = attend_next(pieces[early:], staged_query, staged_keys, staged_values)

    turns = [list(range(bits)), list(range(bits))]
    if bits > 1:
        turns[1][:2] = [1, 0]
    orders = [
        [sum(((r >> (bits - 1 - t)) & 1) << bit for t, bit in enumerate(turn)) for r in range(hist_devices)]
        for turn in turns
    ]
    kept_a, sent_a, kept_b, sent_b = place(layout, orders, shard_rows, all_ids, first, following)
    held = [(kept_a, sent_a), (kept_b, sent_b)]
    embed, gating, staged_out, *staged_experts = prepare(
        layout, shard_rows, kept_a, item_ids, w_gate, w_out, experts, pieces
    )
    for at in range(bits - 1):
        for side, turn in enumerate(turns):
            kept, sent = held[side]
            total = kept.astype(F32) + swapped(sent, 1 << turn[at]).astype(F32)
            half = total.shape[0] // 2
            held[side] = (total[:half], total[half:].astype(BF16))
    kept = jnp.concatenate([pair[0] for pair in held], axis=1)
    sent = jnp.concatenate([pair[1] for pair in held], axis=1)
    come = swapped(sent, 1 << (bits - 1))

    slot_index = hist_index * slot_count + jnp.arange(slot_count, dtype=jnp.int32)
    steps_away = lax.rem(domain_ids[0] - user_index + users, users)
    owner = jnp.where(slot_index < candidate_counts[0], steps_away, -1)[:, None]
    return finish(kept, come, embed, gating, attn_gain[None], owner, staged_out, staged_experts)


def solution(mesh):
    in_specs = (
        P("hist", None),
        P(("groups", "user"), "hist"),
        P(("groups", "user")),
        P(("groups", "user"), "hist"),
        P(("groups", "user")),
        P(("groups", "user"), "hist", None),
        P(("groups", "user"), "hist", None),
        P(),
        P(),
        P(),
        P(),
        P("user", None, None, None),
    )
    out_specs = P(("groups", "user"), "hist", None)
    return jax.shard_map(
        on_device, mesh=mesh, in_specs=in_specs, out_specs=out_specs, check_vma=False
    )
```

```python
import functools

import jax
import jax.numpy as jnp
from jax import lax
from jax.experimental import pallas as pl
from jax.experimental.pallas import tpu as pltpu
from jax.sharding import PartitionSpec as P

H = 8
LAYERS = 2
VMEM_LIMIT = 24 * 1024 * 1024

norm_eps = 1e-05
F32 = jnp.float32
BF16 = jnp.bfloat16
ANY = pl.BlockSpec(memory_space=pl.ANY)
VMEM = pl.BlockSpec(memory_space=pltpu.VMEM)
SMEM = pl.BlockSpec(memory_space=pltpu.SMEM)
HBM = pl.BlockSpec(memory_space=pltpu.HBM)


def rms_scale(matrix):
    return matrix * lax.rsqrt(jnp.mean(matrix * matrix, axis=-1, keepdims=True) + norm_eps)


def silu(value):
    half = 0.5 * value
    return half + half * jnp.tanh(half)


def swapped(value, flip):
    count = lax.axis_size("hist")
    return lax.ppermute(value, "hist", [(i, i ^ flip) for i in range(count)])


def swapped_by_user(value, flips):
    count = lax.axis_size("hist")
    pairs = [
        (u * count + i, u * count + (i ^ flip)) for u, flip in enumerate(flips) for i in range(count)
    ]
    return lax.ppermute(value, ("user", "hist"), pairs)


def from_user(value, steps):
    count = lax.axis_size("user")
    return lax.ppermute(value, "user", [((i + steps) % count, i) for i in range(count)])


def kernel_call(body, name, out_shapes, in_specs, scratch=(), flops=0, moved=0):
    return pl.pallas_call(
        body,
        out_shape=out_shapes,
        in_specs=in_specs,
        out_specs=[VMEM] * len(out_shapes),
        scratch_shapes=scratch,
        compiler_params=pltpu.CompilerParams(vmem_limit_bytes=VMEM_LIMIT),
        cost_estimate=pl.CostEstimate(flops=flops, bytes_accessed=moved, transcendentals=0),
        name=name,
    )


def attend_rows(row_refs, w_query_ref, keys_ref, values_ref, sums_ref):
    width = sums_ref.shape[1]
    head_size = width // H
    rows = jnp.concatenate([ref[...] for ref in row_refs], axis=0)
    normed = rms_scale(rows.astype(F32)).astype(BF16)
    queries = jnp.dot(normed, w_query_ref[...], preferred_element_type=F32).astype(BF16)
    for head in range(H):
        cut = slice(head * head_size, (head + 1) * head_size)
        scores = lax.dot_general(
            queries[:, cut], keys_ref[0, :, cut], (((1,), (1,)), ((), ())), preferred_element_type=F32
        )
        half = scores * (0.5 * head_size ** (-0.5))
        weights = (half + half * jnp.tanh(half)).astype(BF16)
        sums_ref[:, cut] = jnp.dot(weights, values_ref[:, cut], preferred_element_type=F32).astype(BF16)


def own_kernel(live_ref, w_query_ref, keys_ref, values_ref, rows_ref, sums_ref, masked_ref):
    place = lax.broadcasted_iota(jnp.int32, masked_ref.shape, 0)
    masked_ref[...] = jnp.where(place < live_ref[0], values_ref[0].astype(F32), 0.0).astype(BF16)
    attend_rows([rows_ref], w_query_ref, keys_ref, masked_ref, sums_ref)


def next_kernel(pieces, w_query_ref, keys_ref, values_ref, *refs):
    attend_rows(refs[:pieces], w_query_ref, keys_ref, values_ref, refs[pieces])


def row_count(pieces):
    return sum(piece.shape[0] for piece in pieces)


def attend_cost(rows, width, history):
    return 2 * rows * width * (width + 2 * history)


def attend_own(rows, live_count, w_query, keys, values):
    shapes = [rows.shape, values.shape[1:]]
    return kernel_call(
        own_kernel,
        "attend_own",
        [jax.ShapeDtypeStruct(shape, BF16) for shape in shapes],
        [SMEM] + [VMEM] * 4,
        flops=attend_cost(rows.shape[0], rows.shape[1], keys.shape[1]),
    )(live_count, w_query, keys, values, rows)


def attend_next(pieces, w_query, keys, values):
    rows, width = row_count(pieces), w_query.shape[0]
    return kernel_call(
        functools.partial(next_kernel, len(pieces)),
        "attend_next",
        [jax.ShapeDtypeStruct((rows, width), BF16)],
        [VMEM] * (3 + len(pieces)),
        flops=attend_cost(rows, width, keys.shape[1]),
    )(w_query, keys, values, *pieces)[0]


def matches(layout, ids_row, hist_index, user_index, shard_rows):
    blocks = []
    for rows, steps, flips in layout:
        users = len(flips)
        owner = lax.rem(user_index + steps, users)
        flip = sum(jnp.where(owner == u, flip, 0) for u, flip in enumerate(flips))
        base = (hist_index ^ flip) * shard_rows
        item = lax.broadcasted_iota(jnp.int32, (rows, ids_row.shape[1]), 0) + base
        blocks.append((item == ids_row).astype(F32).astype(BF16))
    return jnp.concatenate(blocks, axis=0)


TRANSPOSED = (((0,), (0,)), ((), ()))


def place_kernel(layout, orders, shard_rows, parts, ids_ref, *refs):
    sums_refs, outs = refs[:parts], refs[parts:]
    slots = ids_ref.shape[1]
    ids_row = jnp.concatenate([ids_ref[flip : flip + 1, :] for flip in orders[0]], axis=1)
    onehot = matches(layout, ids_row, lax.axis_index("hist"), lax.axis_index("user"), shard_rows)
    width = sums_refs[0].shape[1] // 2
    for side, order in enumerate(orders):
        columns = slice(side * width, (side + 1) * width)
        sums = jnp.concatenate([ref[:, columns] for ref in sums_refs], axis=0)
        placed = lax.dot_general(onehot, sums, TRANSPOSED, preferred_element_type=F32).astype(BF16)
        half = len(order) // 2
        for at, flip in enumerate(order):
            block = orders[0].index(flip)
            target = outs[2 * side + at // half]
            target[at % half * slots : (at % half + 1) * slots, :] = placed[block * slots : (block + 1) * slots, :]


def place(layout, orders, shard_rows, all_ids, sums):
    devices, slots = all_ids.shape
    items, width = row_count(sums), sums[0].shape[1]
    out = jax.ShapeDtypeStruct((devices * slots // 2, width // 2), BF16)
    body = functools.partial(place_kernel, layout, orders, shard_rows, len(sums))
    return kernel_call(
        body, "place", [out] * 4, [VMEM] * (1 + len(sums)), flops=2 * items * devices * slots * width
    )(all_ids, *sums)


def prepare_kernel(layout, shard_rows, after_ref, ids_ref, w_gate_hbm, w_out_hbm, layers_hbm, *refs):
    del after_ref
    row_refs, refs = refs[: len(layout)], refs[len(layout) :]
    embed_ref, gating_ref, w_out_ref, layers_ref, w_gate_ref, sems = refs
    copies = [
        pltpu.make_async_copy(w_gate_hbm, w_gate_ref, sems.at[0]),
        pltpu.make_async_copy(w_out_hbm, w_out_ref, sems.at[1]),
        pltpu.make_async_copy(layers_hbm.at[0], layers_ref, sems.at[2]),
    ]
    for copy in copies:
        copy.start()
    onehot = matches(layout, ids_ref[...], lax.axis_index("hist"), lax.axis_index("user"), shard_rows)
    table = jnp.concatenate([ref[...] for ref in row_refs], axis=0)
    embedded = lax.dot_general(onehot, table, TRANSPOSED, preferred_element_type=F32)
    embed_ref[...] = embedded
    normed = rms_scale(embedded).astype(BF16)
    copies[0].wait()
    gating_ref[...] = silu(jnp.dot(normed, w_gate_ref[...], preferred_element_type=F32))
    for copy in copies[1:]:
        copy.wait()


def prepare(layout, shard_rows, after, ids, w_gate, w_out, expert_weights, pieces):
    slots, width = ids.shape[1], w_gate.shape[0]
    rows = jax.ShapeDtypeStruct((slots, width), F32)
    staged = [jax.ShapeDtypeStruct(shape, BF16) for shape in (w_out.shape, expert_weights.shape[1:])]
    return kernel_call(
        functools.partial(prepare_kernel, layout, shard_rows),
        "prepare",
        [rows, rows, *staged],
        [ANY, VMEM, HBM, HBM, HBM] + [VMEM] * len(pieces),
        scratch=[pltpu.VMEM(w_gate.shape, BF16), pltpu.SemaphoreType.DMA((3,))],
        flops=2 * slots * width * (width + row_count(pieces)),
        moved=2 * (w_gate.size + w_out.size + expert_weights.size),
    )(after, ids, w_gate, w_out, expert_weights, *pieces)


def finish_kernel(users, kept_ref, come_ref, embed_ref, gating_ref, gain_ref, live_ref, domain_ref, w_out_ref, *refs):
    expert_refs, out_ref = refs[:users], refs[users]
    attended = kept_ref[...] + come_ref[...].astype(F32)
    gated = (rms_scale(attended) * gain_ref[...] * gating_ref[...]).astype(BF16)
    mixed = jnp.dot(gated, w_out_ref[...], preferred_element_type=F32)
    state = (embed_ref[...] + mixed).astype(BF16)

    slots = state.shape[0]
    row_at = lax.broadcasted_iota(jnp.int32, (slots, slots), 0)
    lane_at = lax.broadcasted_iota(jnp.int32, (slots, slots), 1)
    steps_away = lax.rem(domain_ref[...] - lax.axis_index("user") + users, users)
    wanted = jnp.where(lane_at < live_ref[0], steps_away, -1)
    owner = jnp.sum(jnp.where(row_at == lane_at, wanted, 0).astype(F32), axis=1, keepdims=True)

    result = jnp.zeros(state.shape, F32)
    for steps, layers in enumerate(expert_refs):
        current = state
        for layer in range(LAYERS):
            lifted = jnp.dot(current, layers[layer], preferred_element_type=F32)
            current = (current.astype(F32) + silu(lifted)).astype(BF16)
        result = jnp.where(owner == steps, current.astype(F32), result)
    out_ref[0] = result.astype(BF16)


def finish(kept, come, embed, gating, gain, live_slots, domains, w_out, experts):
    slots, width = kept.shape
    return kernel_call(
        functools.partial(finish_kernel, len(experts)),
        "finish",
        [jax.ShapeDtypeStruct((1, slots, width), BF16)],
        [VMEM] * 5 + [SMEM] + [VMEM] * (2 + len(experts)),
        flops=2 * slots * width * width * (1 + LAYERS * len(experts)),
    )(kept, come, embed, gating, gain, live_slots, domains, w_out, *experts)[0]


def on_device(
    item_table,
    item_ids,
    candidate_counts,
    domain_ids,
    history_lengths,
    history_keys,
    history_values,
    w_query,
    w_gate,
    w_out,
    attn_gain,
    expert_weights,
):
    slot_count = item_ids.shape[1]
    shard_rows, feat_width = item_table.shape
    hist_devices = lax.axis_size("hist")
    users = lax.axis_size("user")
    hist_index = lax.axis_index("hist")
    user_index = lax.axis_index("user")
    bits = hist_devices.bit_length() - 1

    flip_groups = [tuple(range(at, min(at + users, hist_devices))) for at in range(1, hist_devices, users)]
    fetched = [swapped_by_user(item_table, flips) for flips in flip_groups]
    all_ids = item_ids
    for bit in range(bits):
        all_ids = jnp.concatenate([all_ids, swapped(all_ids, 1 << bit)], axis=0)

    def traded(block, flips):
        if len(flips) == users:
            return [from_user(block, steps) if steps else block for steps in range(users)]
        everyone = [from_user(block, steps) if steps else block for steps in range(users)]
        return [
            functools.reduce(
                lambda other, steps: jnp.where((user_index + steps) % users == u, everyone[steps], other),
                range(1, users),
                everyone[0],
            )
            for u in range(len(flips))
        ]

    def described(flips):
        if len(flips) == users:
            return [(shard_rows, steps, flips) for steps in range(users)]
        return [(shard_rows, 0, (flip,) * users) for flip in flips]

    history = history_keys.shape[1]
    live_count = jnp.clip(history_lengths - hist_index * history, 0, history).astype(jnp.int32)
    own, masked_values = attend_own(item_table, live_count, w_query, history_keys, history_values)
    sums, pieces, layout = [own], [item_table], [(shard_rows, 0, (0,) * users)]
    early = len(flip_groups) // 2
    for part in (slice(0, early), slice(early, None)):
        blocks = fetched[part]
        if part.start and early:
            *blocks, _ = lax.optimization_barrier((*blocks, sums[-1]))
        arrived = []
        for block, flips in zip(blocks, flip_groups[part]):
            arrived += traded(block, flips)
            layout += described(flips)
        if arrived:
            pieces += arrived
            sums.append(attend_next(arrived, w_query, history_keys, masked_values))

    turns = [list(range(bits)), list(range(bits))]
    if bits > 1:
        turns[1][:2] = [1, 0]
    orders = [
        [sum(((r >> (bits - 1 - t)) & 1) << bit for t, bit in enumerate(turn)) for r in range(hist_devices)]
        for turn in turns
    ]
    kept_a, sent_a, kept_b, sent_b = place(layout, orders, shard_rows, all_ids, sums)
    held = [(kept_a, sent_a), (kept_b, sent_b)]

    leaving, kept_a = lax.optimization_barrier((expert_weights[0], kept_a))
    other_layers = [from_user(leaving, steps) for steps in range(1, users)]
    embed, gating, staged_out, own_layers = prepare(
        layout, shard_rows, kept_a, item_ids, w_gate, w_out, expert_weights, pieces
    )
    for at in range(bits - 1):
        arriving = [swapped(held[side][1], 1 << turn[at]) for side, turn in enumerate(turns)]
        if at == 0:
            *arriving, embed = lax.optimization_barrier((*arriving, embed))
        for side in range(len(turns)):
            total = held[side][0].astype(F32) + arriving[side].astype(F32)
            half = total.shape[0] // 2
            held[side] = (total[:half], total[half:].astype(BF16))
    kept = jnp.concatenate([pair[0] for pair in held], axis=1)
    sent = jnp.concatenate([pair[1] for pair in held], axis=1)
    come = swapped(sent, 1 << (bits - 1))

    live_slots = candidate_counts - hist_index * slot_count
    return finish(kept, come, embed, gating, attn_gain[None], live_slots, domain_ids, staged_out, [own_layers] + other_layers)


def solution(mesh):
    in_specs = (
        P("hist", None),
        P(("groups", "user"), "hist"),
        P(("groups", "user")),
        P(("groups", "user"), "hist"),
        P(("groups", "user")),
        P(("groups", "user"), "hist", None),
        P(("groups", "user"), "hist", None),
        P(),
        P(),
        P(),
        P(),
        P("user", None, None, None),
    )
    out_specs = P(("groups", "user"), "hist", None)
    return jax.shard_map(
        on_device, mesh=mesh, in_specs=in_specs, out_specs=out_specs, check_vma=False
    )
```

```python
import functools

import jax
import jax.numpy as jnp
from jax import lax
from jax.experimental import pallas as pl
from jax.experimental.pallas import tpu as pltpu
from jax.sharding import PartitionSpec as P

H = 8
LAYERS = 2
ID_ROWS = 16
ID_BASE = 128
VMEM_LIMIT = 24 * 1024 * 1024
LOADS_BESIDE = 8 * 10**9

norm_eps = 1e-05
F32 = jnp.float32
BF16 = jnp.bfloat16
ANY = pl.BlockSpec(memory_space=pl.ANY)
VMEM = pl.BlockSpec(memory_space=pltpu.VMEM)
SMEM = pl.BlockSpec(memory_space=pltpu.SMEM)
TRANSPOSED = (((0,), (0,)), ((), ()))


def rms_scale(matrix):
    return matrix * lax.rsqrt(jnp.mean(matrix * matrix, axis=-1, keepdims=True) + norm_eps)


def silu(value):
    half = 0.5 * value
    return half + half * jnp.tanh(half)


def swapped(value, flip):
    count = lax.axis_size("hist")
    return lax.ppermute(value, "hist", [(i, i ^ flip) for i in range(count)])


def swapped_by_user(value, flips):
    count = lax.axis_size("hist")
    pairs = [
        (u * count + i, u * count + (i ^ flip)) for u, flip in enumerate(flips) for i in range(count)
    ]
    return lax.ppermute(value, ("user", "hist"), pairs)


def from_user(value, steps):
    count = lax.axis_size("user")
    return lax.ppermute(value, "user", [((i + steps) % count, i) for i in range(count)])


def kernel_call(body, name, out_shapes, in_specs, scratch=(), flops=0, moved=0):
    return pl.pallas_call(
        body,
        out_shape=out_shapes,
        in_specs=in_specs,
        out_specs=[VMEM] * len(out_shapes),
        scratch_shapes=scratch,
        compiler_params=pltpu.CompilerParams(vmem_limit_bytes=VMEM_LIMIT),
        cost_estimate=pl.CostEstimate(flops=flops, bytes_accessed=moved, transcendentals=0),
        name=name,
    )


def core_at(steps):
    return lax.rem(lax.axis_index("user") + steps, lax.axis_size("user"))


def of_core(core, arrivals):
    chosen = arrivals[0]
    for steps in range(1, len(arrivals)):
        chosen = jnp.where(core_at(steps) == core, arrivals[steps], chosen)
    return chosen


def blocks_of(piece, arrivals):
    _, steps, core = piece
    return arrivals[steps : steps + 1] if core is None else arrivals


def flip_of(piece):
    flips, steps, core = piece
    if core is not None:
        return flips[core]
    return sum(jnp.where(core_at(steps) == u, flip, 0) for u, flip in enumerate(flips))


def rows_of(pieces, refs):
    blocks, at = [], 0
    for piece in pieces:
        count = 1 if piece[2] is None else lax.axis_size("user")
        shards = [ref[: ref.shape[0] - ID_ROWS, :] for ref in refs[at : at + count]]
        blocks.append(shards[0] if piece[2] is None else of_core(piece[2], shards))
        at += count
    return jnp.concatenate(blocks, axis=0)


def ids_of(flips, refs, slots):
    rows = refs[0].shape[0] - ID_ROWS
    blocks = [ref[rows:, :slots].astype(F32) for ref in refs]
    row = lax.broadcasted_iota(jnp.int32, (ID_ROWS, slots), 0)
    high_row = 2 * core_at(0)
    weight = jnp.where(row == high_row, float(ID_BASE), jnp.where(row == high_row + 1, 1.0, 0.0))
    return {
        flip: jnp.sum(of_core(core, blocks) * weight, axis=0, keepdims=True).astype(jnp.int32)
        for core, flip in enumerate(flips)
    }


def matches(pieces, shard_rows, ids_row):
    hist_index = lax.axis_index("hist")
    blocks = []
    for piece in pieces:
        item = lax.broadcasted_iota(jnp.int32, (shard_rows, ids_row.shape[1]), 0)
        item += (hist_index ^ flip_of(piece)) * shard_rows
        blocks.append((item == ids_row).astype(F32).astype(BF16))
    return jnp.concatenate(blocks, axis=0)


def payload_kernel(rows_ref, own_ref, *refs):
    other_refs, out_ref = refs[:-1], refs[-1]
    rows, width = rows_ref.shape
    slots = own_ref.shape[1]
    out_ref[:rows, :] = rows_ref[...]
    row = lax.broadcasted_iota(jnp.int32, (ID_ROWS, slots), 0)
    digits = jnp.zeros((ID_ROWS, slots), jnp.int32)
    for steps, ref in enumerate((own_ref, *other_refs)):
        high_row = 2 * core_at(steps)
        high = ref[...] // ID_BASE
        digits = jnp.where(row == high_row, high, digits)
        digits = jnp.where(row == high_row + 1, ref[...] - high * ID_BASE, digits)
    out_ref[rows:, :] = jnp.zeros((ID_ROWS, width), BF16)
    out_ref[rows:, :slots] = digits.astype(F32).astype(BF16)


def payload_of(rows, ids, other_ids):
    return kernel_call(
        payload_kernel,
        "payload",
        [jax.ShapeDtypeStruct((rows.shape[0] + ID_ROWS, rows.shape[1]), BF16)],
        [VMEM] * (2 + len(other_ids)),
        flops=LOADS_BESIDE,
    )(rows, ids, *other_ids)[0]


def attend_rows(pieces, refs, w_query_ref, keys_ref, values_ref, sums_ref):
    width = sums_ref.shape[1]
    head_size = width // H
    rows = rows_of(pieces, refs)
    normed = rms_scale(rows.astype(F32)).astype(BF16)
    queries = jnp.dot(normed, w_query_ref[...], preferred_element_type=F32).astype(BF16)
    for head in range(H):
        cut = slice(head * head_size, (head + 1) * head_size)
        scores = lax.dot_general(
            queries[:, cut], keys_ref[0, :, cut], (((1,), (1,)), ((), ())), preferred_element_type=F32
        )
        half = scores * (0.5 * head_size ** (-0.5))
        weights = (half + half * jnp.tanh(half)).astype(BF16)
        sums_ref[:, cut] = jnp.dot(weights, values_ref[:, cut], preferred_element_type=F32).astype(BF16)


def first_kernel(pieces, length_ref, w_query_ref, keys_ref, values_ref, *refs):
    *refs, sums_ref, masked_ref = refs
    history = masked_ref.shape[0]
    place = lax.broadcasted_iota(jnp.int32, masked_ref.shape, 0) + lax.axis_index("hist") * history
    masked_ref[...] = jnp.where(place < length_ref[0], values_ref[0].astype(F32), 0.0).astype(BF16)
    attend_rows(pieces, refs, w_query_ref, keys_ref, masked_ref, sums_ref)


def next_kernel(pieces, w_query_ref, keys_ref, values_ref, *refs):
    *refs, sums_ref = refs
    attend_rows(pieces, refs, w_query_ref, keys_ref, values_ref, sums_ref)


def attend_cost(rows, width, history):
    return 2 * rows * width * (width + 2 * history)


def attend_first(pieces, blocks, shard_rows, lengths, w_query, keys, values):
    rows, width = len(pieces) * shard_rows, w_query.shape[0]
    return kernel_call(
        functools.partial(first_kernel, pieces),
        "attend_first",
        [jax.ShapeDtypeStruct((rows, width), BF16), jax.ShapeDtypeStruct(values.shape[1:], BF16)],
        [SMEM] + [VMEM] * (3 + len(blocks)),
        flops=attend_cost(rows, width, keys.shape[1]),
    )(lengths, w_query, keys, values, *blocks)


def attend_next(pieces, blocks, shard_rows, w_query, keys, values):
    rows, width = len(pieces) * shard_rows, w_query.shape[0]
    return kernel_call(
        functools.partial(next_kernel, pieces),
        "attend_next",
        [jax.ShapeDtypeStruct((rows, width), BF16)],
        [VMEM] * (3 + len(blocks)),
        flops=attend_cost(rows, width, keys.shape[1]),
    )(w_query, keys, values, *blocks)[0]


def place_kernel(pieces, all_flips, orders, parts, shard_rows, ids_ref, *refs):
    *refs, kept_a, sent_a, kept_b, sent_b = refs
    sums_refs, refs = refs[:parts], refs[parts:]
    slots, users = ids_ref.shape[1], lax.axis_size("user")
    ids = {0: ids_ref[...]}
    for at, flips in enumerate(all_flips):
        ids.update(ids_of(flips, refs[at * users : (at + 1) * users], slots))
    ids_row = jnp.concatenate([ids[flip] for flip in orders[0]], axis=1)
    onehot = matches(pieces, shard_rows, ids_row)
    width = sums_refs[0].shape[1] // 2
    for side, order in enumerate(orders):
        columns = slice(side * width, (side + 1) * width)
        sums = jnp.concatenate([ref[:, columns] for ref in sums_refs], axis=0)
        placed = lax.dot_general(onehot, sums, TRANSPOSED, preferred_element_type=F32).astype(BF16)
        half = len(order) // 2
        for at, flip in enumerate(order):
            block = orders[0].index(flip)
            target = ((kept_a, sent_a), (kept_b, sent_b))[side][at // half]
            target[at % half * slots : (at % half + 1) * slots, :] = placed[block * slots : (block + 1) * slots, :]


def place(pieces, groups, orders, shard_rows, ids, sums):
    devices, slots = len(orders[0]), ids.shape[1]
    width = sums[0].shape[1]
    out = jax.ShapeDtypeStruct((devices * slots // 2, width // 2), BF16)
    all_flips = [flips for flips, _ in groups]
    blocks = [block for _, arrivals in groups for block in arrivals]
    return kernel_call(
        functools.partial(place_kernel, pieces, all_flips, orders, len(sums), shard_rows),
        "place",
        [out] * 4,
        [VMEM] * (1 + len(sums) + len(blocks)),
        flops=2 * sum(part.shape[0] for part in sums) * devices * slots * width,
    )(ids, *sums, *blocks)


def fold_kernel(sides, *refs):
    ins, (kept_ref, sent_ref) = refs[: 2 * sides], refs[2 * sides :]
    half, width = ins[0].shape[0] // 2, ins[0].shape[1]
    for side in range(sides):
        total = ins[2 * side][...].astype(F32) + ins[2 * side + 1][...].astype(F32)
        columns = slice(side * width, (side + 1) * width)
        kept_ref[:, columns] = total[:half]
        sent_ref[:, columns] = total[half:].astype(BF16)


def fold(pairs):
    rows, width = pairs[0][0].shape
    shape = (rows // 2, width * len(pairs))
    blocks = [block for pair in pairs for block in pair]
    return kernel_call(
        functools.partial(fold_kernel, len(pairs)),
        "fold",
        [jax.ShapeDtypeStruct(shape, F32), jax.ShapeDtypeStruct(shape, BF16)],
        [VMEM] * len(blocks),
        moved=8 * rows * width * len(pairs),
    )(*blocks)


def prepare_kernel(pieces, after_ref, ids_ref, w_gate_ref, *refs):
    del after_ref
    *refs, embed_ref, gating_ref = refs
    table = rows_of(pieces, refs)
    onehot = matches(pieces, table.shape[0] // len(pieces), ids_ref[...])
    embedded = lax.dot_general(onehot, table, TRANSPOSED, preferred_element_type=F32)
    embed_ref[...] = embedded
    normed = rms_scale(embedded).astype(BF16)
    gating_ref[...] = silu(jnp.dot(normed, w_gate_ref[...], preferred_element_type=F32))


def prepare(pieces, blocks, shard_rows, after, ids, w_gate):
    slots, width = ids.shape[1], w_gate.shape[0]
    return kernel_call(
        functools.partial(prepare_kernel, pieces),
        "prepare",
        [jax.ShapeDtypeStruct((slots, width), F32)] * 2,
        [ANY, VMEM, VMEM] + [VMEM] * len(blocks),
        flops=2 * slots * width * (width + len(pieces) * shard_rows),
    )(after, ids, w_gate, *blocks)


def finish_kernel(kept_ref, come_ref, embed_ref, gating_ref, gain_ref, count_ref, domain_ref, w_out_ref, *refs):
    expert_refs, out_ref = refs[:-1], refs[-1]
    users = len(expert_refs)
    attended = kept_ref[...] + come_ref[...].astype(F32)
    gated = (rms_scale(attended) * gain_ref[...] * gating_ref[...]).astype(BF16)
    mixed = jnp.dot(gated, w_out_ref[...], preferred_element_type=F32)
    state = (embed_ref[...] + mixed).astype(BF16)

    slots = state.shape[0]
    row_at = lax.broadcasted_iota(jnp.int32, (slots, slots), 0)
    lane_at = lax.broadcasted_iota(jnp.int32, (slots, slots), 1)
    steps_away = lax.rem(domain_ref[...] - lax.axis_index("user") + users, users)
    live = lane_at + lax.axis_index("hist") * slots < count_ref[0]
    wanted = jnp.where(live, steps_away, -1)
    owner = jnp.sum(jnp.where(row_at == lane_at, wanted, 0).astype(F32), axis=1, keepdims=True)

    result = jnp.zeros(state.shape, F32)
    for steps, layers in enumerate(expert_refs):
        current = state
        for layer in range(LAYERS):
            lifted = jnp.dot(current, layers[0, layer], preferred_element_type=F32)
            current = (current.astype(F32) + silu(lifted)).astype(BF16)
        result = jnp.where(owner == steps, current.astype(F32), result)
    out_ref[0] = result.astype(BF16)


def finish(kept, come, embed, gating, gain, counts, domains, w_out, experts):
    slots, width = kept.shape
    return kernel_call(
        finish_kernel,
        "finish",
        [jax.ShapeDtypeStruct((1, slots, width), BF16)],
        [VMEM] * 5 + [SMEM] + [VMEM] * (2 + len(experts)),
        flops=2 * slots * width * width * (1 + LAYERS * len(experts)),
    )(kept, come, embed, gating, gain, counts, domains, w_out, *experts)[0]


def on_device(
    item_table,
    item_ids,
    candidate_counts,
    domain_ids,
    history_lengths,
    history_keys,
    history_values,
    w_query,
    w_gate,
    w_out,
    attn_gain,
    expert_weights,
):
    shard_rows = item_table.shape[0]
    hist_devices = lax.axis_size("hist")
    users = lax.axis_size("user")
    bits = hist_devices.bit_length() - 1
    others = range(1, users)

    payload = payload_of(item_table, item_ids, [from_user(item_ids, steps) for steps in others])
    all_flips = [tuple(range(at, min(at + users, hist_devices))) for at in range(1, hist_devices, users)]
    fetched = [swapped_by_user(payload, flips) for flips in all_flips]

    early = len(all_flips) // 2
    first_pieces = [((0,) * users, 0, None)] + [(flips, 0, None) for flips in all_flips[:early]]
    first_blocks = [payload] + fetched[:early]
    first, masked_values = attend_first(
        first_pieces, first_blocks, shard_rows, history_lengths, w_query, history_keys, history_values
    )
    first, *fetched = lax.optimization_barrier((first, *fetched))
    groups, next_pieces, next_blocks = [], [], []
    for at, (flips, block) in enumerate(zip(all_flips, fetched)):
        arrivals = [block] + [from_user(block, steps) for steps in others]
        groups.append((flips, arrivals))
        found = [(flips, steps, None) for steps in range(users)]
        if at < early:
            found = found[1:]
        elif len(flips) < users:
            found = [(flips, 0, core) for core in range(len(flips))]
        next_pieces += found
        next_blocks += [block for piece in found for block in blocks_of(piece, arrivals)]
    following = attend_next(next_pieces, next_blocks, shard_rows, w_query, history_keys, masked_values)
    pieces, blocks = first_pieces + next_pieces, first_blocks + next_blocks

    turns = [list(range(bits)), list(range(bits))]
    turns[1][:2] = [1, 0]
    orders = [
        [sum(((r >> (bits - 1 - t)) & 1) << bit for t, bit in enumerate(turn)) for r in range(hist_devices)]
        for turn in turns
    ]
    kept_a, sent_a, kept_b, sent_b = place(
        pieces, groups, orders, shard_rows, item_ids, [first, following]
    )
    embed, gating = prepare(pieces, blocks, shard_rows, kept_a, item_ids, w_gate)

    leaving, kept_a = lax.optimization_barrier((expert_weights, kept_a))
    experts = [expert_weights] + [from_user(leaving, steps) for steps in others]

    held = [(kept_a, sent_a), (kept_b, sent_b)]
    for at in range(bits - 1):
        arriving = [swapped(held[side][1], 1 << turn[at]) for side, turn in enumerate(turns)]
        if at == 0:
            *arriving, embed = lax.optimization_barrier((*arriving, embed))
        pairs = [(held[side][0], arriving[side]) for side in range(len(turns))]
        if at < bits - 2:
            held = [fold([pair]) for pair in pairs]
        else:
            kept, sent = fold(pairs)
    come = swapped(sent, 1 << (bits - 1))
    return finish(kept, come, embed, gating, attn_gain[None], candidate_counts, domain_ids, w_out, experts)


def solution(mesh):
    in_specs = (
        P("hist", None),
        P(("groups", "user"), "hist"),
        P(("groups", "user")),
        P(("groups", "user"), "hist"),
        P(("groups", "user")),
        P(("groups", "user"), "hist", None),
        P(("groups", "user"), "hist", None),
        P(),
        P(),
        P(),
        P(),
        P("user", None, None, None),
    )
    out_specs = P(("groups", "user"), "hist", None)
    return jax.shard_map(
        on_device, mesh=mesh, in_specs=in_specs, out_specs=out_specs, check_vma=False
    )
```

```python
import functools

import jax
import jax.numpy as jnp
from jax import lax
from jax.experimental import pallas as pl
from jax.experimental.pallas import tpu as pltpu
from jax.sharding import PartitionSpec as P

H = 8
LAYERS = 2
VMEM_LIMIT = 24 * 1024 * 1024
LOADS_BESIDE = 8 * 10**9

norm_eps = 1e-05
F32 = jnp.float32
BF16 = jnp.bfloat16
ANY = pl.BlockSpec(memory_space=pl.ANY)
VMEM = pl.BlockSpec(memory_space=pltpu.VMEM)
SMEM = pl.BlockSpec(memory_space=pltpu.SMEM)
TRANSPOSED = (((0,), (0,)), ((), ()))


def rms_scale(matrix):
    return matrix * lax.rsqrt(jnp.mean(matrix * matrix, axis=-1, keepdims=True) + norm_eps)


def silu(value):
    half = 0.5 * value
    return half + half * jnp.tanh(half)


def swapped(value, flip):
    count = lax.axis_size("hist")
    return lax.ppermute(value, "hist", [(i, i ^ flip) for i in range(count)])


def swapped_by_user(value, flips):
    count = lax.axis_size("hist")
    pairs = [
        (u * count + i, u * count + (i ^ flip)) for u, flip in enumerate(flips) for i in range(count)
    ]
    return lax.ppermute(value, ("user", "hist"), pairs)


def from_user(value, steps):
    count = lax.axis_size("user")
    return lax.ppermute(value, "user", [((i + steps) % count, i) for i in range(count)])


def kernel_call(body, name, out_shapes, in_specs, scratch=(), flops=0, moved=0):
    return pl.pallas_call(
        body,
        out_shape=out_shapes,
        in_specs=in_specs,
        out_specs=[VMEM] * len(out_shapes),
        scratch_shapes=scratch,
        compiler_params=pltpu.CompilerParams(vmem_limit_bytes=VMEM_LIMIT),
        cost_estimate=pl.CostEstimate(flops=flops, bytes_accessed=moved, transcendentals=0),
        name=name,
    )


def core_at(steps):
    return lax.rem(lax.axis_index("user") + steps, lax.axis_size("user"))


def of_core(core, arrivals):
    chosen = arrivals[0]
    for steps in range(1, len(arrivals)):
        chosen = jnp.where(core_at(steps) == core, arrivals[steps], chosen)
    return chosen


def blocks_of(piece, arrivals):
    _, steps, core = piece
    return arrivals[steps : steps + 1] if core is None else arrivals


def flip_of(piece):
    flips, steps, core = piece
    if core is not None:
        return flips[core]
    return sum(jnp.where(core_at(steps) == u, flip, 0) for u, flip in enumerate(flips))


def rows_of(pieces, refs):
    blocks, at = [], 0
    for piece in pieces:
        count = 1 if piece[2] is None else lax.axis_size("user")
        shards = [ref[...] for ref in refs[at : at + count]]
        blocks.append(shards[0] if piece[2] is None else of_core(piece[2], shards))
        at += count
    return jnp.concatenate(blocks, axis=0)


def matches(pieces, shard_rows, ids_row):
    hist_index = lax.axis_index("hist")
    blocks = []
    for piece in pieces:
        item = lax.broadcasted_iota(jnp.int32, (shard_rows, ids_row.shape[1]), 0)
        item += (hist_index ^ flip_of(piece)) * shard_rows
        blocks.append((item == ids_row).astype(F32).astype(BF16))
    return jnp.concatenate(blocks, axis=0)


def stack_kernel(*refs):
    *refs, out_ref = refs
    at = 0
    for ref in refs:
        out_ref[at : at + ref.shape[0], :] = ref[...]
        at += ref.shape[0]


def stack(blocks, flops=0):
    shape = (sum(block.shape[0] for block in blocks), blocks[0].shape[1])
    return kernel_call(
        stack_kernel, "stack", [jax.ShapeDtypeStruct(shape, blocks[0].dtype)], [VMEM] * len(blocks), flops=flops
    )(*blocks)[0]


def attend_rows(pieces, refs, w_query_ref, keys_ref, values_ref, sums_ref):
    width = sums_ref.shape[1]
    head_size = width // H
    rows = rows_of(pieces, refs)
    normed = rms_scale(rows.astype(F32)).astype(BF16)
    queries = jnp.dot(normed, w_query_ref[...], preferred_element_type=F32).astype(BF16)
    for head in range(H):
        cut = slice(head * head_size, (head + 1) * head_size)
        scores = lax.dot_general(
            queries[:, cut], keys_ref[0, :, cut], (((1,), (1,)), ((), ())), preferred_element_type=F32
        )
        half = scores * (0.5 * head_size ** (-0.5))
        weights = (half + half * jnp.tanh(half)).astype(BF16)
        sums_ref[:, cut] = jnp.dot(weights, values_ref[:, cut], preferred_element_type=F32).astype(BF16)


def first_kernel(pieces, length_ref, w_query_ref, keys_ref, values_ref, *refs):
    *refs, sums_ref, masked_ref = refs
    history = masked_ref.shape[0]
    place = lax.broadcasted_iota(jnp.int32, masked_ref.shape, 0) + lax.axis_index("hist") * history
    masked_ref[...] = jnp.where(place < length_ref[0], values_ref[0].astype(F32), 0.0).astype(BF16)
    attend_rows(pieces, refs, w_query_ref, keys_ref, masked_ref, sums_ref)


def next_kernel(pieces, w_query_ref, keys_ref, values_ref, *refs):
    *refs, sums_ref = refs
    attend_rows(pieces, refs, w_query_ref, keys_ref, values_ref, sums_ref)


def attend_cost(rows, width, history):
    return 2 * rows * width * (width + 2 * history)


def attend_first(pieces, blocks, shard_rows, lengths, w_query, keys, values):
    rows, width = len(pieces) * shard_rows, w_query.shape[0]
    return kernel_call(
        functools.partial(first_kernel, pieces),
        "attend_first",
        [jax.ShapeDtypeStruct((rows, width), BF16), jax.ShapeDtypeStruct(values.shape[1:], BF16)],
        [SMEM] + [VMEM] * (3 + len(blocks)),
        flops=attend_cost(rows, width, keys.shape[1]),
    )(lengths, w_query, keys, values, *blocks)


def attend_next(pieces, blocks, shard_rows, w_query, keys, values):
    rows, width = len(pieces) * shard_rows, w_query.shape[0]
    return kernel_call(
        functools.partial(next_kernel, pieces),
        "attend_next",
        [jax.ShapeDtypeStruct((rows, width), BF16)],
        [VMEM] * (3 + len(blocks)),
        flops=attend_cost(rows, width, keys.shape[1]),
    )(w_query, keys, values, *blocks)[0]


def place_kernel(pieces, id_flips, orders, shard_rows, near_ids_ref, far_ids_ref, *refs):
    *sums_refs, kept_a, sent_a, kept_b, sent_b = refs
    half, slots = near_ids_ref.shape
    rows = [id_flips.index(flip) for flip in orders[0]]
    refs_rows = [(near_ids_ref, row) if row < half else (far_ids_ref, row - half) for row in rows]
    ids_row = jnp.concatenate([ref[row : row + 1, :] for ref, row in refs_rows], axis=1)
    onehot = matches(pieces, shard_rows, ids_row)
    width = sums_refs[0].shape[1] // 2
    for side, order in enumerate(orders):
        columns = slice(side * width, (side + 1) * width)
        sums = jnp.concatenate([ref[:, columns] for ref in sums_refs], axis=0)
        placed = lax.dot_general(onehot, sums, TRANSPOSED, preferred_element_type=F32).astype(BF16)
        half = len(order) // 2
        for at, flip in enumerate(order):
            block = orders[0].index(flip)
            target = ((kept_a, sent_a), (kept_b, sent_b))[side][at // half]
            target[at % half * slots : (at % half + 1) * slots, :] = placed[block * slots : (block + 1) * slots, :]


def place(pieces, id_flips, orders, shard_rows, near_ids, far_ids, sums):
    devices, slots = len(orders[0]), near_ids.shape[1]
    width = sums[0].shape[1]
    out = jax.ShapeDtypeStruct((devices * slots // 2, width // 2), BF16)
    return kernel_call(
        functools.partial(place_kernel, pieces, id_flips, orders, shard_rows),
        "place",
        [out] * 4,
        [VMEM] * (2 + len(sums)),
        flops=2 * sum(part.shape[0] for part in sums) * devices * slots * width,
    )(near_ids, far_ids, *sums)


def fold_kernel(sides, *refs):
    ins, (kept_ref, sent_ref) = refs[: 2 * sides], refs[2 * sides :]
    half, width = ins[0].shape[0] // 2, ins[0].shape[1]
    for side in range(sides):
        total = ins[2 * side][...].astype(F32) + ins[2 * side + 1][...].astype(F32)
        columns = slice(side * width, (side + 1) * width)
        kept_ref[:, columns] = total[:half]
        sent_ref[:, columns] = total[half:].astype(BF16)


def fold(pairs):
    rows, width = pairs[0][0].shape
    shape = (rows // 2, width * len(pairs))
    blocks = [block for pair in pairs for block in pair]
    return kernel_call(
        functools.partial(fold_kernel, len(pairs)),
        "fold",
        [jax.ShapeDtypeStruct(shape, F32), jax.ShapeDtypeStruct(shape, BF16)],
        [VMEM] * len(blocks),
        moved=8 * rows * width * len(pairs),
    )(*blocks)


def prepare_kernel(pieces, after_ref, ids_ref, w_gate_ref, *refs):
    del after_ref
    *refs, embed_ref, gating_ref = refs
    table = rows_of(pieces, refs)
    onehot = matches(pieces, table.shape[0] // len(pieces), ids_ref[...])
    embedded = lax.dot_general(onehot, table, TRANSPOSED, preferred_element_type=F32)
    embed_ref[...] = embedded
    normed = rms_scale(embedded).astype(BF16)
    gating_ref[...] = silu(jnp.dot(normed, w_gate_ref[...], preferred_element_type=F32))


def prepare(pieces, blocks, shard_rows, after, ids, w_gate):
    slots, width = ids.shape[1], w_gate.shape[0]
    return kernel_call(
        functools.partial(prepare_kernel, pieces),
        "prepare",
        [jax.ShapeDtypeStruct((slots, width), F32)] * 2,
        [ANY, VMEM, VMEM] + [VMEM] * len(blocks),
        flops=2 * slots * width * (width + len(pieces) * shard_rows),
    )(after, ids, w_gate, *blocks)


def finish_kernel(kept_ref, come_ref, embed_ref, gating_ref, gain_ref, count_ref, domain_ref, w_out_ref, *refs):
    expert_refs, out_ref = refs[:-1], refs[-1]
    users = len(expert_refs)
    attended = kept_ref[...] + come_ref[...].astype(F32)
    gated = (rms_scale(attended) * gain_ref[...] * gating_ref[...]).astype(BF16)
    mixed = jnp.dot(gated, w_out_ref[...], preferred_element_type=F32)
    state = (embed_ref[...] + mixed).astype(BF16)

    slots = state.shape[0]
    row_at = lax.broadcasted_iota(jnp.int32, (slots, slots), 0)
    lane_at = lax.broadcasted_iota(jnp.int32, (slots, slots), 1)
    steps_away = lax.rem(domain_ref[...] - lax.axis_index("user") + users, users)
    live = lane_at + lax.axis_index("hist") * slots < count_ref[0]
    wanted = jnp.where(live, steps_away, -1)
    owner = jnp.sum(jnp.where(row_at == lane_at, wanted, 0).astype(F32), axis=1, keepdims=True)

    result = jnp.zeros(state.shape, F32)
    for steps, layers in enumerate(expert_refs):
        current = state
        for layer in range(LAYERS):
            lifted = jnp.dot(current, layers[0, layer], preferred_element_type=F32)
            current = (current.astype(F32) + silu(lifted)).astype(BF16)
        result = jnp.where(owner == steps, current.astype(F32), result)
    out_ref[0] = result.astype(BF16)


def finish(kept, come, embed, gating, gain, counts, domains, w_out, experts):
    slots, width = kept.shape
    return kernel_call(
        finish_kernel,
        "finish",
        [jax.ShapeDtypeStruct((1, slots, width), BF16)],
        [VMEM] * 5 + [SMEM] + [VMEM] * (2 + len(experts)),
        flops=2 * slots * width * width * (1 + LAYERS * len(experts)),
    )(kept, come, embed, gating, gain, counts, domains, w_out, *experts)[0]


def on_device(
    item_table,
    item_ids,
    candidate_counts,
    domain_ids,
    history_lengths,
    history_keys,
    history_values,
    w_query,
    w_gate,
    w_out,
    attn_gain,
    expert_weights,
):
    shard_rows = item_table.shape[0]
    hist_devices = lax.axis_size("hist")
    users = lax.axis_size("user")
    bits = hist_devices.bit_length() - 1
    others = range(1, users)

    all_flips = [tuple(range(at, min(at + users, hist_devices))) for at in range(1, hist_devices, users)]
    fetched = [swapped_by_user(item_table, flips) for flips in all_flips]

    known_ids, id_flips = [stack([item_ids], flops=LOADS_BESIDE)], [0]
    for bit in reversed(range(bits)):
        far_ids = swapped(known_ids[-1], 1 << bit)
        id_flips += [flip + (1 << bit) for flip in id_flips]
        if bit:
            known_ids.append(stack([known_ids[-1], far_ids]))
    near_ids = known_ids[-1]

    early = len(all_flips) // 2
    first_pieces = [((0,) * users, 0, None)] + [(flips, 0, None) for flips in all_flips[:early]]
    first_blocks = [item_table] + fetched[:early]
    w_query, _ = lax.optimization_barrier((w_query, known_ids[1]))
    first, masked_values = attend_first(
        first_pieces, first_blocks, shard_rows, history_lengths, w_query, history_keys, history_values
    )
    first, *fetched[:early] = lax.optimization_barrier((first, *fetched[:early]))
    first, near_ids, *fetched[early:] = lax.optimization_barrier((first, near_ids, *fetched[early:]))
    next_pieces, next_blocks = [], []
    for at, (flips, block) in enumerate(zip(all_flips, fetched)):
        arrivals = [block] + [from_user(block, steps) for steps in others]
        found = [(flips, steps, None) for steps in range(users)]
        if at < early:
            found = found[1:]
        elif len(flips) < users:
            found = [(flips, 0, core) for core in range(len(flips))]
        next_pieces += found
        next_blocks += [block for piece in found for block in blocks_of(piece, arrivals)]
    following = attend_next(next_pieces, next_blocks, shard_rows, w_query, history_keys, masked_values)
    pieces, blocks = first_pieces + next_pieces, first_blocks + next_blocks

    turns = [list(range(bits)), list(range(bits))]
    turns[1][:2] = [1, 0]
    orders = [
        [sum(((r >> (bits - 1 - t)) & 1) << bit for t, bit in enumerate(turn)) for r in range(hist_devices)]
        for turn in turns
    ]
    kept_a, sent_a, kept_b, sent_b = place(
        pieces, id_flips, orders, shard_rows, near_ids, far_ids, [first, following]
    )
    embed, gating = prepare(pieces, blocks, shard_rows, kept_a, item_ids, w_gate)

    leaving, kept_a = lax.optimization_barrier((expert_weights, kept_a))
    experts = [expert_weights] + [from_user(leaving, steps) for steps in others]

    held = [(kept_a, sent_a), (kept_b, sent_b)]
    for at in range(bits - 1):
        arriving = [swapped(held[side][1], 1 << turn[at]) for side, turn in enumerate(turns)]
        if at == 0:
            *arriving, embed = lax.optimization_barrier((*arriving, embed))
        pairs = [(held[side][0], arriving[side]) for side in range(len(turns))]
        if at < bits - 2:
            held = [fold([pair]) for pair in pairs]
        else:
            kept, sent = fold(pairs)
    come = swapped(sent, 1 << (bits - 1))
    return finish(kept, come, embed, gating, attn_gain[None], candidate_counts, domain_ids, w_out, experts)


def solution(mesh):
    in_specs = (
        P("hist", None),
        P(("groups", "user"), "hist"),
        P(("groups", "user")),
        P(("groups", "user"), "hist"),
        P(("groups", "user")),
        P(("groups", "user"), "hist", None),
        P(("groups", "user"), "hist", None),
        P(),
        P(),
        P(),
        P(),
        P("user", None, None, None),
    )
    out_specs = P(("groups", "user"), "hist", None)
    return jax.shard_map(
        on_device, mesh=mesh, in_specs=in_specs, out_specs=out_specs, check_vma=False
    )
```

```python
import functools

import jax
import jax.numpy as jnp
from jax import lax
from jax.experimental import pallas as pl
from jax.experimental.pallas import tpu as pltpu
from jax.sharding import PartitionSpec as P

H = 8
LAYERS = 2
VMEM_LIMIT = 24 * 1024 * 1024
LOADS_BESIDE = 8 * 10**9

norm_eps = 1e-05
F32 = jnp.float32
BF16 = jnp.bfloat16
ANY = pl.BlockSpec(memory_space=pl.ANY)
VMEM = pl.BlockSpec(memory_space=pltpu.VMEM)
SMEM = pl.BlockSpec(memory_space=pltpu.SMEM)
TRANSPOSED = (((0,), (0,)), ((), ()))


def rms_scale(matrix):
    return matrix * lax.rsqrt(jnp.mean(matrix * matrix, axis=-1, keepdims=True) + norm_eps)


def silu(value):
    half = 0.5 * value
    return half + half * jnp.tanh(half)


def swapped(value, flip):
    count = lax.axis_size("hist")
    return lax.ppermute(value, "hist", [(i, i ^ flip) for i in range(count)])


def swapped_by_user(value, flips):
    count = lax.axis_size("hist")
    pairs = [
        (u * count + i, u * count + (i ^ flip)) for u, flip in enumerate(flips) for i in range(count)
    ]
    return lax.ppermute(value, ("user", "hist"), pairs)


def from_user(value, steps):
    count = lax.axis_size("user")
    return lax.ppermute(value, "user", [((i + steps) % count, i) for i in range(count)])


def kernel_call(body, name, out_shapes, in_specs, scratch=(), flops=0, moved=0):
    return pl.pallas_call(
        body,
        out_shape=out_shapes,
        in_specs=in_specs,
        out_specs=[VMEM] * len(out_shapes),
        scratch_shapes=scratch,
        compiler_params=pltpu.CompilerParams(vmem_limit_bytes=VMEM_LIMIT),
        cost_estimate=pl.CostEstimate(flops=flops, bytes_accessed=moved, transcendentals=0),
        name=name,
    )


def core_at(steps):
    return lax.rem(lax.axis_index("user") + steps, lax.axis_size("user"))


def of_core(core, arrivals):
    chosen = arrivals[0]
    for steps in range(1, len(arrivals)):
        chosen = jnp.where(core_at(steps) == core, arrivals[steps], chosen)
    return chosen


def blocks_of(piece, arrivals):
    _, steps, core = piece
    return arrivals[steps : steps + 1] if core is None else arrivals


def flip_of(piece):
    flips, steps, core = piece
    if core is not None:
        return flips[core]
    return sum(jnp.where(core_at(steps) == u, flip, 0) for u, flip in enumerate(flips))


def rows_of(pieces, refs):
    blocks, at = [], 0
    for piece in pieces:
        count = 1 if piece[2] is None else lax.axis_size("user")
        shards = [ref[...] for ref in refs[at : at + count]]
        blocks.append(shards[0] if piece[2] is None else of_core(piece[2], shards))
        at += count
    return jnp.concatenate(blocks, axis=0)


def matches(pieces, shard_rows, ids_row):
    hist_index = lax.axis_index("hist")
    blocks = []
    for piece in pieces:
        item = lax.broadcasted_iota(jnp.int32, (shard_rows, ids_row.shape[1]), 0)
        item += (hist_index ^ flip_of(piece)) * shard_rows
        blocks.append((item == ids_row).astype(F32).astype(BF16))
    return jnp.concatenate(blocks, axis=0)


def stack_kernel(*refs):
    *refs, out_ref = refs
    at = 0
    for ref in refs:
        out_ref[at : at + ref.shape[0], :] = ref[...]
        at += ref.shape[0]


def stack(blocks, flops=0):
    shape = (sum(block.shape[0] for block in blocks), blocks[0].shape[1])
    return kernel_call(
        stack_kernel, "stack", [jax.ShapeDtypeStruct(shape, blocks[0].dtype)], [VMEM] * len(blocks), flops=flops
    )(*blocks)[0]


def attend_rows(pieces, refs, w_query_ref, keys_ref, values_ref, sums_ref):
    width = sums_ref.shape[1]
    head_size = width // H
    rows = rows_of(pieces, refs)
    normed = rms_scale(rows.astype(F32)).astype(BF16)
    queries = jnp.dot(normed, w_query_ref[...], preferred_element_type=F32).astype(BF16)
    for head in range(H):
        cut = slice(head * head_size, (head + 1) * head_size)
        scores = lax.dot_general(
            queries[:, cut], keys_ref[0, :, cut], (((1,), (1,)), ((), ())), preferred_element_type=F32
        )
        half = scores * (0.5 * head_size ** (-0.5))
        weights = (half + half * jnp.tanh(half)).astype(BF16)
        sums_ref[:, cut] = jnp.dot(weights, values_ref[:, cut], preferred_element_type=F32).astype(BF16)


def first_kernel(pieces, length_ref, w_query_ref, keys_ref, values_ref, *refs):
    *refs, sums_ref, masked_ref = refs
    history = masked_ref.shape[0]
    place = lax.broadcasted_iota(jnp.int32, masked_ref.shape, 0) + lax.axis_index("hist") * history
    masked_ref[...] = jnp.where(place < length_ref[0], values_ref[0].astype(F32), 0.0).astype(BF16)
    attend_rows(pieces, refs, w_query_ref, keys_ref, masked_ref, sums_ref)


def next_kernel(pieces, w_query_ref, keys_ref, values_ref, *refs):
    *refs, sums_ref = refs
    attend_rows(pieces, refs, w_query_ref, keys_ref, values_ref, sums_ref)


def attend_cost(rows, width, history):
    return 2 * rows * width * (width + 2 * history)


def attend_first(pieces, blocks, shard_rows, lengths, w_query, keys, values):
    rows, width = len(pieces) * shard_rows, w_query.shape[0]
    return kernel_call(
        functools.partial(first_kernel, pieces),
        "attend_first",
        [jax.ShapeDtypeStruct((rows, width), BF16), jax.ShapeDtypeStruct(values.shape[1:], BF16)],
        [SMEM] + [VMEM] * (3 + len(blocks)),
        flops=attend_cost(rows, width, keys.shape[1]),
    )(lengths, w_query, keys, values, *blocks)


def attend_next(pieces, blocks, shard_rows, w_query, keys, values):
    rows, width = len(pieces) * shard_rows, w_query.shape[0]
    return kernel_call(
        functools.partial(next_kernel, pieces),
        "attend_next",
        [jax.ShapeDtypeStruct((rows, width), BF16)],
        [VMEM] * (3 + len(blocks)),
        flops=attend_cost(rows, width, keys.shape[1]),
    )(w_query, keys, values, *blocks)[0]


def place_kernel(pieces, id_flips, orders, shard_rows, near_ids_ref, far_ids_ref, *refs):
    *sums_refs, kept_a, sent_a, kept_b, sent_b = refs
    half, slots = near_ids_ref.shape
    rows = [id_flips.index(flip) for flip in orders[0]]
    refs_rows = [(near_ids_ref, row) if row < half else (far_ids_ref, row - half) for row in rows]
    ids_row = jnp.concatenate([ref[row : row + 1, :] for ref, row in refs_rows], axis=1)
    onehot = matches(pieces, shard_rows, ids_row)
    width = sums_refs[0].shape[1] // 2
    for side, order in enumerate(orders):
        columns = slice(side * width, (side + 1) * width)
        sums = jnp.concatenate([ref[:, columns] for ref in sums_refs], axis=0)
        placed = lax.dot_general(onehot, sums, TRANSPOSED, preferred_element_type=F32).astype(BF16)
        half = len(order) // 2
        for at, flip in enumerate(order):
            block = orders[0].index(flip)
            target = ((kept_a, sent_a), (kept_b, sent_b))[side][at // half]
            target[at % half * slots : (at % half + 1) * slots, :] = placed[block * slots : (block + 1) * slots, :]


def place(pieces, id_flips, orders, shard_rows, near_ids, far_ids, sums):
    devices, slots = len(orders[0]), near_ids.shape[1]
    width = sums[0].shape[1]
    out = jax.ShapeDtypeStruct((devices * slots // 2, width // 2), BF16)
    return kernel_call(
        functools.partial(place_kernel, pieces, id_flips, orders, shard_rows),
        "place",
        [out] * 4,
        [VMEM] * (2 + len(sums)),
        flops=2 * sum(part.shape[0] for part in sums) * devices * slots * width,
    )(near_ids, far_ids, *sums)


def fold_kernel(sides, *refs):
    ins, (kept_ref, sent_ref) = refs[: 2 * sides], refs[2 * sides :]
    half, width = ins[0].shape[0] // 2, ins[0].shape[1]
    for side in range(sides):
        total = ins[2 * side][...].astype(F32) + ins[2 * side + 1][...].astype(F32)
        columns = slice(side * width, (side + 1) * width)
        kept_ref[:, columns] = total[:half]
        sent_ref[:, columns] = total[half:].astype(BF16)


def fold(pairs):
    rows, width = pairs[0][0].shape
    shape = (rows // 2, width * len(pairs))
    blocks = [block for pair in pairs for block in pair]
    return kernel_call(
        functools.partial(fold_kernel, len(pairs)),
        "fold",
        [jax.ShapeDtypeStruct(shape, F32), jax.ShapeDtypeStruct(shape, BF16)],
        [VMEM] * len(blocks),
        moved=8 * rows * width * len(pairs),
    )(*blocks)


def prepare_kernel(pieces, after_ref, ids_ref, w_gate_ref, *refs):
    del after_ref
    *refs, embed_ref, gating_ref = refs
    table = rows_of(pieces, refs)
    onehot = matches(pieces, table.shape[0] // len(pieces), ids_ref[...])
    embedded = lax.dot_general(onehot, table, TRANSPOSED, preferred_element_type=F32)
    embed_ref[...] = embedded
    normed = rms_scale(embedded).astype(BF16)
    gating_ref[...] = silu(jnp.dot(normed, w_gate_ref[...], preferred_element_type=F32))


def prepare(pieces, blocks, shard_rows, after, ids, w_gate):
    slots, width = ids.shape[1], w_gate.shape[0]
    return kernel_call(
        functools.partial(prepare_kernel, pieces),
        "prepare",
        [jax.ShapeDtypeStruct((slots, width), F32)] * 2,
        [ANY, VMEM, VMEM] + [VMEM] * len(blocks),
        flops=2 * slots * width * (width + len(pieces) * shard_rows),
    )(after, ids, w_gate, *blocks)


def finish_kernel(kept_ref, come_ref, embed_ref, gating_ref, gain_ref, count_ref, domain_ref, w_out_ref, *refs):
    expert_refs, out_ref = refs[:-1], refs[-1]
    users = len(expert_refs)
    attended = kept_ref[...] + come_ref[...].astype(F32)
    gated = (rms_scale(attended) * gain_ref[...] * gating_ref[...]).astype(BF16)
    mixed = jnp.dot(gated, w_out_ref[...], preferred_element_type=F32)
    state = (embed_ref[...] + mixed).astype(BF16)

    slots = state.shape[0]
    row_at = lax.broadcasted_iota(jnp.int32, (slots, slots), 0)
    lane_at = lax.broadcasted_iota(jnp.int32, (slots, slots), 1)
    steps_away = lax.rem(domain_ref[...] - lax.axis_index("user") + users, users)
    live = lane_at + lax.axis_index("hist") * slots < count_ref[0]
    wanted = jnp.where(live, steps_away, -1)
    owner = jnp.sum(jnp.where(row_at == lane_at, wanted, 0).astype(F32), axis=1, keepdims=True)

    result = jnp.zeros(state.shape, F32)
    for steps, layers in enumerate(expert_refs):
        current = state
        for layer in range(LAYERS):
            lifted = jnp.dot(current, layers[0, layer], preferred_element_type=F32)
            current = (current.astype(F32) + silu(lifted)).astype(BF16)
        result = jnp.where(owner == steps, current.astype(F32), result)
    out_ref[0] = result.astype(BF16)


def finish(kept, come, embed, gating, gain, counts, domains, w_out, experts):
    slots, width = kept.shape
    return kernel_call(
        finish_kernel,
        "finish",
        [jax.ShapeDtypeStruct((1, slots, width), BF16)],
        [VMEM] * 5 + [SMEM] + [VMEM] * (2 + len(experts)),
        flops=2 * slots * width * width * (1 + LAYERS * len(experts)),
    )(kept, come, embed, gating, gain, counts, domains, w_out, *experts)[0]


def on_device(
    item_table,
    item_ids,
    candidate_counts,
    domain_ids,
    history_lengths,
    history_keys,
    history_values,
    w_query,
    w_gate,
    w_out,
    attn_gain,
    expert_weights,
):
    shard_rows = item_table.shape[0]
    hist_devices = lax.axis_size("hist")
    users = lax.axis_size("user")
    bits = hist_devices.bit_length() - 1
    others = range(1, users)

    all_flips = [tuple(range(at, min(at + users, hist_devices))) for at in range(1, hist_devices, users)]
    fetched = [swapped_by_user(item_table, flips) for flips in all_flips]

    near_ids, id_flips = stack([item_ids], flops=LOADS_BESIDE), [0]
    far_ids = swapped(near_ids, 1 << (bits - 1))

    early = len(all_flips) // 2
    first_pieces = [((0,) * users, 0, None)] + [(flips, 0, None) for flips in all_flips[:early]]
    first_blocks = [item_table] + fetched[:early]
    id_flips += [flip + (1 << (bits - 1)) for flip in id_flips]
    near_ids = stack([near_ids, far_ids])
    w_query, near_ids = lax.optimization_barrier((w_query, near_ids))
    first, masked_values = attend_first(
        first_pieces, first_blocks, shard_rows, history_lengths, w_query, history_keys, history_values
    )
    for bit in reversed(range(bits - 1)):
        far_ids = swapped(near_ids, 1 << bit)
        id_flips += [flip + (1 << bit) for flip in id_flips]
        if bit:
            first, far_ids = lax.optimization_barrier((first, far_ids))
            near_ids = stack([near_ids, far_ids])
    first, *fetched[:early] = lax.optimization_barrier((first, *fetched[:early]))
    first, near_ids, *fetched[early:] = lax.optimization_barrier((first, near_ids, *fetched[early:]))
    next_pieces, next_blocks = [], []
    for at, (flips, block) in enumerate(zip(all_flips, fetched)):
        arrivals = [block] + [from_user(block, steps) for steps in others]
        found = [(flips, steps, None) for steps in range(users)]
        if at < early:
            found = found[1:]
        elif len(flips) < users:
            found = [(flips, 0, core) for core in range(len(flips))]
        next_pieces += found
        next_blocks += [block for piece in found for block in blocks_of(piece, arrivals)]
    following = attend_next(next_pieces, next_blocks, shard_rows, w_query, history_keys, masked_values)
    pieces, blocks = first_pieces + next_pieces, first_blocks + next_blocks

    turns = [list(range(bits)), list(range(bits))]
    turns[1][:2] = [1, 0]
    orders = [
        [sum(((r >> (bits - 1 - t)) & 1) << bit for t, bit in enumerate(turn)) for r in range(hist_devices)]
        for turn in turns
    ]
    kept_a, sent_a, kept_b, sent_b = place(
        pieces, id_flips, orders, shard_rows, near_ids, far_ids, [first, following]
    )
    embed, gating = prepare(pieces, blocks, shard_rows, kept_a, item_ids, w_gate)

    leaving, kept_a = lax.optimization_barrier((expert_weights, kept_a))
    experts = [expert_weights] + [from_user(leaving, steps) for steps in others]

    held = [(kept_a, sent_a), (kept_b, sent_b)]
    for at in range(bits - 1):
        arriving = [swapped(held[side][1], 1 << turn[at]) for side, turn in enumerate(turns)]
        if at == 0:
            *arriving, embed = lax.optimization_barrier((*arriving, embed))
        pairs = [(held[side][0], arriving[side]) for side in range(len(turns))]
        if at < bits - 2:
            held = [fold([pair]) for pair in pairs]
        else:
            kept, sent = fold(pairs)
    come = swapped(sent, 1 << (bits - 1))
    return finish(kept, come, embed, gating, attn_gain[None], candidate_counts, domain_ids, w_out, experts)


def solution(mesh):
    in_specs = (
        P("hist", None),
        P(("groups", "user"), "hist"),
        P(("groups", "user")),
        P(("groups", "user"), "hist"),
        P(("groups", "user")),
        P(("groups", "user"), "hist", None),
        P(("groups", "user"), "hist", None),
        P(),
        P(),
        P(),
        P(),
        P("user", None, None, None),
    )
    out_specs = P(("groups", "user"), "hist", None)
    return jax.shard_map(
        on_device, mesh=mesh, in_specs=in_specs, out_specs=out_specs, check_vma=False
    )
```

```python
import functools

import jax
import jax.numpy as jnp
from jax import lax
from jax.experimental import pallas as pl
from jax.experimental.pallas import tpu as pltpu
from jax.sharding import PartitionSpec as P

H = 8
LAYERS = 2
VMEM_LIMIT = 24 * 1024 * 1024
LOADS_BESIDE = 8 * 10**9

norm_eps = 1e-05
F32 = jnp.float32
BF16 = jnp.bfloat16
ANY = pl.BlockSpec(memory_space=pl.ANY)
VMEM = pl.BlockSpec(memory_space=pltpu.VMEM)
SMEM = pl.BlockSpec(memory_space=pltpu.SMEM)
TRANSPOSED = (((0,), (0,)), ((), ()))


def rms_scale(matrix):
    return matrix * lax.rsqrt(jnp.mean(matrix * matrix, axis=-1, keepdims=True) + norm_eps)


def silu(value):
    half = 0.5 * value
    return half + half * jnp.tanh(half)


def swapped(value, flip):
    count = lax.axis_size("hist")
    return lax.ppermute(value, "hist", [(i, i ^ flip) for i in range(count)])


def swapped_by_user(value, flips):
    count = lax.axis_size("hist")
    pairs = [
        (u * count + i, u * count + (i ^ flip)) for u, flip in enumerate(flips) for i in range(count)
    ]
    return lax.ppermute(value, ("user", "hist"), pairs)


def from_user(value, steps):
    count = lax.axis_size("user")
    return lax.ppermute(value, "user", [((i + steps) % count, i) for i in range(count)])


def kernel_call(body, name, out_shapes, in_specs, scratch=(), flops=0, moved=0):
    return pl.pallas_call(
        body,
        out_shape=out_shapes,
        in_specs=in_specs,
        out_specs=[VMEM] * len(out_shapes),
        scratch_shapes=scratch,
        compiler_params=pltpu.CompilerParams(vmem_limit_bytes=VMEM_LIMIT),
        cost_estimate=pl.CostEstimate(flops=flops, bytes_accessed=moved, transcendentals=0),
        name=name,
    )


def core_at(steps):
    return lax.rem(lax.axis_index("user") + steps, lax.axis_size("user"))


def of_core(core, arrivals):
    chosen = arrivals[0]
    for steps in range(1, len(arrivals)):
        chosen = jnp.where(core_at(steps) == core, arrivals[steps], chosen)
    return chosen


def blocks_of(piece, arrivals):
    _, steps, core = piece
    return arrivals[steps : steps + 1] if core is None else arrivals


def flip_of(piece):
    flips, steps, core = piece
    if core is not None:
        return flips[core]
    return sum(jnp.where(core_at(steps) == u, flip, 0) for u, flip in enumerate(flips))


def rows_of(pieces, refs):
    blocks, at = [], 0
    for piece in pieces:
        count = 1 if piece[2] is None else lax.axis_size("user")
        shards = [ref[...] for ref in refs[at : at + count]]
        blocks.append(shards[0] if piece[2] is None else of_core(piece[2], shards))
        at += count
    return jnp.concatenate(blocks, axis=0)


def matches(pieces, shard_rows, ids_row):
    hist_index = lax.axis_index("hist")
    blocks = []
    for piece in pieces:
        item = lax.broadcasted_iota(jnp.int32, (shard_rows, ids_row.shape[1]), 0)
        item += (hist_index ^ flip_of(piece)) * shard_rows
        blocks.append((item == ids_row).astype(F32).astype(BF16))
    return jnp.concatenate(blocks, axis=0)


def stack_kernel(*refs):
    *refs, out_ref = refs
    at = 0
    for ref in refs:
        out_ref[at : at + ref.shape[0], :] = ref[...]
        at += ref.shape[0]


def stack(blocks, flops=0):
    shape = (sum(block.shape[0] for block in blocks), blocks[0].shape[1])
    return kernel_call(
        stack_kernel, "stack", [jax.ShapeDtypeStruct(shape, blocks[0].dtype)], [VMEM] * len(blocks), flops=flops
    )(*blocks)[0]


def attend_rows(pieces, refs, w_query_ref, keys_ref, values_ref, sums_ref):
    width = sums_ref.shape[1]
    head_size = width // H
    rows = rows_of(pieces, refs)
    normed = rms_scale(rows.astype(F32)).astype(BF16)
    queries = jnp.dot(normed, w_query_ref[...], preferred_element_type=F32).astype(BF16)
    for head in range(H):
        cut = slice(head * head_size, (head + 1) * head_size)
        scores = lax.dot_general(
            queries[:, cut], keys_ref[0, :, cut], (((1,), (1,)), ((), ())), preferred_element_type=F32
        )
        half = scores * (0.5 * head_size ** (-0.5))
        weights = (half + half * jnp.tanh(half)).astype(BF16)
        sums_ref[:, cut] = jnp.dot(weights, values_ref[:, cut], preferred_element_type=F32).astype(BF16)


def first_kernel(pieces, length_ref, w_query_ref, keys_ref, values_ref, *refs):
    *refs, sums_ref, masked_ref = refs
    history = masked_ref.shape[0]
    place = lax.broadcasted_iota(jnp.int32, masked_ref.shape, 0) + lax.axis_index("hist") * history
    masked_ref[...] = jnp.where(place < length_ref[0], values_ref[0].astype(F32), 0.0).astype(BF16)
    attend_rows(pieces, refs, w_query_ref, keys_ref, masked_ref, sums_ref)


def next_kernel(pieces, w_query_ref, keys_ref, values_ref, *refs):
    *refs, sums_ref = refs
    attend_rows(pieces, refs, w_query_ref, keys_ref, values_ref, sums_ref)


def attend_cost(rows, width, history):
    return 2 * rows * width * (width + 2 * history)


def attend_first(pieces, blocks, shard_rows, lengths, w_query, keys, values):
    rows, width = len(pieces) * shard_rows, w_query.shape[0]
    return kernel_call(
        functools.partial(first_kernel, pieces),
        "attend_first",
        [jax.ShapeDtypeStruct((rows, width), BF16), jax.ShapeDtypeStruct(values.shape[1:], BF16)],
        [SMEM] + [VMEM] * (3 + len(blocks)),
        flops=attend_cost(rows, width, keys.shape[1]),
    )(lengths, w_query, keys, values, *blocks)


def attend_next(pieces, blocks, shard_rows, w_query, keys, values):
    rows, width = len(pieces) * shard_rows, w_query.shape[0]
    return kernel_call(
        functools.partial(next_kernel, pieces),
        "attend_next",
        [jax.ShapeDtypeStruct((rows, width), BF16)],
        [VMEM] * (3 + len(blocks)),
        flops=attend_cost(rows, width, keys.shape[1]),
    )(w_query, keys, values, *blocks)[0]


def place_kernel(pieces, id_flips, orders, shard_rows, near_ids_ref, far_ids_ref, *refs):
    *sums_refs, kept_a, sent_a, kept_b, sent_b = refs
    half, slots = near_ids_ref.shape
    rows = [id_flips.index(flip) for flip in orders[0]]
    refs_rows = [(near_ids_ref, row) if row < half else (far_ids_ref, row - half) for row in rows]
    ids_row = jnp.concatenate([ref[row : row + 1, :] for ref, row in refs_rows], axis=1)
    onehot = matches(pieces, shard_rows, ids_row)
    width = sums_refs[0].shape[1] // 2
    for side, order in enumerate(orders):
        columns = slice(side * width, (side + 1) * width)
        sums = jnp.concatenate([ref[:, columns] for ref in sums_refs], axis=0)
        placed = lax.dot_general(onehot, sums, TRANSPOSED, preferred_element_type=F32).astype(BF16)
        half = len(order) // 2
        for at, flip in enumerate(order):
            block = orders[0].index(flip)
            target = ((kept_a, sent_a), (kept_b, sent_b))[side][at // half]
            target[at % half * slots : (at % half + 1) * slots, :] = placed[block * slots : (block + 1) * slots, :]


def place(pieces, id_flips, orders, shard_rows, near_ids, far_ids, sums):
    devices, slots = len(orders[0]), near_ids.shape[1]
    width = sums[0].shape[1]
    out = jax.ShapeDtypeStruct((devices * slots // 2, width // 2), BF16)
    return kernel_call(
        functools.partial(place_kernel, pieces, id_flips, orders, shard_rows),
        "place",
        [out] * 4,
        [VMEM] * (2 + len(sums)),
        flops=2 * sum(part.shape[0] for part in sums) * devices * slots * width,
    )(near_ids, far_ids, *sums)


def fold_kernel(sides, *refs):
    ins, (kept_ref, sent_ref) = refs[: 2 * sides], refs[2 * sides :]
    half, width = ins[0].shape[0] // 2, ins[0].shape[1]
    for side in range(sides):
        total = ins[2 * side][...].astype(F32) + ins[2 * side + 1][...].astype(F32)
        columns = slice(side * width, (side + 1) * width)
        kept_ref[:, columns] = total[:half]
        sent_ref[:, columns] = total[half:].astype(BF16)


def fold(pairs):
    rows, width = pairs[0][0].shape
    shape = (rows // 2, width * len(pairs))
    blocks = [block for pair in pairs for block in pair]
    return kernel_call(
        functools.partial(fold_kernel, len(pairs)),
        "fold",
        [jax.ShapeDtypeStruct(shape, F32), jax.ShapeDtypeStruct(shape, BF16)],
        [VMEM] * len(blocks),
        moved=8 * rows * width * len(pairs),
    )(*blocks)


def prepare_kernel(pieces, after_ref, ids_ref, w_gate_ref, *refs):
    del after_ref
    *refs, embed_ref, gating_ref = refs
    table = rows_of(pieces, refs)
    onehot = matches(pieces, table.shape[0] // len(pieces), ids_ref[...])
    embedded = lax.dot_general(onehot, table, TRANSPOSED, preferred_element_type=F32)
    embed_ref[...] = embedded
    normed = rms_scale(embedded).astype(BF16)
    gating_ref[...] = silu(jnp.dot(normed, w_gate_ref[...], preferred_element_type=F32))


def prepare(pieces, blocks, shard_rows, after, ids, w_gate):
    slots, width = ids.shape[1], w_gate.shape[0]
    return kernel_call(
        functools.partial(prepare_kernel, pieces),
        "prepare",
        [jax.ShapeDtypeStruct((slots, width), F32)] * 2,
        [ANY, VMEM, VMEM] + [VMEM] * len(blocks),
        flops=2 * slots * width * (width + len(pieces) * shard_rows),
    )(after, ids, w_gate, *blocks)


def finish_kernel(kept_ref, come_ref, embed_ref, gating_ref, gain_ref, count_ref, domain_ref, w_out_ref, *refs):
    expert_refs, out_ref = refs[:-1], refs[-1]
    users = len(expert_refs)
    attended = kept_ref[...] + come_ref[...].astype(F32)
    gated = (rms_scale(attended) * gain_ref[...] * gating_ref[...]).astype(BF16)
    mixed = jnp.dot(gated, w_out_ref[...], preferred_element_type=F32)
    state = (embed_ref[...] + mixed).astype(BF16)

    slots = state.shape[0]
    row_at = lax.broadcasted_iota(jnp.int32, (slots, slots), 0)
    lane_at = lax.broadcasted_iota(jnp.int32, (slots, slots), 1)
    steps_away = lax.rem(domain_ref[...] - lax.axis_index("user") + users, users)
    live = lane_at + lax.axis_index("hist") * slots < count_ref[0]
    wanted = jnp.where(live, steps_away, -1)
    owner = jnp.sum(jnp.where(row_at == lane_at, wanted, 0).astype(F32), axis=1, keepdims=True)

    result = jnp.zeros(state.shape, F32)
    for steps, layers in enumerate(expert_refs):
        current = state
        for layer in range(LAYERS):
            lifted = jnp.dot(current, layers[0, layer], preferred_element_type=F32)
            current = (current.astype(F32) + silu(lifted)).astype(BF16)
        result = jnp.where(owner == steps, current.astype(F32), result)
    out_ref[0] = result.astype(BF16)


def finish(kept, come, embed, gating, gain, counts, domains, w_out, experts):
    slots, width = kept.shape
    return kernel_call(
        finish_kernel,
        "finish",
        [jax.ShapeDtypeStruct((1, slots, width), BF16)],
        [VMEM] * 5 + [SMEM] + [VMEM] * (2 + len(experts)),
        flops=2 * slots * width * width * (1 + LAYERS * len(experts)),
    )(kept, come, embed, gating, gain, counts, domains, w_out, *experts)[0]


def on_device(
    item_table,
    item_ids,
    candidate_counts,
    domain_ids,
    history_lengths,
    history_keys,
    history_values,
    w_query,
    w_gate,
    w_out,
    attn_gain,
    expert_weights,
):
    shard_rows = item_table.shape[0]
    hist_devices = lax.axis_size("hist")
    users = lax.axis_size("user")
    bits = hist_devices.bit_length() - 1
    others = range(1, users)

    shared = hist_devices // 4
    far = list(range(hist_devices - 1, hist_devices // 2 - 1, -1))
    near = [flip for flip in range(1, hist_devices // 2) if flip != shared]
    far_flips = [tuple(far[at : at + users][:: (-1) ** (at // users)]) for at in range(0, len(far), users)]
    near_flips = [tuple(near[at : at + users]) for at in range(0, len(near), users)]
    far_shards = [swapped_by_user(item_table, flips) for flips in far_flips]
    near_shards = [swapped_by_user(item_table, flips) for flips in near_flips]
    shared_shard = swapped(item_table, shared)

    near_ids, id_flips = stack([item_ids], flops=LOADS_BESIDE), [0]
    far_ids = swapped(near_ids, 1 << (bits - 1))

    first_pieces = [((flip,) * users, 0, None) for flip in (0, shared)] + [(flips, 0, None) for flips in near_flips]
    first_blocks = [item_table, shared_shard] + near_shards
    id_flips += [flip + (1 << (bits - 1)) for flip in id_flips]
    near_ids = stack([near_ids, far_ids])
    w_query, near_ids = lax.optimization_barrier((w_query, near_ids))
    first, masked_values = attend_first(
        first_pieces, first_blocks, shard_rows, history_lengths, w_query, history_keys, history_values
    )
    for bit in reversed(range(bits - 1)):
        far_ids = swapped(near_ids, 1 << bit)
        id_flips += [flip + (1 << bit) for flip in id_flips]
        if bit:
            first, far_ids = lax.optimization_barrier((first, far_ids))
            near_ids = stack([near_ids, far_ids])
    first, *near_shards = lax.optimization_barrier((first, *near_shards))
    first, near_ids, *far_shards = lax.optimization_barrier((first, near_ids, *far_shards))
    next_pieces, next_blocks = [], []
    for flips, block in zip(near_flips + far_flips, near_shards + far_shards):
        arrivals = [block] + [from_user(block, steps) for steps in others]
        found = [(flips, steps, None) for steps in range(users)]
        if flips in near_flips:
            found = found[1:]
        elif len(flips) < users:
            found = [(flips, 0, core) for core in range(len(flips))]
        next_pieces += found
        next_blocks += [block for piece in found for block in blocks_of(piece, arrivals)]
    following = attend_next(next_pieces, next_blocks, shard_rows, w_query, history_keys, masked_values)
    pieces, blocks = first_pieces + next_pieces, first_blocks + next_blocks

    turns = [list(range(bits)), list(range(bits))]
    turns[1][:2] = [1, 0]
    orders = [
        [sum(((r >> (bits - 1 - t)) & 1) << bit for t, bit in enumerate(turn)) for r in range(hist_devices)]
        for turn in turns
    ]
    kept_a, sent_a, kept_b, sent_b = place(
        pieces, id_flips, orders, shard_rows, near_ids, far_ids, [first, following]
    )
    embed, gating = prepare(pieces, blocks, shard_rows, kept_a, item_ids, w_gate)

    leaving, kept_a = lax.optimization_barrier((expert_weights, kept_a))
    experts = [expert_weights] + [from_user(leaving, steps) for steps in others]

    held = [(kept_a, sent_a), (kept_b, sent_b)]
    for at in range(bits - 1):
        arriving = [swapped(held[side][1], 1 << turn[at]) for side, turn in enumerate(turns)]
        if at == 0:
            *arriving, embed = lax.optimization_barrier((*arriving, embed))
        pairs = [(held[side][0], arriving[side]) for side in range(len(turns))]
        if at < bits - 2:
            held = [fold([pair]) for pair in pairs]
        else:
            kept, sent = fold(pairs)
    come = swapped(sent, 1 << (bits - 1))
    return finish(kept, come, embed, gating, attn_gain[None], candidate_counts, domain_ids, w_out, experts)


def solution(mesh):
    in_specs = (
        P("hist", None),
        P(("groups", "user"), "hist"),
        P(("groups", "user")),
        P(("groups", "user"), "hist"),
        P(("groups", "user")),
        P(("groups", "user"), "hist", None),
        P(("groups", "user"), "hist", None),
        P(),
        P(),
        P(),
        P(),
        P("user", None, None, None),
    )
    out_specs = P(("groups", "user"), "hist", None)
    return jax.shard_map(
        on_device, mesh=mesh, in_specs=in_specs, out_specs=out_specs, check_vma=False
    )
```

```python
import functools

import jax
import jax.numpy as jnp
from jax import lax
from jax.experimental import pallas as pl
from jax.experimental.pallas import tpu as pltpu
from jax.sharding import PartitionSpec as P

H = 8
LAYERS = 2
VMEM_LIMIT = 24 * 1024 * 1024
LOADS_BESIDE = 8 * 10**9

norm_eps = 1e-05
F32 = jnp.float32
BF16 = jnp.bfloat16
ANY = pl.BlockSpec(memory_space=pl.ANY)
VMEM = pl.BlockSpec(memory_space=pltpu.VMEM)
SMEM = pl.BlockSpec(memory_space=pltpu.SMEM)
TRANSPOSED = (((0,), (0,)), ((), ()))


def rms_scale(matrix):
    return matrix * lax.rsqrt(jnp.mean(matrix * matrix, axis=-1, keepdims=True) + norm_eps)


def silu(value):
    half = 0.5 * value
    return half + half * jnp.tanh(half)


def swapped(value, flip):
    count = lax.axis_size("hist")
    return lax.ppermute(value, "hist", [(i, i ^ flip) for i in range(count)])


def swapped_by_user(value, flips):
    count = lax.axis_size("hist")
    pairs = [
        (u * count + i, u * count + (i ^ flip)) for u, flip in enumerate(flips) for i in range(count)
    ]
    return lax.ppermute(value, ("user", "hist"), pairs)


def from_user(value, steps):
    count = lax.axis_size("user")
    return lax.ppermute(value, "user", [((i + steps) % count, i) for i in range(count)])


def kernel_call(body, name, out_shapes, in_specs, scratch=(), flops=0, moved=0):
    return pl.pallas_call(
        body,
        out_shape=out_shapes,
        in_specs=in_specs,
        out_specs=[VMEM] * len(out_shapes),
        scratch_shapes=scratch,
        compiler_params=pltpu.CompilerParams(vmem_limit_bytes=VMEM_LIMIT),
        cost_estimate=pl.CostEstimate(flops=flops, bytes_accessed=moved, transcendentals=0),
        name=name,
    )


def core_at(steps):
    return lax.rem(lax.axis_index("user") + steps, lax.axis_size("user"))


def of_core(core, arrivals):
    chosen = arrivals[0]
    for steps in range(1, len(arrivals)):
        chosen = jnp.where(core_at(steps) == core, arrivals[steps], chosen)
    return chosen


def blocks_of(piece, arrivals):
    _, steps, core = piece
    return arrivals[steps : steps + 1] if core is None else arrivals


def flip_of(piece):
    flips, steps, core = piece
    if core is not None:
        return flips[core]
    return sum(jnp.where(core_at(steps) == u, flip, 0) for u, flip in enumerate(flips))


def rows_of(pieces, refs):
    blocks, at = [], 0
    for piece in pieces:
        count = 1 if piece[2] is None else lax.axis_size("user")
        shards = [ref[...] for ref in refs[at : at + count]]
        blocks.append(shards[0] if piece[2] is None else of_core(piece[2], shards))
        at += count
    return jnp.concatenate(blocks, axis=0)


def matches(pieces, shard_rows, ids_row):
    hist_index = lax.axis_index("hist")
    blocks = []
    for piece in pieces:
        item = lax.broadcasted_iota(jnp.int32, (shard_rows, ids_row.shape[1]), 0)
        item += (hist_index ^ flip_of(piece)) * shard_rows
        blocks.append((item == ids_row).astype(F32).astype(BF16))
    return jnp.concatenate(blocks, axis=0)


def stack_kernel(*refs):
    *refs, out_ref = refs
    at = 0
    for ref in refs:
        out_ref[at : at + ref.shape[0], :] = ref[...]
        at += ref.shape[0]


def stack(blocks, flops=0):
    shape = (sum(block.shape[0] for block in blocks), blocks[0].shape[1])
    return kernel_call(
        stack_kernel, "stack", [jax.ShapeDtypeStruct(shape, blocks[0].dtype)], [VMEM] * len(blocks), flops=flops
    )(*blocks)[0]


def attend_rows(pieces, refs, w_query_ref, keys_ref, values_ref, sums_ref):
    width = sums_ref.shape[1]
    head_size = width // H
    rows = rows_of(pieces, refs)
    normed = rms_scale(rows.astype(F32)).astype(BF16)
    queries = jnp.dot(normed, w_query_ref[...], preferred_element_type=F32).astype(BF16)
    for head in range(H):
        cut = slice(head * head_size, (head + 1) * head_size)
        scores = lax.dot_general(
            queries[:, cut], keys_ref[0, :, cut], (((1,), (1,)), ((), ())), preferred_element_type=F32
        )
        half = scores * (0.5 * head_size ** (-0.5))
        weights = (half + half * jnp.tanh(half)).astype(BF16)
        sums_ref[:, cut] = jnp.dot(weights, values_ref[:, cut], preferred_element_type=F32).astype(BF16)


def first_kernel(pieces, length_ref, w_query_ref, keys_ref, values_ref, *refs):
    *refs, sums_ref, masked_ref = refs
    history = masked_ref.shape[0]
    place = lax.broadcasted_iota(jnp.int32, masked_ref.shape, 0) + lax.axis_index("hist") * history
    masked_ref[...] = jnp.where(place < length_ref[0], values_ref[0].astype(F32), 0.0).astype(BF16)
    attend_rows(pieces, refs, w_query_ref, keys_ref, masked_ref, sums_ref)


def next_kernel(pieces, w_query_ref, keys_ref, values_ref, *refs):
    *refs, sums_ref = refs
    attend_rows(pieces, refs, w_query_ref, keys_ref, values_ref, sums_ref)


def attend_cost(rows, width, history):
    return 2 * rows * width * (width + 2 * history)


def attend_first(pieces, blocks, shard_rows, lengths, w_query, keys, values):
    rows, width = len(pieces) * shard_rows, w_query.shape[0]
    return kernel_call(
        functools.partial(first_kernel, pieces),
        "attend_first",
        [jax.ShapeDtypeStruct((rows, width), BF16), jax.ShapeDtypeStruct(values.shape[1:], BF16)],
        [SMEM] + [VMEM] * (3 + len(blocks)),
        flops=attend_cost(rows, width, keys.shape[1]),
    )(lengths, w_query, keys, values, *blocks)


def attend_next(pieces, blocks, shard_rows, w_query, keys, values):
    rows, width = len(pieces) * shard_rows, w_query.shape[0]
    return kernel_call(
        functools.partial(next_kernel, pieces),
        "attend_next",
        [jax.ShapeDtypeStruct((rows, width), BF16)],
        [VMEM] * (3 + len(blocks)),
        flops=attend_cost(rows, width, keys.shape[1]),
    )(w_query, keys, values, *blocks)[0]


def place_kernel(pieces, id_flips, orders, shard_rows, near_ids_ref, far_ids_ref, *refs):
    *sums_refs, kept_a, sent_a, kept_b, sent_b = refs
    half, slots = near_ids_ref.shape
    rows = [id_flips.index(flip) for flip in orders[0]]
    refs_rows = [(near_ids_ref, row) if row < half else (far_ids_ref, row - half) for row in rows]
    ids_row = jnp.concatenate([ref[row : row + 1, :] for ref, row in refs_rows], axis=1)
    onehot = matches(pieces, shard_rows, ids_row)
    width = sums_refs[0].shape[1] // 2
    for side, order in enumerate(orders):
        columns = slice(side * width, (side + 1) * width)
        sums = jnp.concatenate([ref[:, columns] for ref in sums_refs], axis=0)
        placed = lax.dot_general(onehot, sums, TRANSPOSED, preferred_element_type=F32).astype(BF16)
        half = len(order) // 2
        for at, flip in enumerate(order):
            block = orders[0].index(flip)
            target = ((kept_a, sent_a), (kept_b, sent_b))[side][at // half]
            target[at % half * slots : (at % half + 1) * slots, :] = placed[block * slots : (block + 1) * slots, :]


def place(pieces, id_flips, orders, shard_rows, near_ids, far_ids, sums):
    devices, slots = len(orders[0]), near_ids.shape[1]
    width = sums[0].shape[1]
    out = jax.ShapeDtypeStruct((devices * slots // 2, width // 2), BF16)
    return kernel_call(
        functools.partial(place_kernel, pieces, id_flips, orders, shard_rows),
        "place",
        [out] * 4,
        [VMEM] * (2 + len(sums)),
        flops=2 * sum(part.shape[0] for part in sums) * devices * slots * width,
    )(near_ids, far_ids, *sums)


def fold_kernel(sides, *refs):
    ins, (kept_ref, sent_ref) = refs[: 2 * sides], refs[2 * sides :]
    half, width = ins[0].shape[0] // 2, ins[0].shape[1]
    for side in range(sides):
        total = ins[2 * side][...].astype(F32) + ins[2 * side + 1][...].astype(F32)
        columns = slice(side * width, (side + 1) * width)
        kept_ref[:, columns] = total[:half]
        sent_ref[:, columns] = total[half:].astype(BF16)


def fold(pairs):
    rows, width = pairs[0][0].shape
    shape = (rows // 2, width * len(pairs))
    blocks = [block for pair in pairs for block in pair]
    return kernel_call(
        functools.partial(fold_kernel, len(pairs)),
        "fold",
        [jax.ShapeDtypeStruct(shape, F32), jax.ShapeDtypeStruct(shape, BF16)],
        [VMEM] * len(blocks),
        moved=8 * rows * width * len(pairs),
    )(*blocks)


def prepare_kernel(pieces, after_ref, ids_ref, w_gate_ref, *refs):
    del after_ref
    *refs, embed_ref, gating_ref = refs
    table = rows_of(pieces, refs)
    onehot = matches(pieces, table.shape[0] // len(pieces), ids_ref[...])
    embedded = lax.dot_general(onehot, table, TRANSPOSED, preferred_element_type=F32)
    embed_ref[...] = embedded
    normed = rms_scale(embedded).astype(BF16)
    gating_ref[...] = silu(jnp.dot(normed, w_gate_ref[...], preferred_element_type=F32))


def prepare(pieces, blocks, shard_rows, after, ids, w_gate):
    slots, width = ids.shape[1], w_gate.shape[0]
    return kernel_call(
        functools.partial(prepare_kernel, pieces),
        "prepare",
        [jax.ShapeDtypeStruct((slots, width), F32)] * 2,
        [ANY, VMEM, VMEM] + [VMEM] * len(blocks),
        flops=2 * slots * width * (width + len(pieces) * shard_rows),
    )(after, ids, w_gate, *blocks)


def finish_kernel(sides, embed_ref, gating_ref, gain_ref, count_ref, domain_ref, w_out_ref, *refs):
    *expert_refs, out_ref = refs[2 * sides :]
    users = len(expert_refs)
    halves = [refs[2 * side][...] + refs[2 * side + 1][...].astype(F32) for side in range(sides)]
    attended = jnp.concatenate(halves, axis=1)
    gated = (rms_scale(attended) * gain_ref[...] * gating_ref[...]).astype(BF16)
    mixed = jnp.dot(gated, w_out_ref[...], preferred_element_type=F32)
    state = (embed_ref[...] + mixed).astype(BF16)

    slots = state.shape[0]
    row_at = lax.broadcasted_iota(jnp.int32, (slots, slots), 0)
    lane_at = lax.broadcasted_iota(jnp.int32, (slots, slots), 1)
    steps_away = lax.rem(domain_ref[...] - lax.axis_index("user") + users, users)
    live = lane_at + lax.axis_index("hist") * slots < count_ref[0]
    wanted = jnp.where(live, steps_away, -1)
    owner = jnp.sum(jnp.where(row_at == lane_at, wanted, 0).astype(F32), axis=1, keepdims=True)

    result = jnp.zeros(state.shape, F32)
    for steps, layers in enumerate(expert_refs):
        current = state
        for layer in range(LAYERS):
            lifted = jnp.dot(current, layers[0, layer], preferred_element_type=F32)
            current = (current.astype(F32) + silu(lifted)).astype(BF16)
        result = jnp.where(owner == steps, current.astype(F32), result)
    out_ref[0] = result.astype(BF16)


def finish(pairs, embed, gating, gain, counts, domains, w_out, experts):
    slots, width = embed.shape
    blocks = [block for pair in pairs for block in pair]
    return kernel_call(
        functools.partial(finish_kernel, len(pairs)),
        "finish",
        [jax.ShapeDtypeStruct((1, slots, width), BF16)],
        [VMEM] * 3 + [SMEM] + [VMEM] * (2 + len(blocks) + len(experts)),
        flops=2 * slots * width * width * (1 + LAYERS * len(experts)),
    )(embed, gating, gain, counts, domains, w_out, *blocks, *experts)[0]


def on_device(
    item_table,
    item_ids,
    candidate_counts,
    domain_ids,
    history_lengths,
    history_keys,
    history_values,
    w_query,
    w_gate,
    w_out,
    attn_gain,
    expert_weights,
):
    shard_rows = item_table.shape[0]
    hist_devices = lax.axis_size("hist")
    users = lax.axis_size("user")
    bits = hist_devices.bit_length() - 1
    others = range(1, users)

    shared = hist_devices // 4
    far = list(range(hist_devices - 1, hist_devices // 2 - 1, -1))
    near = [flip for flip in range(1, hist_devices // 2) if flip != shared]
    far_flips = [tuple(far[at : at + users][:: (-1) ** (at // users)]) for at in range(0, len(far), users)]
    near_flips = [tuple(near[at : at + users]) for at in range(0, len(near), users)]
    far_shards = [swapped_by_user(item_table, flips) for flips in far_flips]
    near_shards = [swapped_by_user(item_table, flips) for flips in near_flips]
    shared_shard = swapped(item_table, shared)

    turns = [bits - 1, 0] + list(range(1, bits - 1))
    far_ids, id_flips = swapped(item_ids, 1 << turns[0]), [0, 1 << turns[0]]

    first_pieces = [((flip,) * users, 0, None) for flip in (0, shared)] + [(flips, 0, None) for flips in near_flips]
    first_blocks = [item_table, shared_shard] + near_shards
    near_ids = stack([item_ids, far_ids], flops=LOADS_BESIDE)
    w_query, near_ids = lax.optimization_barrier((w_query, near_ids))
    first, masked_values = attend_first(
        first_pieces, first_blocks, shard_rows, history_lengths, w_query, history_keys, history_values
    )
    for bit in turns[1:]:
        far_ids = swapped(near_ids, 1 << bit)
        id_flips += [flip + (1 << bit) for flip in id_flips]
        if bit != turns[-1]:
            first, far_ids = lax.optimization_barrier((first, far_ids))
            near_ids = stack([near_ids, far_ids])
    first, *near_shards = lax.optimization_barrier((first, *near_shards))
    first, near_ids, *far_shards = lax.optimization_barrier((first, near_ids, *far_shards))
    next_pieces, next_blocks = [], []
    for flips, block in zip(near_flips + far_flips, near_shards + far_shards):
        arrivals = [block] + [from_user(block, steps) for steps in others]
        found = [(flips, steps, None) for steps in range(users)]
        if flips in near_flips:
            found = found[1:]
        elif len(flips) < users:
            found = [(flips, 0, core) for core in range(len(flips))]
        next_pieces += found
        next_blocks += [block for piece in found for block in blocks_of(piece, arrivals)]
    following = attend_next(next_pieces, next_blocks, shard_rows, w_query, history_keys, masked_values)
    pieces, blocks = first_pieces + next_pieces, first_blocks + next_blocks

    side_turns = [list(range(bits)), list(range(bits))]
    side_turns[1][:2] = [1, 0]
    orders = [
        [sum(((r >> (bits - 1 - t)) & 1) << bit for t, bit in enumerate(turn)) for r in range(hist_devices)]
        for turn in side_turns
    ]
    kept_a, sent_a, kept_b, sent_b = place(
        pieces, id_flips, orders, shard_rows, near_ids, far_ids, [first, following]
    )
    embed, gating = prepare(pieces, blocks, shard_rows, kept_a, item_ids, w_gate)

    leaving, kept_a = lax.optimization_barrier((expert_weights, kept_a))
    experts = [expert_weights] + [from_user(leaving, steps) for steps in others]

    held = [(kept_a, sent_a), (kept_b, sent_b)]
    for at in range(bits):
        arriving = [swapped(sent, 1 << turn[at]) for (_, sent), turn in zip(held, side_turns)]
        if at == 0:
            *arriving, embed = lax.optimization_barrier((*arriving, embed))
        pairs = [(kept, come) for (kept, _), come in zip(held, arriving)]
        if at < bits - 1:
            held = [fold([pair]) for pair in pairs]
    return finish(pairs, embed, gating, attn_gain[None], candidate_counts, domain_ids, w_out, experts)


def solution(mesh):
    in_specs = (
        P("hist", None),
        P(("groups", "user"), "hist"),
        P(("groups", "user")),
        P(("groups", "user"), "hist"),
        P(("groups", "user")),
        P(("groups", "user"), "hist", None),
        P(("groups", "user"), "hist", None),
        P(),
        P(),
        P(),
        P(),
        P("user", None, None, None),
    )
    out_specs = P(("groups", "user"), "hist", None)
    return jax.shard_map(
        on_device, mesh=mesh, in_specs=in_specs, out_specs=out_specs, check_vma=False
    )
```

```python
import functools

import jax
import jax.numpy as jnp
from jax import lax
from jax.experimental import pallas as pl
from jax.experimental.pallas import tpu as pltpu
from jax.sharding import PartitionSpec as P

H = 8
LAYERS = 2
VMEM_LIMIT = 24 * 1024 * 1024
LOADS_BESIDE = 8 * 10**9

norm_eps = 1e-05
F32 = jnp.float32
BF16 = jnp.bfloat16
ANY = pl.BlockSpec(memory_space=pl.ANY)
VMEM = pl.BlockSpec(memory_space=pltpu.VMEM)
SMEM = pl.BlockSpec(memory_space=pltpu.SMEM)
TRANSPOSED = (((0,), (0,)), ((), ()))


def rms_scale(matrix):
    return matrix * lax.rsqrt(jnp.mean(matrix * matrix, axis=-1, keepdims=True) + norm_eps)


def silu(value):
    half = 0.5 * value
    return half + half * jnp.tanh(half)


def swapped(value, flip):
    count = lax.axis_size("hist")
    return lax.ppermute(value, "hist", [(i, i ^ flip) for i in range(count)])


def swapped_by_user(value, flips):
    count = lax.axis_size("hist")
    pairs = [
        (u * count + i, u * count + (i ^ flip)) for u, flip in enumerate(flips) for i in range(count)
    ]
    return lax.ppermute(value, ("user", "hist"), pairs)


def from_user(value, steps):
    count = lax.axis_size("user")
    return lax.ppermute(value, "user", [((i + steps) % count, i) for i in range(count)])


def kernel_call(body, name, out_shapes, in_specs, scratch=(), flops=0, moved=0):
    return pl.pallas_call(
        body,
        out_shape=out_shapes,
        in_specs=in_specs,
        out_specs=[VMEM] * len(out_shapes),
        scratch_shapes=scratch,
        compiler_params=pltpu.CompilerParams(vmem_limit_bytes=VMEM_LIMIT),
        cost_estimate=pl.CostEstimate(flops=flops, bytes_accessed=moved, transcendentals=0),
        name=name,
    )


def core_at(steps):
    return lax.rem(lax.axis_index("user") + steps, lax.axis_size("user"))


def of_core(core, arrivals):
    chosen = arrivals[0]
    for steps in range(1, len(arrivals)):
        chosen = jnp.where(core_at(steps) == core, arrivals[steps], chosen)
    return chosen


def blocks_of(piece, arrivals):
    _, steps, core = piece
    return arrivals[steps : steps + 1] if core is None else arrivals


def flip_of(piece):
    flips, steps, core = piece
    if core is not None:
        return flips[core]
    return sum(jnp.where(core_at(steps) == u, flip, 0) for u, flip in enumerate(flips))


def rows_of(pieces, refs):
    blocks, at = [], 0
    for piece in pieces:
        count = 1 if piece[2] is None else lax.axis_size("user")
        shards = [ref[...] for ref in refs[at : at + count]]
        blocks.append(shards[0] if piece[2] is None else of_core(piece[2], shards))
        at += count
    return jnp.concatenate(blocks, axis=0)


def matches(pieces, shard_rows, ids_row):
    hist_index = lax.axis_index("hist")
    blocks = []
    for piece in pieces:
        item = lax.broadcasted_iota(jnp.int32, (shard_rows, ids_row.shape[1]), 0)
        item += (hist_index ^ flip_of(piece)) * shard_rows
        blocks.append((item == ids_row).astype(F32).astype(BF16))
    return jnp.concatenate(blocks, axis=0)


def stack_kernel(*refs):
    *refs, out_ref = refs
    at = 0
    for ref in refs:
        out_ref[at : at + ref.shape[0], :] = ref[...]
        at += ref.shape[0]


def stack(blocks, flops=0):
    shape = (sum(block.shape[0] for block in blocks), blocks[0].shape[1])
    return kernel_call(
        stack_kernel, "stack", [jax.ShapeDtypeStruct(shape, blocks[0].dtype)], [VMEM] * len(blocks), flops=flops
    )(*blocks)[0]


def attend_rows(pieces, refs, w_query_ref, keys_ref, values_ref, sums_ref):
    width = sums_ref.shape[1]
    head_size = width // H
    rows = rows_of(pieces, refs)
    normed = rms_scale(rows.astype(F32)).astype(BF16)
    queries = jnp.dot(normed, w_query_ref[...], preferred_element_type=F32).astype(BF16)
    for head in range(H):
        cut = slice(head * head_size, (head + 1) * head_size)
        scores = lax.dot_general(
            queries[:, cut], keys_ref[0, :, cut], (((1,), (1,)), ((), ())), preferred_element_type=F32
        )
        half = scores * (0.5 * head_size ** (-0.5))
        weights = (half + half * jnp.tanh(half)).astype(BF16)
        sums_ref[:, cut] = jnp.dot(weights, values_ref[:, cut], preferred_element_type=F32).astype(BF16)


def first_kernel(pieces, length_ref, w_query_ref, keys_ref, values_ref, *refs):
    *refs, sums_ref, masked_ref = refs
    history = masked_ref.shape[0]
    place = lax.broadcasted_iota(jnp.int32, masked_ref.shape, 0) + lax.axis_index("hist") * history
    masked_ref[...] = jnp.where(place < length_ref[0], values_ref[0].astype(F32), 0.0).astype(BF16)
    attend_rows(pieces, refs, w_query_ref, keys_ref, masked_ref, sums_ref)


def next_kernel(pieces, w_query_ref, keys_ref, values_ref, *refs):
    *refs, sums_ref = refs
    attend_rows(pieces, refs, w_query_ref, keys_ref, values_ref, sums_ref)


def attend_cost(rows, width, history):
    return 2 * rows * width * (width + 2 * history)


def attend_first(pieces, blocks, shard_rows, lengths, w_query, keys, values):
    rows, width = len(pieces) * shard_rows, w_query.shape[0]
    return kernel_call(
        functools.partial(first_kernel, pieces),
        "attend_first",
        [jax.ShapeDtypeStruct((rows, width), BF16), jax.ShapeDtypeStruct(values.shape[1:], BF16)],
        [SMEM] + [VMEM] * (3 + len(blocks)),
        flops=attend_cost(rows, width, keys.shape[1]),
    )(lengths, w_query, keys, values, *blocks)


def attend_next(pieces, blocks, shard_rows, w_query, keys, values):
    rows, width = len(pieces) * shard_rows, w_query.shape[0]
    return kernel_call(
        functools.partial(next_kernel, pieces),
        "attend_next",
        [jax.ShapeDtypeStruct((rows, width), BF16)],
        [VMEM] * (3 + len(blocks)),
        flops=attend_cost(rows, width, keys.shape[1]),
    )(w_query, keys, values, *blocks)[0]


def place_kernel(pieces, id_flips, orders, shard_rows, near_ids_ref, far_ids_ref, *refs):
    *sums_refs, kept_a, sent_a, kept_b, sent_b = refs
    half, slots = near_ids_ref.shape
    rows = [id_flips.index(flip) for flip in orders[0]]
    refs_rows = [(near_ids_ref, row) if row < half else (far_ids_ref, row - half) for row in rows]
    ids_row = jnp.concatenate([ref[row : row + 1, :] for ref, row in refs_rows], axis=1)
    onehot = matches(pieces, shard_rows, ids_row)
    width = sums_refs[0].shape[1] // 2
    for side, order in enumerate(orders):
        columns = slice(side * width, (side + 1) * width)
        sums = jnp.concatenate([ref[:, columns] for ref in sums_refs], axis=0)
        placed = lax.dot_general(onehot, sums, TRANSPOSED, preferred_element_type=F32).astype(BF16)
        half = len(order) // 2
        for at, flip in enumerate(order):
            block = orders[0].index(flip)
            target = ((kept_a, sent_a), (kept_b, sent_b))[side][at // half]
            target[at % half * slots : (at % half + 1) * slots, :] = placed[block * slots : (block + 1) * slots, :]


def place(pieces, id_flips, orders, shard_rows, near_ids, far_ids, sums):
    devices, slots = len(orders[0]), near_ids.shape[1]
    width = sums[0].shape[1]
    out = jax.ShapeDtypeStruct((devices * slots // 2, width // 2), BF16)
    return kernel_call(
        functools.partial(place_kernel, pieces, id_flips, orders, shard_rows),
        "place",
        [out] * 4,
        [VMEM] * (2 + len(sums)),
        flops=2 * sum(part.shape[0] for part in sums) * devices * slots * width,
    )(near_ids, far_ids, *sums)


def fold_kernel(sides, *refs):
    ins, (kept_ref, sent_ref) = refs[: 2 * sides], refs[2 * sides :]
    half, width = ins[0].shape[0] // 2, ins[0].shape[1]
    for side in range(sides):
        total = ins[2 * side][...].astype(F32) + ins[2 * side + 1][...].astype(F32)
        columns = slice(side * width, (side + 1) * width)
        kept_ref[:, columns] = total[:half]
        sent_ref[:, columns] = total[half:].astype(BF16)


def fold(pairs):
    rows, width = pairs[0][0].shape
    shape = (rows // 2, width * len(pairs))
    blocks = [block for pair in pairs for block in pair]
    return kernel_call(
        functools.partial(fold_kernel, len(pairs)),
        "fold",
        [jax.ShapeDtypeStruct(shape, F32), jax.ShapeDtypeStruct(shape, BF16)],
        [VMEM] * len(blocks),
        moved=8 * rows * width * len(pairs),
    )(*blocks)


def prepare_kernel(pieces, after_ref, ids_ref, w_gate_ref, *refs):
    del after_ref
    *refs, embed_ref, gating_ref = refs
    table = rows_of(pieces, refs)
    onehot = matches(pieces, table.shape[0] // len(pieces), ids_ref[...])
    embedded = lax.dot_general(onehot, table, TRANSPOSED, preferred_element_type=F32)
    embed_ref[...] = embedded
    normed = rms_scale(embedded).astype(BF16)
    gating_ref[...] = silu(jnp.dot(normed, w_gate_ref[...], preferred_element_type=F32))


def prepare(pieces, blocks, shard_rows, after, ids, w_gate):
    slots, width = ids.shape[1], w_gate.shape[0]
    return kernel_call(
        functools.partial(prepare_kernel, pieces),
        "prepare",
        [jax.ShapeDtypeStruct((slots, width), F32)] * 2,
        [ANY, VMEM, VMEM] + [VMEM] * len(blocks),
        flops=2 * slots * width * (width + len(pieces) * shard_rows),
    )(after, ids, w_gate, *blocks)


def finish_kernel(sides, embed_ref, gating_ref, gain_ref, count_ref, domain_ref, w_out_ref, *refs):
    *expert_refs, out_ref = refs[2 * sides :]
    users = len(expert_refs)
    halves = [refs[2 * side][...] + refs[2 * side + 1][...].astype(F32) for side in range(sides)]
    attended = jnp.concatenate(halves, axis=1)
    gated = (rms_scale(attended) * gain_ref[...] * gating_ref[...]).astype(BF16)
    mixed = jnp.dot(gated, w_out_ref[...], preferred_element_type=F32)
    state = (embed_ref[...] + mixed).astype(BF16)

    slots = state.shape[0]
    row_at = lax.broadcasted_iota(jnp.int32, (slots, slots), 0)
    lane_at = lax.broadcasted_iota(jnp.int32, (slots, slots), 1)
    steps_away = lax.rem(domain_ref[...] - lax.axis_index("user") + users, users)
    live = lane_at + lax.axis_index("hist") * slots < count_ref[0]
    wanted = jnp.where(live, steps_away, -1)
    owner = jnp.sum(jnp.where(row_at == lane_at, wanted, 0).astype(F32), axis=1, keepdims=True)

    result = jnp.zeros(state.shape, F32)
    for steps, layers in enumerate(expert_refs):
        current = state
        for layer in range(LAYERS):
            lifted = jnp.dot(current, layers[0, layer], preferred_element_type=F32)
            current = (current.astype(F32) + silu(lifted)).astype(BF16)
        result = jnp.where(owner == steps, current.astype(F32), result)
    out_ref[0] = result.astype(BF16)


def finish(pairs, embed, gating, gain, counts, domains, w_out, experts):
    slots, width = embed.shape
    blocks = [block for pair in pairs for block in pair]
    return kernel_call(
        functools.partial(finish_kernel, len(pairs)),
        "finish",
        [jax.ShapeDtypeStruct((1, slots, width), BF16)],
        [VMEM] * 3 + [SMEM] + [VMEM] * (2 + len(blocks) + len(experts)),
        flops=2 * slots * width * width * (1 + LAYERS * len(experts)),
    )(embed, gating, gain, counts, domains, w_out, *blocks, *experts)[0]


def on_device(
    item_table,
    item_ids,
    candidate_counts,
    domain_ids,
    history_lengths,
    history_keys,
    history_values,
    w_query,
    w_gate,
    w_out,
    attn_gain,
    expert_weights,
):
    shard_rows = item_table.shape[0]
    hist_devices = lax.axis_size("hist")
    users = lax.axis_size("user")
    bits = hist_devices.bit_length() - 1
    others = range(1, users)

    shared = 1
    far = list(range(hist_devices - 1, hist_devices // 2 - 1, -1))
    near = [flip for flip in range(1, hist_devices // 2) if flip != shared]
    far_flips = [tuple(far[at : at + users][:: (-1) ** (at // users)]) for at in range(0, len(far), users)]
    near_flips = [tuple(near[at : at + users]) for at in range(0, len(near), users)]
    far_shards = [swapped_by_user(item_table, flips) for flips in far_flips]
    near_shards = [swapped_by_user(item_table, flips) for flips in near_flips]
    shared_shard = swapped(item_table, shared)

    turns = [1] + list(range(2, bits)) + [0]
    far_ids, id_flips = swapped(item_ids, 1 << turns[0]), [0, 1 << turns[0]]

    first_pieces = [((flip,) * users, 0, None) for flip in (0, shared)] + [(flips, 0, None) for flips in near_flips]
    first_blocks = [item_table, shared_shard] + near_shards
    near_ids = stack([item_ids, far_ids], flops=LOADS_BESIDE)
    w_query, near_ids = lax.optimization_barrier((w_query, near_ids))
    first, masked_values = attend_first(
        first_pieces, first_blocks, shard_rows, history_lengths, w_query, history_keys, history_values
    )
    for bit in turns[1:]:
        far_ids = swapped(near_ids, 1 << bit)
        id_flips += [flip + (1 << bit) for flip in id_flips]
        if bit != turns[-1]:
            first, far_ids = lax.optimization_barrier((first, far_ids))
            near_ids = stack([near_ids, far_ids])
    first, *near_shards = lax.optimization_barrier((first, *near_shards))
    first, near_ids, *far_shards = lax.optimization_barrier((first, near_ids, *far_shards))
    next_pieces, next_blocks = [], []
    for flips, block in zip(near_flips + far_flips, near_shards + far_shards):
        arrivals = [block] + [from_user(block, steps) for steps in others]
        found = [(flips, steps, None) for steps in range(users)]
        if flips in near_flips:
            found = found[1:]
        elif len(flips) < users:
            found = [(flips, 0, core) for core in range(len(flips))]
        next_pieces += found
        next_blocks += [block for piece in found for block in blocks_of(piece, arrivals)]
    following = attend_next(next_pieces, next_blocks, shard_rows, w_query, history_keys, masked_values)
    pieces, blocks = first_pieces + next_pieces, first_blocks + next_blocks

    side_turns = [list(range(bits)), list(range(bits))]
    side_turns[1][:2] = [1, 0]
    orders = [
        [sum(((r >> (bits - 1 - t)) & 1) << bit for t, bit in enumerate(turn)) for r in range(hist_devices)]
        for turn in side_turns
    ]
    kept_a, sent_a, kept_b, sent_b = place(
        pieces, id_flips, orders, shard_rows, near_ids, far_ids, [first, following]
    )
    embed, gating = prepare(pieces, blocks, shard_rows, kept_a, item_ids, w_gate)

    leaving, kept_a = lax.optimization_barrier((expert_weights, kept_a))
    experts = [expert_weights] + [from_user(leaving, steps) for steps in others]

    held = [(kept_a, sent_a), (kept_b, sent_b)]
    for at in range(bits):
        arriving = [swapped(sent, 1 << turn[at]) for (_, sent), turn in zip(held, side_turns)]
        if at == 0:
            *arriving, embed = lax.optimization_barrier((*arriving, embed))
        pairs = [(kept, come) for (kept, _), come in zip(held, arriving)]
        if at < bits - 1:
            held = [fold([pair]) for pair in pairs]
    return finish(pairs, embed, gating, attn_gain[None], candidate_counts, domain_ids, w_out, experts)


def solution(mesh):
    in_specs = (
        P("hist", None),
        P(("groups", "user"), "hist"),
        P(("groups", "user")),
        P(("groups", "user"), "hist"),
        P(("groups", "user")),
        P(("groups", "user"), "hist", None),
        P(("groups", "user"), "hist", None),
        P(),
        P(),
        P(),
        P(),
        P("user", None, None, None),
    )
    out_specs = P(("groups", "user"), "hist", None)
    return jax.shard_map(
        on_device, mesh=mesh, in_specs=in_specs, out_specs=out_specs, check_vma=False
    )
```

```python
import functools

import jax
import jax.numpy as jnp
from jax import lax
from jax.experimental import pallas as pl
from jax.experimental.pallas import tpu as pltpu
from jax.sharding import PartitionSpec as P

H = 8
LAYERS = 2
VMEM_LIMIT = 24 * 1024 * 1024
LOADS_BESIDE = 8 * 10**9

norm_eps = 1e-05
F32 = jnp.float32
BF16 = jnp.bfloat16
ANY = pl.BlockSpec(memory_space=pl.ANY)
VMEM = pl.BlockSpec(memory_space=pltpu.VMEM)
SMEM = pl.BlockSpec(memory_space=pltpu.SMEM)
TRANSPOSED = (((0,), (0,)), ((), ()))


def rms_scale(matrix):
    return matrix * lax.rsqrt(jnp.mean(matrix * matrix, axis=-1, keepdims=True) + norm_eps)


def silu(value):
    half = 0.5 * value
    return half + half * jnp.tanh(half)


def swapped(value, flip):
    count = lax.axis_size("hist")
    return lax.ppermute(value, "hist", [(i, i ^ flip) for i in range(count)])


def swapped_by_user(value, flips):
    count = lax.axis_size("hist")
    pairs = [
        (u * count + i, u * count + (i ^ flip)) for u, flip in enumerate(flips) for i in range(count)
    ]
    return lax.ppermute(value, ("user", "hist"), pairs)


def from_user(value, steps):
    count = lax.axis_size("user")
    return lax.ppermute(value, "user", [((i + steps) % count, i) for i in range(count)])


def kernel_call(body, name, out_shapes, in_specs, scratch=(), flops=0, moved=0):
    return pl.pallas_call(
        body,
        out_shape=out_shapes,
        in_specs=in_specs,
        out_specs=[VMEM] * len(out_shapes),
        scratch_shapes=scratch,
        compiler_params=pltpu.CompilerParams(vmem_limit_bytes=VMEM_LIMIT),
        cost_estimate=pl.CostEstimate(flops=flops, bytes_accessed=moved, transcendentals=0),
        name=name,
    )


def core_at(steps):
    return lax.rem(lax.axis_index("user") + steps, lax.axis_size("user"))


def of_core(core, arrivals):
    chosen = arrivals[0]
    for steps in range(1, len(arrivals)):
        chosen = jnp.where(core_at(steps) == core, arrivals[steps], chosen)
    return chosen


def blocks_of(piece, arrivals):
    _, steps, core = piece
    return arrivals[steps : steps + 1] if core is None else arrivals


def flip_of(piece):
    flips, steps, core = piece
    if core is not None:
        return flips[core]
    return sum(jnp.where(core_at(steps) == u, flip, 0) for u, flip in enumerate(flips))


def rows_of(pieces, refs):
    blocks, at = [], 0
    for piece in pieces:
        count = 1 if piece[2] is None else lax.axis_size("user")
        shards = [ref[...] for ref in refs[at : at + count]]
        blocks.append(shards[0] if piece[2] is None else of_core(piece[2], shards))
        at += count
    return jnp.concatenate(blocks, axis=0)


def matches(pieces, shard_rows, ids_row):
    hist_index = lax.axis_index("hist")
    blocks = []
    for piece in pieces:
        item = lax.broadcasted_iota(jnp.int32, (shard_rows, ids_row.shape[1]), 0)
        item += (hist_index ^ flip_of(piece)) * shard_rows
        blocks.append((item == ids_row).astype(F32).astype(BF16))
    return jnp.concatenate(blocks, axis=0)


def stack_kernel(*refs):
    *refs, out_ref = refs
    at = 0
    for ref in refs:
        out_ref[at : at + ref.shape[0], :] = ref[...]
        at += ref.shape[0]


def stack(blocks, flops=0):
    shape = (sum(block.shape[0] for block in blocks), blocks[0].shape[1])
    return kernel_call(
        stack_kernel, "stack", [jax.ShapeDtypeStruct(shape, blocks[0].dtype)], [VMEM] * len(blocks), flops=flops
    )(*blocks)[0]


def attend_rows(pieces, refs, w_query_ref, keys_ref, values_ref, sums_ref):
    width = sums_ref.shape[1]
    head_size = width // H
    rows = rows_of(pieces, refs)
    normed = rms_scale(rows.astype(F32)).astype(BF16)
    queries = jnp.dot(normed, w_query_ref[...], preferred_element_type=F32).astype(BF16)
    for head in range(H):
        cut = slice(head * head_size, (head + 1) * head_size)
        scores = lax.dot_general(
            queries[:, cut], keys_ref[0, :, cut], (((1,), (1,)), ((), ())), preferred_element_type=F32
        )
        half = scores * (0.5 * head_size ** (-0.5))
        weights = (half + half * jnp.tanh(half)).astype(BF16)
        sums_ref[:, cut] = jnp.dot(weights, values_ref[:, cut], preferred_element_type=F32).astype(BF16)


def first_kernel(pieces, length_ref, w_query_ref, keys_ref, values_ref, *refs):
    *refs, sums_ref, masked_ref = refs
    history = masked_ref.shape[0]
    place = lax.broadcasted_iota(jnp.int32, masked_ref.shape, 0) + lax.axis_index("hist") * history
    masked_ref[...] = jnp.where(place < length_ref[0], values_ref[0].astype(F32), 0.0).astype(BF16)
    attend_rows(pieces, refs, w_query_ref, keys_ref, masked_ref, sums_ref)


def next_kernel(pieces, w_query_ref, keys_ref, values_ref, *refs):
    *refs, sums_ref = refs
    attend_rows(pieces, refs, w_query_ref, keys_ref, values_ref, sums_ref)


def attend_cost(rows, width, history):
    return 2 * rows * width * (width + 2 * history)


def attend_first(pieces, blocks, shard_rows, lengths, w_query, keys, values):
    rows, width = len(pieces) * shard_rows, w_query.shape[0]
    return kernel_call(
        functools.partial(first_kernel, pieces),
        "attend_first",
        [jax.ShapeDtypeStruct((rows, width), BF16), jax.ShapeDtypeStruct(values.shape[1:], BF16)],
        [SMEM] + [VMEM] * (3 + len(blocks)),
        flops=attend_cost(rows, width, keys.shape[1]),
    )(lengths, w_query, keys, values, *blocks)


def attend_next(pieces, blocks, shard_rows, w_query, keys, values):
    rows, width = len(pieces) * shard_rows, w_query.shape[0]
    return kernel_call(
        functools.partial(next_kernel, pieces),
        "attend_next",
        [jax.ShapeDtypeStruct((rows, width), BF16)],
        [VMEM] * (3 + len(blocks)),
        flops=attend_cost(rows, width, keys.shape[1]),
    )(w_query, keys, values, *blocks)[0]


def place_kernel(pieces, id_flips, orders, shard_rows, near_ids_ref, far_ids_ref, *refs):
    *sums_refs, kept_a, sent_a, kept_b, sent_b = refs
    half, slots = near_ids_ref.shape
    rows = [id_flips.index(flip) for flip in orders[0]]
    refs_rows = [(near_ids_ref, row) if row < half else (far_ids_ref, row - half) for row in rows]
    ids_row = jnp.concatenate([ref[row : row + 1, :] for ref, row in refs_rows], axis=1)
    onehot = matches(pieces, shard_rows, ids_row)
    width = sums_refs[0].shape[1] // 2
    for side, order in enumerate(orders):
        columns = slice(side * width, (side + 1) * width)
        sums = jnp.concatenate([ref[:, columns] for ref in sums_refs], axis=0)
        placed = lax.dot_general(onehot, sums, TRANSPOSED, preferred_element_type=F32).astype(BF16)
        half = len(order) // 2
        for at, flip in enumerate(order):
            block = orders[0].index(flip)
            target = ((kept_a, sent_a), (kept_b, sent_b))[side][at // half]
            target[at % half * slots : (at % half + 1) * slots, :] = placed[block * slots : (block + 1) * slots, :]


def place(pieces, id_flips, orders, shard_rows, near_ids, far_ids, sums):
    devices, slots = len(orders[0]), near_ids.shape[1]
    width = sums[0].shape[1]
    out = jax.ShapeDtypeStruct((devices * slots // 2, width // 2), BF16)
    return kernel_call(
        functools.partial(place_kernel, pieces, id_flips, orders, shard_rows),
        "place",
        [out] * 4,
        [VMEM] * (2 + len(sums)),
        flops=2 * sum(part.shape[0] for part in sums) * devices * slots * width,
    )(near_ids, far_ids, *sums)


def fold_kernel(sides, *refs):
    ins, (kept_ref, sent_ref) = refs[: 2 * sides], refs[2 * sides :]
    half, width = ins[0].shape[0] // 2, ins[0].shape[1]
    for side in range(sides):
        total = ins[2 * side][...].astype(F32) + ins[2 * side + 1][...].astype(F32)
        columns = slice(side * width, (side + 1) * width)
        kept_ref[:, columns] = total[:half]
        sent_ref[:, columns] = total[half:].astype(BF16)


def fold(pairs):
    rows, width = pairs[0][0].shape
    shape = (rows // 2, width * len(pairs))
    blocks = [block for pair in pairs for block in pair]
    return kernel_call(
        functools.partial(fold_kernel, len(pairs)),
        "fold",
        [jax.ShapeDtypeStruct(shape, F32), jax.ShapeDtypeStruct(shape, BF16)],
        [VMEM] * len(blocks),
        moved=8 * rows * width * len(pairs),
    )(*blocks)


def prepare_kernel(pieces, after_ref, ids_ref, w_gate_ref, *refs):
    del after_ref
    *refs, embed_ref, gating_ref = refs
    table = rows_of(pieces, refs)
    onehot = matches(pieces, table.shape[0] // len(pieces), ids_ref[...])
    embedded = lax.dot_general(onehot, table, TRANSPOSED, preferred_element_type=F32)
    embed_ref[...] = embedded
    normed = rms_scale(embedded).astype(BF16)
    gating_ref[...] = silu(jnp.dot(normed, w_gate_ref[...], preferred_element_type=F32))


def prepare(pieces, blocks, shard_rows, after, ids, w_gate):
    slots, width = ids.shape[1], w_gate.shape[0]
    return kernel_call(
        functools.partial(prepare_kernel, pieces),
        "prepare",
        [jax.ShapeDtypeStruct((slots, width), F32)] * 2,
        [ANY, VMEM, VMEM] + [VMEM] * len(blocks),
        flops=2 * slots * width * (width + len(pieces) * shard_rows),
    )(after, ids, w_gate, *blocks)


def finish_kernel(sides, embed_ref, gating_ref, gain_ref, count_ref, domain_ref, w_out_ref, *refs):
    *expert_refs, out_ref = refs[2 * sides :]
    users = len(expert_refs)
    halves = [refs[2 * side][...] + refs[2 * side + 1][...].astype(F32) for side in range(sides)]
    attended = jnp.concatenate(halves, axis=1)
    gated = (rms_scale(attended) * gain_ref[...] * gating_ref[...]).astype(BF16)
    mixed = jnp.dot(gated, w_out_ref[...], preferred_element_type=F32)
    state = (embed_ref[...] + mixed).astype(BF16)

    slots = state.shape[0]
    row_at = lax.broadcasted_iota(jnp.int32, (slots, slots), 0)
    lane_at = lax.broadcasted_iota(jnp.int32, (slots, slots), 1)
    steps_away = lax.rem(domain_ref[...] - lax.axis_index("user") + users, users)
    live = lane_at + lax.axis_index("hist") * slots < count_ref[0]
    wanted = jnp.where(live, steps_away, -1)
    owner = jnp.sum(jnp.where(row_at == lane_at, wanted, 0).astype(F32), axis=1, keepdims=True)

    result = jnp.zeros(state.shape, F32)
    for steps, layers in enumerate(expert_refs):
        current = state
        for layer in range(LAYERS):
            lifted = jnp.dot(current, layers[0, layer], preferred_element_type=F32)
            current = (current.astype(F32) + silu(lifted)).astype(BF16)
        result = jnp.where(owner == steps, current.astype(F32), result)
    out_ref[0] = result.astype(BF16)


def finish(pairs, embed, gating, gain, counts, domains, w_out, experts):
    slots, width = embed.shape
    blocks = [block for pair in pairs for block in pair]
    return kernel_call(
        functools.partial(finish_kernel, len(pairs)),
        "finish",
        [jax.ShapeDtypeStruct((1, slots, width), BF16)],
        [VMEM] * 3 + [SMEM] + [VMEM] * (2 + len(blocks) + len(experts)),
        flops=2 * slots * width * width * (1 + LAYERS * len(experts)),
    )(embed, gating, gain, counts, domains, w_out, *blocks, *experts)[0]


def on_device(
    item_table,
    item_ids,
    candidate_counts,
    domain_ids,
    history_lengths,
    history_keys,
    history_values,
    w_query,
    w_gate,
    w_out,
    attn_gain,
    expert_weights,
):
    shard_rows = item_table.shape[0]
    hist_devices = lax.axis_size("hist")
    users = lax.axis_size("user")
    bits = hist_devices.bit_length() - 1
    others = range(1, users)

    shared = 1
    far = list(range(hist_devices // 2, hist_devices))
    far = [flip for pair in zip(far[::-1], far) for flip in pair][: len(far)]
    near = [flip for flip in range(1, hist_devices // 2) if flip != shared]
    far_flips = [tuple(far[at : at + users][:: (-1) ** (at // users)]) for at in range(0, len(far), users)]
    near_flips = [tuple(near[at : at + users]) for at in range(0, len(near), users)]
    far_shards = [swapped_by_user(item_table, flips) for flips in far_flips]
    near_shards = [swapped_by_user(item_table, flips) for flips in near_flips]
    shared_shard = swapped(item_table, shared)

    turns = [1] + list(range(2, bits)) + [0]
    far_ids, id_flips = swapped(item_ids, 1 << turns[0]), [0, 1 << turns[0]]

    first_pieces = [((flip,) * users, 0, None) for flip in (0, shared)] + [(flips, 0, None) for flips in near_flips]
    first_blocks = [item_table, shared_shard] + near_shards
    near_ids = stack([item_ids, far_ids], flops=LOADS_BESIDE)
    w_query, near_ids = lax.optimization_barrier((w_query, near_ids))
    first, masked_values = attend_first(
        first_pieces, first_blocks, shard_rows, history_lengths, w_query, history_keys, history_values
    )
    for bit in turns[1:]:
        far_ids = swapped(near_ids, 1 << bit)
        id_flips += [flip + (1 << bit) for flip in id_flips]
        if bit != turns[-1]:
            first, far_ids = lax.optimization_barrier((first, far_ids))
            near_ids = stack([near_ids, far_ids])
    first, *near_shards = lax.optimization_barrier((first, *near_shards))
    first, near_ids, *far_shards = lax.optimization_barrier((first, near_ids, *far_shards))
    next_pieces, next_blocks = [], []
    for flips, block in zip(near_flips + far_flips, near_shards + far_shards):
        arrivals = [block] + [from_user(block, steps) for steps in others]
        found = [(flips, steps, None) for steps in range(users)]
        if flips in near_flips:
            found = found[1:]
        elif len(flips) < users:
            found = [(flips, 0, core) for core in range(len(flips))]
        next_pieces += found
        next_blocks += [block for piece in found for block in blocks_of(piece, arrivals)]
    following = attend_next(next_pieces, next_blocks, shard_rows, w_query, history_keys, masked_values)
    pieces, blocks = first_pieces + next_pieces, first_blocks + next_blocks

    side_turns = [list(range(bits)), list(range(bits))]
    side_turns[1][:2] = [1, 0]
    orders = [
        [sum(((r >> (bits - 1 - t)) & 1) << bit for t, bit in enumerate(turn)) for r in range(hist_devices)]
        for turn in side_turns
    ]
    kept_a, sent_a, kept_b, sent_b = place(
        pieces, id_flips, orders, shard_rows, near_ids, far_ids, [first, following]
    )
    embed, gating = prepare(pieces, blocks, shard_rows, kept_a, item_ids, w_gate)

    leaving, kept_a = lax.optimization_barrier((expert_weights, kept_a))
    experts = [expert_weights] + [from_user(leaving, steps) for steps in others]

    held = [(kept_a, sent_a), (kept_b, sent_b)]
    for at in range(bits):
        arriving = [swapped(sent, 1 << turn[at]) for (_, sent), turn in zip(held, side_turns)]
        if at == 0:
            *arriving, embed = lax.optimization_barrier((*arriving, embed))
        pairs = [(kept, come) for (kept, _), come in zip(held, arriving)]
        if at < bits - 1:
            held = [fold([pair]) for pair in pairs]
    return finish(pairs, embed, gating, attn_gain[None], candidate_counts, domain_ids, w_out, experts)


def solution(mesh):
    in_specs = (
        P("hist", None),
        P(("groups", "user"), "hist"),
        P(("groups", "user")),
        P(("groups", "user"), "hist"),
        P(("groups", "user")),
        P(("groups", "user"), "hist", None),
        P(("groups", "user"), "hist", None),
        P(),
        P(),
        P(),
        P(),
        P("user", None, None, None),
    )
    out_specs = P(("groups", "user"), "hist", None)
    return jax.shard_map(
        on_device, mesh=mesh, in_specs=in_specs, out_specs=out_specs, check_vma=False
    )
```

```python
import functools

import jax
import jax.numpy as jnp
from jax import lax
from jax.experimental import pallas as pl
from jax.experimental.pallas import tpu as pltpu
from jax.sharding import PartitionSpec as P

H = 8
LAYERS = 2
VMEM_LIMIT = 24 * 1024 * 1024
LOADS_BESIDE = 8 * 10**9

norm_eps = 1e-05
F32 = jnp.float32
BF16 = jnp.bfloat16
ANY = pl.BlockSpec(memory_space=pl.ANY)
VMEM = pl.BlockSpec(memory_space=pltpu.VMEM)
SMEM = pl.BlockSpec(memory_space=pltpu.SMEM)
TRANSPOSED = (((0,), (0,)), ((), ()))


def rms_scale(matrix):
    return matrix * lax.rsqrt(jnp.mean(matrix * matrix, axis=-1, keepdims=True) + norm_eps)


def silu(value):
    half = 0.5 * value
    return half + half * jnp.tanh(half)


def swapped(value, flip):
    count = lax.axis_size("hist")
    return lax.ppermute(value, "hist", [(i, i ^ flip) for i in range(count)])


def swapped_by_user(value, flips):
    count = lax.axis_size("hist")
    pairs = [
        (u * count + i, u * count + (i ^ flip)) for u, flip in enumerate(flips) for i in range(count)
    ]
    return lax.ppermute(value, ("user", "hist"), pairs)


def from_user(value, steps):
    count = lax.axis_size("user")
    return lax.ppermute(value, "user", [((i + steps) % count, i) for i in range(count)])


def kernel_call(body, name, out_shapes, in_specs, scratch=(), flops=0, moved=0):
    return pl.pallas_call(
        body,
        out_shape=out_shapes,
        in_specs=in_specs,
        out_specs=[VMEM] * len(out_shapes),
        scratch_shapes=scratch,
        compiler_params=pltpu.CompilerParams(vmem_limit_bytes=VMEM_LIMIT),
        cost_estimate=pl.CostEstimate(flops=flops, bytes_accessed=moved, transcendentals=0),
        name=name,
    )


def core_at(steps):
    return lax.rem(lax.axis_index("user") + steps, lax.axis_size("user"))


def of_core(core, arrivals):
    chosen = arrivals[0]
    for steps in range(1, len(arrivals)):
        chosen = jnp.where(core_at(steps) == core, arrivals[steps], chosen)
    return chosen


def blocks_of(piece, arrivals):
    _, steps, core = piece
    return arrivals[steps : steps + 1] if core is None else arrivals


def flip_of(piece):
    flips, steps, core = piece
    if core is not None:
        return flips[core]
    return sum(jnp.where(core_at(steps) == u, flip, 0) for u, flip in enumerate(flips))


def rows_of(pieces, refs):
    blocks, at = [], 0
    for piece in pieces:
        count = 1 if piece[2] is None else lax.axis_size("user")
        shards = [ref[...] for ref in refs[at : at + count]]
        blocks.append(shards[0] if piece[2] is None else of_core(piece[2], shards))
        at += count
    return jnp.concatenate(blocks, axis=0)


def matches(pieces, shard_rows, ids_row):
    hist_index = lax.axis_index("hist")
    blocks = []
    for piece in pieces:
        item = lax.broadcasted_iota(jnp.int32, (shard_rows, ids_row.shape[1]), 0)
        item += (hist_index ^ flip_of(piece)) * shard_rows
        blocks.append((item == ids_row).astype(F32).astype(BF16))
    return jnp.concatenate(blocks, axis=0)


def stack_kernel(*refs):
    *refs, out_ref = refs
    at = 0
    for ref in refs:
        out_ref[at : at + ref.shape[0], :] = ref[...]
        at += ref.shape[0]


def stack(blocks, flops=0):
    shape = (sum(block.shape[0] for block in blocks), blocks[0].shape[1])
    return kernel_call(
        stack_kernel, "stack", [jax.ShapeDtypeStruct(shape, blocks[0].dtype)], [VMEM] * len(blocks), flops=flops
    )(*blocks)[0]


def attend_rows(pieces, refs, w_query_ref, keys_ref, values_ref, sums_ref):
    width = sums_ref.shape[1]
    head_size = width // H
    rows = rows_of(pieces, refs)
    normed = rms_scale(rows.astype(F32)).astype(BF16)
    queries = jnp.dot(normed, w_query_ref[...], preferred_element_type=F32).astype(BF16)
    for head in range(H):
        cut = slice(head * head_size, (head + 1) * head_size)
        scores = lax.dot_general(
            queries[:, cut], keys_ref[0, :, cut], (((1,), (1,)), ((), ())), preferred_element_type=F32
        )
        half = scores * (0.5 * head_size ** (-0.5))
        weights = (half + half * jnp.tanh(half)).astype(BF16)
        sums_ref[:, cut] = jnp.dot(weights, values_ref[:, cut], preferred_element_type=F32).astype(BF16)


def first_kernel(pieces, length_ref, w_query_ref, keys_ref, values_ref, *refs):
    *refs, sums_ref, masked_ref = refs
    history = masked_ref.shape[0]
    place = lax.broadcasted_iota(jnp.int32, masked_ref.shape, 0) + lax.axis_index("hist") * history
    masked_ref[...] = jnp.where(place < length_ref[0], values_ref[0].astype(F32), 0.0).astype(BF16)
    attend_rows(pieces, refs, w_query_ref, keys_ref, masked_ref, sums_ref)


def next_kernel(pieces, w_query_ref, keys_ref, values_ref, *refs):
    *refs, sums_ref = refs
    attend_rows(pieces, refs, w_query_ref, keys_ref, values_ref, sums_ref)


def attend_cost(rows, width, history):
    return 2 * rows * width * (width + 2 * history)


def attend_first(pieces, blocks, shard_rows, lengths, w_query, keys, values):
    rows, width = len(pieces) * shard_rows, w_query.shape[0]
    return kernel_call(
        functools.partial(first_kernel, pieces),
        "attend_first",
        [jax.ShapeDtypeStruct((rows, width), BF16), jax.ShapeDtypeStruct(values.shape[1:], BF16)],
        [SMEM] + [VMEM] * (3 + len(blocks)),
        flops=attend_cost(rows, width, keys.shape[1]),
    )(lengths, w_query, keys, values, *blocks)


def attend_next(pieces, blocks, shard_rows, w_query, keys, values):
    rows, width = len(pieces) * shard_rows, w_query.shape[0]
    return kernel_call(
        functools.partial(next_kernel, pieces),
        "attend_next",
        [jax.ShapeDtypeStruct((rows, width), BF16)],
        [VMEM] * (3 + len(blocks)),
        flops=attend_cost(rows, width, keys.shape[1]),
    )(w_query, keys, values, *blocks)[0]


def place_kernel(pieces, id_flips, orders, shard_rows, near_ids_ref, far_ids_ref, *refs):
    *sums_refs, kept_a, sent_a, kept_b, sent_b = refs
    half, slots = near_ids_ref.shape
    rows = [id_flips.index(flip) for flip in orders[0]]
    refs_rows = [(near_ids_ref, row) if row < half else (far_ids_ref, row - half) for row in rows]
    ids_row = jnp.concatenate([ref[row : row + 1, :] for ref, row in refs_rows], axis=1)
    onehot = matches(pieces, shard_rows, ids_row)
    width = sums_refs[0].shape[1] // 2
    for side, order in enumerate(orders):
        columns = slice(side * width, (side + 1) * width)
        sums = jnp.concatenate([ref[:, columns] for ref in sums_refs], axis=0)
        placed = lax.dot_general(onehot, sums, TRANSPOSED, preferred_element_type=F32).astype(BF16)
        half = len(order) // 2
        for at, flip in enumerate(order):
            block = orders[0].index(flip)
            target = ((kept_a, sent_a), (kept_b, sent_b))[side][at // half]
            target[at % half * slots : (at % half + 1) * slots, :] = placed[block * slots : (block + 1) * slots, :]


def place(pieces, id_flips, orders, shard_rows, near_ids, far_ids, sums):
    devices, slots = len(orders[0]), near_ids.shape[1]
    width = sums[0].shape[1]
    out = jax.ShapeDtypeStruct((devices * slots // 2, width // 2), BF16)
    return kernel_call(
        functools.partial(place_kernel, pieces, id_flips, orders, shard_rows),
        "place",
        [out] * 4,
        [VMEM] * (2 + len(sums)),
        flops=2 * sum(part.shape[0] for part in sums) * devices * slots * width,
    )(near_ids, far_ids, *sums)


def fold_kernel(sides, *refs):
    ins, (kept_ref, sent_ref) = refs[: 2 * sides], refs[2 * sides :]
    half, width = ins[0].shape[0] // 2, ins[0].shape[1]
    for side in range(sides):
        total = ins[2 * side][...].astype(F32) + ins[2 * side + 1][...].astype(F32)
        columns = slice(side * width, (side + 1) * width)
        kept_ref[:, columns] = total[:half]
        sent_ref[:, columns] = total[half:].astype(BF16)


def fold(pairs):
    rows, width = pairs[0][0].shape
    shape = (rows // 2, width * len(pairs))
    blocks = [block for pair in pairs for block in pair]
    return kernel_call(
        functools.partial(fold_kernel, len(pairs)),
        "fold",
        [jax.ShapeDtypeStruct(shape, F32), jax.ShapeDtypeStruct(shape, BF16)],
        [VMEM] * len(blocks),
        moved=8 * rows * width * len(pairs),
    )(*blocks)


def prepare_kernel(pieces, after_ref, ids_ref, w_gate_ref, *refs):
    del after_ref
    *refs, embed_ref, gating_ref = refs
    table = rows_of(pieces, refs)
    onehot = matches(pieces, table.shape[0] // len(pieces), ids_ref[...])
    embedded = lax.dot_general(onehot, table, TRANSPOSED, preferred_element_type=F32)
    embed_ref[...] = embedded
    normed = rms_scale(embedded).astype(BF16)
    gating_ref[...] = silu(jnp.dot(normed, w_gate_ref[...], preferred_element_type=F32))


def prepare(pieces, blocks, shard_rows, after, ids, w_gate):
    slots, width = ids.shape[1], w_gate.shape[0]
    return kernel_call(
        functools.partial(prepare_kernel, pieces),
        "prepare",
        [jax.ShapeDtypeStruct((slots, width), F32)] * 2,
        [ANY, VMEM, VMEM] + [VMEM] * len(blocks),
        flops=2 * slots * width * (width + len(pieces) * shard_rows),
    )(after, ids, w_gate, *blocks)


def mixed_part(start, kept_ref, come_ref, gating_ref, gain_ref, w_out_ref):
    attended = kept_ref[...] + come_ref[...].astype(F32)
    columns = slice(start, start + attended.shape[1])
    gated = (attended * gain_ref[:, columns] * gating_ref[:, columns]).astype(BF16)
    squares = jnp.sum(attended * attended, axis=1, keepdims=True)
    return squares, jnp.dot(gated, w_out_ref[columns, :], preferred_element_type=F32)


def mix_kernel(kept_ref, come_ref, gating_ref, gain_ref, w_out_ref, squares_ref, mixed_ref):
    squares, mixed = mixed_part(0, kept_ref, come_ref, gating_ref, gain_ref, w_out_ref)
    squares_ref[...] = jnp.broadcast_to(squares, squares_ref.shape)
    mixed_ref[...] = mixed


def mix(pair, gating, gain, w_out):
    slots, width = gating.shape
    return kernel_call(
        mix_kernel,
        "mix",
        [jax.ShapeDtypeStruct((slots, 128), F32), jax.ShapeDtypeStruct((slots, width), F32)],
        [VMEM] * 5,
        flops=2 * slots * width * pair[0].shape[1],
    )(*pair, gating, gain, w_out)


def finish_kernel(kept_ref, come_ref, squares_ref, mixed_ref, embed_ref, gating_ref, gain_ref, *refs):
    count_ref, domain_ref, w_out_ref, *expert_refs, out_ref = refs
    users = len(expert_refs)
    width = embed_ref.shape[1]
    squares, mixed = mixed_part(width - kept_ref.shape[1], kept_ref, come_ref, gating_ref, gain_ref, w_out_ref)
    scale = lax.rsqrt((squares_ref[:, :1] + squares) / width + norm_eps)
    state = (embed_ref[...] + (mixed_ref[...] + mixed) * scale).astype(BF16)

    slots = state.shape[0]
    row_at = lax.broadcasted_iota(jnp.int32, (slots, slots), 0)
    lane_at = lax.broadcasted_iota(jnp.int32, (slots, slots), 1)
    steps_away = lax.rem(domain_ref[...] - lax.axis_index("user") + users, users)
    live = lane_at + lax.axis_index("hist") * slots < count_ref[0]
    wanted = jnp.where(live, steps_away, -1)
    owner = jnp.sum(jnp.where(row_at == lane_at, wanted, 0).astype(F32), axis=1, keepdims=True)

    result = jnp.zeros(state.shape, F32)
    for steps, layers in enumerate(expert_refs):
        current = state
        for layer in range(LAYERS):
            lifted = jnp.dot(current, layers[0, layer], preferred_element_type=F32)
            current = (current.astype(F32) + silu(lifted)).astype(BF16)
        result = jnp.where(owner == steps, current.astype(F32), result)
    out_ref[0] = result.astype(BF16)


def finish(pairs, embed, gating, gain, counts, domains, w_out, experts):
    slots, width = embed.shape
    first, last = pairs
    squares, mixed = mix(first, gating, gain, w_out)
    return kernel_call(
        finish_kernel,
        "finish",
        [jax.ShapeDtypeStruct((1, slots, width), BF16)],
        [VMEM] * 7 + [SMEM] + [VMEM] * (2 + len(experts)),
        flops=2 * slots * width * width * (1 + LAYERS * len(experts)),
    )(*last, squares, mixed, embed, gating, gain, counts, domains, w_out, *experts)[0]


def on_device(
    item_table,
    item_ids,
    candidate_counts,
    domain_ids,
    history_lengths,
    history_keys,
    history_values,
    w_query,
    w_gate,
    w_out,
    attn_gain,
    expert_weights,
):
    shard_rows = item_table.shape[0]
    hist_devices = lax.axis_size("hist")
    users = lax.axis_size("user")
    bits = hist_devices.bit_length() - 1
    others = range(1, users)

    shared = 1
    far = list(range(hist_devices // 2, hist_devices))
    far = [flip for pair in zip(far[::-1], far) for flip in pair][: len(far)]
    near = [flip for flip in range(1, hist_devices // 2) if flip != shared]
    far_flips = [tuple(far[at : at + users][:: (-1) ** (at // users)]) for at in range(0, len(far), users)]
    near_flips = [tuple(near[at : at + users]) for at in range(0, len(near), users)]
    far_shards = [swapped_by_user(item_table, flips) for flips in far_flips]
    near_shards = [swapped_by_user(item_table, flips) for flips in near_flips]
    shared_shard = swapped(item_table, shared)

    turns = [1] + list(range(2, bits)) + [0]
    far_ids, id_flips = swapped(item_ids, 1 << turns[0]), [0, 1 << turns[0]]

    first_pieces = [((flip,) * users, 0, None) for flip in (0, shared)] + [(flips, 0, None) for flips in near_flips]
    first_blocks = [item_table, shared_shard] + near_shards
    near_ids = stack([item_ids, far_ids], flops=LOADS_BESIDE)
    w_query, near_ids = lax.optimization_barrier((w_query, near_ids))
    first, masked_values = attend_first(
        first_pieces, first_blocks, shard_rows, history_lengths, w_query, history_keys, history_values
    )
    for bit in turns[1:]:
        far_ids = swapped(near_ids, 1 << bit)
        id_flips += [flip + (1 << bit) for flip in id_flips]
        if bit != turns[-1]:
            first, far_ids = lax.optimization_barrier((first, far_ids))
            near_ids = stack([near_ids, far_ids])
    first, *near_shards = lax.optimization_barrier((first, *near_shards))
    first, near_ids, *far_shards = lax.optimization_barrier((first, near_ids, *far_shards))
    next_pieces, next_blocks = [], []
    for flips, block in zip(near_flips + far_flips, near_shards + far_shards):
        arrivals = [block] + [from_user(block, steps) for steps in others]
        found = [(flips, steps, None) for steps in range(users)]
        if flips in near_flips:
            found = found[1:]
        elif len(flips) < users:
            found = [(flips, 0, core) for core in range(len(flips))]
        next_pieces += found
        next_blocks += [block for piece in found for block in blocks_of(piece, arrivals)]
    following = attend_next(next_pieces, next_blocks, shard_rows, w_query, history_keys, masked_values)
    pieces, blocks = first_pieces + next_pieces, first_blocks + next_blocks

    side_turns = [list(range(bits)), list(range(bits))]
    side_turns[1][:2] = [1, 0]
    orders = [
        [sum(((r >> (bits - 1 - t)) & 1) << bit for t, bit in enumerate(turn)) for r in range(hist_devices)]
        for turn in side_turns
    ]
    kept_a, sent_a, kept_b, sent_b = place(
        pieces, id_flips, orders, shard_rows, near_ids, far_ids, [first, following]
    )
    embed, gating = prepare(pieces, blocks, shard_rows, kept_a, item_ids, w_gate)

    leaving, kept_a = lax.optimization_barrier((expert_weights, kept_a))
    experts = [expert_weights] + [from_user(leaving, steps) for steps in others]

    held = [(kept_a, sent_a), (kept_b, sent_b)]
    for at in range(bits):
        arriving = [swapped(sent, 1 << turn[at]) for (_, sent), turn in zip(held, side_turns)]
        if at == 0:
            *arriving, embed = lax.optimization_barrier((*arriving, embed))
        pairs = [(kept, come) for (kept, _), come in zip(held, arriving)]
        if at < bits - 1:
            held = [fold([pair]) for pair in pairs]
    return finish(pairs, embed, gating, attn_gain[None], candidate_counts, domain_ids, w_out, experts)


def solution(mesh):
    in_specs = (
        P("hist", None),
        P(("groups", "user"), "hist"),
        P(("groups", "user")),
        P(("groups", "user"), "hist"),
        P(("groups", "user")),
        P(("groups", "user"), "hist", None),
        P(("groups", "user"), "hist", None),
        P(),
        P(),
        P(),
        P(),
        P("user", None, None, None),
    )
    out_specs = P(("groups", "user"), "hist", None)
    return jax.shard_map(
        on_device, mesh=mesh, in_specs=in_specs, out_specs=out_specs, check_vma=False
    )
```

```python
import functools

import jax
import jax.numpy as jnp
from jax import lax
from jax.experimental import pallas as pl
from jax.experimental.pallas import tpu as pltpu
from jax.sharding import PartitionSpec as P

H = 8
LAYERS = 2
VMEM_LIMIT = 24 * 1024 * 1024
LOADS_BESIDE = 8 * 10**9

norm_eps = 1e-05
F32 = jnp.float32
BF16 = jnp.bfloat16
ANY = pl.BlockSpec(memory_space=pl.ANY)
VMEM = pl.BlockSpec(memory_space=pltpu.VMEM)
SMEM = pl.BlockSpec(memory_space=pltpu.SMEM)
TRANSPOSED = (((0,), (0,)), ((), ()))


def rms_scale(matrix):
    return matrix * lax.rsqrt(jnp.mean(matrix * matrix, axis=-1, keepdims=True) + norm_eps)


def silu(value):
    half = 0.5 * value
    return half + half * jnp.tanh(half)


def swapped(value, flip):
    count = lax.axis_size("hist")
    return lax.ppermute(value, "hist", [(i, i ^ flip) for i in range(count)])


def swapped_by_user(value, flips):
    count = lax.axis_size("hist")
    pairs = [
        (u * count + i, u * count + (i ^ flip)) for u, flip in enumerate(flips) for i in range(count)
    ]
    return lax.ppermute(value, ("user", "hist"), pairs)


def from_user(value, steps):
    count = lax.axis_size("user")
    return lax.ppermute(value, "user", [((i + steps) % count, i) for i in range(count)])


def kernel_call(body, name, out_shapes, in_specs, scratch=(), flops=0, moved=0):
    return pl.pallas_call(
        body,
        out_shape=out_shapes,
        in_specs=in_specs,
        out_specs=[VMEM] * len(out_shapes),
        scratch_shapes=scratch,
        compiler_params=pltpu.CompilerParams(vmem_limit_bytes=VMEM_LIMIT),
        cost_estimate=pl.CostEstimate(flops=flops, bytes_accessed=moved, transcendentals=0),
        name=name,
    )


def core_at(steps):
    return lax.rem(lax.axis_index("user") + steps, lax.axis_size("user"))


def of_core(core, arrivals):
    chosen = arrivals[0]
    for steps in range(1, len(arrivals)):
        chosen = jnp.where(core_at(steps) == core, arrivals[steps], chosen)
    return chosen


def blocks_of(piece, arrivals):
    _, steps, core = piece
    return arrivals[steps : steps + 1] if core is None else arrivals


def flip_of(piece):
    flips, steps, core = piece
    if core is not None:
        return flips[core]
    return sum(jnp.where(core_at(steps) == u, flip, 0) for u, flip in enumerate(flips))


def rows_of(pieces, refs):
    blocks, at = [], 0
    for piece in pieces:
        count = 1 if piece[2] is None else lax.axis_size("user")
        shards = [ref[...] for ref in refs[at : at + count]]
        blocks.append(shards[0] if piece[2] is None else of_core(piece[2], shards))
        at += count
    return jnp.concatenate(blocks, axis=0)


def matches(pieces, shard_rows, ids_row):
    hist_index = lax.axis_index("hist")
    blocks = []
    for piece in pieces:
        item = lax.broadcasted_iota(jnp.int32, (shard_rows, ids_row.shape[1]), 0)
        item += (hist_index ^ flip_of(piece)) * shard_rows
        blocks.append((item == ids_row).astype(F32).astype(BF16))
    return jnp.concatenate(blocks, axis=0)


def first_ids_kernel(own_hbm, far_ref, out_ref, own_ref, sem):
    copy = pltpu.make_async_copy(own_hbm, own_ref, sem)
    copy.start()
    copy.wait()
    out_ref[:1, :] = own_ref[...]
    out_ref[1:, :] = far_ref[...]


def first_ids(own, far):
    return kernel_call(
        first_ids_kernel,
        "first_ids",
        [jax.ShapeDtypeStruct((2, own.shape[1]), own.dtype)],
        [ANY, VMEM],
        scratch=[pltpu.VMEM(own.shape, own.dtype), pltpu.SemaphoreType.DMA],
        flops=LOADS_BESIDE,
    )(own, far)[0]


def stack_kernel(*refs):
    *refs, out_ref = refs
    at = 0
    for ref in refs:
        out_ref[at : at + ref.shape[0], :] = ref[...]
        at += ref.shape[0]


def stack(blocks, flops=0):
    shape = (sum(block.shape[0] for block in blocks), blocks[0].shape[1])
    return kernel_call(
        stack_kernel, "stack", [jax.ShapeDtypeStruct(shape, blocks[0].dtype)], [VMEM] * len(blocks), flops=flops
    )(*blocks)[0]


def attend_rows(pieces, refs, w_query_ref, keys_ref, values_ref, sums_ref):
    width = sums_ref.shape[1]
    head_size = width // H
    rows = rows_of(pieces, refs)
    normed = rms_scale(rows.astype(F32)).astype(BF16)
    queries = jnp.dot(normed, w_query_ref[...], preferred_element_type=F32).astype(BF16)
    for head in range(H):
        cut = slice(head * head_size, (head + 1) * head_size)
        scores = lax.dot_general(
            queries[:, cut], keys_ref[0, :, cut], (((1,), (1,)), ((), ())), preferred_element_type=F32
        )
        half = scores * (0.5 * head_size ** (-0.5))
        weights = (half + half * jnp.tanh(half)).astype(BF16)
        sums_ref[:, cut] = jnp.dot(weights, values_ref[:, cut], preferred_element_type=F32).astype(BF16)


def first_kernel(pieces, length_ref, w_query_ref, keys_ref, values_ref, *refs):
    *refs, sums_ref, masked_ref = refs
    history = masked_ref.shape[0]
    place = lax.broadcasted_iota(jnp.int32, masked_ref.shape, 0) + lax.axis_index("hist") * history
    masked_ref[...] = jnp.where(place < length_ref[0], values_ref[0].astype(F32), 0.0).astype(BF16)
    attend_rows(pieces, refs, w_query_ref, keys_ref, masked_ref, sums_ref)


def next_kernel(pieces, w_query_ref, keys_ref, values_ref, *refs):
    *refs, sums_ref = refs
    attend_rows(pieces, refs, w_query_ref, keys_ref, values_ref, sums_ref)


def attend_cost(rows, width, history):
    return 2 * rows * width * (width + 2 * history)


def attend_first(pieces, blocks, shard_rows, lengths, w_query, keys, values):
    rows, width = len(pieces) * shard_rows, w_query.shape[0]
    return kernel_call(
        functools.partial(first_kernel, pieces),
        "attend_first",
        [jax.ShapeDtypeStruct((rows, width), BF16), jax.ShapeDtypeStruct(values.shape[1:], BF16)],
        [SMEM] + [VMEM] * (3 + len(blocks)),
        flops=attend_cost(rows, width, keys.shape[1]),
    )(lengths, w_query, keys, values, *blocks)


def attend_next(pieces, blocks, shard_rows, w_query, keys, values):
    rows, width = len(pieces) * shard_rows, w_query.shape[0]
    return kernel_call(
        functools.partial(next_kernel, pieces),
        "attend_next",
        [jax.ShapeDtypeStruct((rows, width), BF16)],
        [VMEM] * (3 + len(blocks)),
        flops=attend_cost(rows, width, keys.shape[1]),
    )(w_query, keys, values, *blocks)[0]


def place_kernel(pieces, id_flips, orders, shard_rows, near_ids_ref, far_ids_ref, *refs):
    *sums_refs, kept_a, sent_a, kept_b, sent_b = refs
    half, slots = near_ids_ref.shape
    rows = [id_flips.index(flip) for flip in orders[0]]
    refs_rows = [(near_ids_ref, row) if row < half else (far_ids_ref, row - half) for row in rows]
    ids_row = jnp.concatenate([ref[row : row + 1, :] for ref, row in refs_rows], axis=1)
    onehot = matches(pieces, shard_rows, ids_row)
    width = sums_refs[0].shape[1] // 2
    for side, order in enumerate(orders):
        columns = slice(side * width, (side + 1) * width)
        sums = jnp.concatenate([ref[:, columns] for ref in sums_refs], axis=0)
        placed = lax.dot_general(onehot, sums, TRANSPOSED, preferred_element_type=F32).astype(BF16)
        half = len(order) // 2
        for at, flip in enumerate(order):
            block = orders[0].index(flip)
            target = ((kept_a, sent_a), (kept_b, sent_b))[side][at // half]
            target[at % half * slots : (at % half + 1) * slots, :] = placed[block * slots : (block + 1) * slots, :]


def place(pieces, id_flips, orders, shard_rows, near_ids, far_ids, sums):
    devices, slots = len(orders[0]), near_ids.shape[1]
    width = sums[0].shape[1]
    out = jax.ShapeDtypeStruct((devices * slots // 2, width // 2), BF16)
    return kernel_call(
        functools.partial(place_kernel, pieces, id_flips, orders, shard_rows),
        "place",
        [out] * 4,
        [VMEM] * (2 + len(sums)),
        flops=2 * sum(part.shape[0] for part in sums) * devices * slots * width,
    )(near_ids, far_ids, *sums)


def fold_kernel(sides, *refs):
    ins, (kept_ref, sent_ref) = refs[: 2 * sides], refs[2 * sides :]
    half, width = ins[0].shape[0] // 2, ins[0].shape[1]
    for side in range(sides):
        total = ins[2 * side][...].astype(F32) + ins[2 * side + 1][...].astype(F32)
        columns = slice(side * width, (side + 1) * width)
        kept_ref[:, columns] = total[:half]
        sent_ref[:, columns] = total[half:].astype(BF16)


def fold(pairs):
    rows, width = pairs[0][0].shape
    shape = (rows // 2, width * len(pairs))
    blocks = [block for pair in pairs for block in pair]
    return kernel_call(
        functools.partial(fold_kernel, len(pairs)),
        "fold",
        [jax.ShapeDtypeStruct(shape, F32), jax.ShapeDtypeStruct(shape, BF16)],
        [VMEM] * len(blocks),
        moved=8 * rows * width * len(pairs),
    )(*blocks)


def prepare_kernel(pieces, after_ref, ids_ref, w_gate_ref, *refs):
    del after_ref
    *refs, embed_ref, gating_ref = refs
    table = rows_of(pieces, refs)
    onehot = matches(pieces, table.shape[0] // len(pieces), ids_ref[...])
    embedded = lax.dot_general(onehot, table, TRANSPOSED, preferred_element_type=F32)
    embed_ref[...] = embedded
    normed = rms_scale(embedded).astype(BF16)
    gating_ref[...] = silu(jnp.dot(normed, w_gate_ref[...], preferred_element_type=F32))


def prepare(pieces, blocks, shard_rows, after, ids, w_gate):
    slots, width = ids.shape[1], w_gate.shape[0]
    return kernel_call(
        functools.partial(prepare_kernel, pieces),
        "prepare",
        [jax.ShapeDtypeStruct((slots, width), F32)] * 2,
        [ANY, VMEM, VMEM] + [VMEM] * len(blocks),
        flops=2 * slots * width * (width + len(pieces) * shard_rows),
    )(after, ids, w_gate, *blocks)


def mixed_part(start, kept_ref, come_ref, gating_ref, gain_ref, w_out_ref):
    attended = kept_ref[...] + come_ref[...].astype(F32)
    columns = slice(start, start + attended.shape[1])
    gated = (attended * gain_ref[:, columns] * gating_ref[:, columns]).astype(BF16)
    squares = jnp.sum(attended * attended, axis=1, keepdims=True)
    return squares, jnp.dot(gated, w_out_ref[columns, :], preferred_element_type=F32)


def mix_kernel(kept_ref, come_ref, gating_ref, gain_ref, w_out_ref, squares_ref, mixed_ref):
    squares, mixed = mixed_part(0, kept_ref, come_ref, gating_ref, gain_ref, w_out_ref)
    squares_ref[...] = jnp.broadcast_to(squares, squares_ref.shape)
    mixed_ref[...] = mixed


def mix(pair, gating, gain, w_out):
    slots, width = gating.shape
    return kernel_call(
        mix_kernel,
        "mix",
        [jax.ShapeDtypeStruct((slots, 128), F32), jax.ShapeDtypeStruct((slots, width), F32)],
        [VMEM] * 5,
        flops=2 * slots * width * pair[0].shape[1],
    )(*pair, gating, gain, w_out)


def finish_kernel(kept_ref, come_ref, squares_ref, mixed_ref, embed_ref, gating_ref, gain_ref, *refs):
    count_ref, domain_ref, w_out_ref, *expert_refs, out_ref = refs
    users = len(expert_refs)
    width = embed_ref.shape[1]
    squares, mixed = mixed_part(width - kept_ref.shape[1], kept_ref, come_ref, gating_ref, gain_ref, w_out_ref)
    scale = lax.rsqrt((squares_ref[:, :1] + squares) / width + norm_eps)
    state = (embed_ref[...] + (mixed_ref[...] + mixed) * scale).astype(BF16)

    slots = state.shape[0]
    row_at = lax.broadcasted_iota(jnp.int32, (slots, slots), 0)
    lane_at = lax.broadcasted_iota(jnp.int32, (slots, slots), 1)
    steps_away = lax.rem(domain_ref[...] - lax.axis_index("user") + users, users)
    live = lane_at + lax.axis_index("hist") * slots < count_ref[0]
    wanted = jnp.where(live, steps_away, -1)
    owner = jnp.sum(jnp.where(row_at == lane_at, wanted, 0).astype(F32), axis=1, keepdims=True)

    result = jnp.zeros(state.shape, F32)
    for steps, layers in enumerate(expert_refs):
        current = state
        for layer in range(LAYERS):
            lifted = jnp.dot(current, layers[0, layer], preferred_element_type=F32)
            current = (current.astype(F32) + silu(lifted)).astype(BF16)
        result = jnp.where(owner == steps, current.astype(F32), result)
    out_ref[0] = result.astype(BF16)


def finish(pairs, embed, gating, gain, counts, domains, w_out, experts):
    slots, width = embed.shape
    first, last = pairs
    squares, mixed = mix(first, gating, gain, w_out)
    return kernel_call(
        finish_kernel,
        "finish",
        [jax.ShapeDtypeStruct((1, slots, width), BF16)],
        [VMEM] * 7 + [SMEM] + [VMEM] * (2 + len(experts)),
        flops=2 * slots * width * width * (1 + LAYERS * len(experts)),
    )(*last, squares, mixed, embed, gating, gain, counts, domains, w_out, *experts)[0]


def on_device(
    item_table,
    item_ids,
    candidate_counts,
    domain_ids,
    history_lengths,
    history_keys,
    history_values,
    w_query,
    w_gate,
    w_out,
    attn_gain,
    expert_weights,
):
    shard_rows = item_table.shape[0]
    hist_devices = lax.axis_size("hist")
    users = lax.axis_size("user")
    bits = hist_devices.bit_length() - 1
    others = range(1, users)

    shared = 1
    far = list(range(hist_devices // 2, hist_devices))
    far = [flip for pair in zip(far[::-1], far) for flip in pair][: len(far)]
    near = [flip for flip in range(1, hist_devices // 2) if flip != shared]
    far_flips = [tuple(far[at : at + users][:: (-1) ** (at // users)]) for at in range(0, len(far), users)]
    near_flips = [tuple(near[at : at + users]) for at in range(0, len(near), users)]
    far_shards = [swapped_by_user(item_table, flips) for flips in far_flips]
    near_shards = [swapped_by_user(item_table, flips) for flips in near_flips]
    shared_shard = swapped(item_table, shared)

    turns = [1] + list(range(2, bits)) + [0]
    far_ids, id_flips = swapped(item_ids, 1 << turns[0]), [0, 1 << turns[0]]

    first_pieces = [((flip,) * users, 0, None) for flip in (0, shared)] + [(flips, 0, None) for flips in near_flips]
    first_blocks = [item_table, shared_shard] + near_shards
    near_ids = first_ids(item_ids, far_ids)
    w_query, near_ids = lax.optimization_barrier((w_query, near_ids))
    first, masked_values = attend_first(
        first_pieces, first_blocks, shard_rows, history_lengths, w_query, history_keys, history_values
    )
    for bit in turns[1:]:
        far_ids = swapped(near_ids, 1 << bit)
        id_flips += [flip + (1 << bit) for flip in id_flips]
        if bit != turns[-1]:
            first, far_ids = lax.optimization_barrier((first, far_ids))
            near_ids = stack([near_ids, far_ids])
    first, *near_shards = lax.optimization_barrier((first, *near_shards))
    first, near_ids, *far_shards = lax.optimization_barrier((first, near_ids, *far_shards))
    next_pieces, next_blocks = [], []
    for flips, block in zip(near_flips + far_flips, near_shards + far_shards):
        arrivals = [block] + [from_user(block, steps) for steps in others]
        found = [(flips, steps, None) for steps in range(users)]
        if flips in near_flips:
            found = found[1:]
        elif len(flips) < users:
            found = [(flips, 0, core) for core in range(len(flips))]
        next_pieces += found
        next_blocks += [block for piece in found for block in blocks_of(piece, arrivals)]
    following = attend_next(next_pieces, next_blocks, shard_rows, w_query, history_keys, masked_values)
    pieces, blocks = first_pieces + next_pieces, first_blocks + next_blocks

    side_turns = [list(range(bits)), list(range(bits))]
    side_turns[1][:2] = [1, 0]
    orders = [
        [sum(((r >> (bits - 1 - t)) & 1) << bit for t, bit in enumerate(turn)) for r in range(hist_devices)]
        for turn in side_turns
    ]
    kept_a, sent_a, kept_b, sent_b = place(
        pieces, id_flips, orders, shard_rows, near_ids, far_ids, [first, following]
    )
    embed, gating = prepare(pieces, blocks, shard_rows, kept_a, item_ids, w_gate)

    leaving, kept_a = lax.optimization_barrier((expert_weights, kept_a))
    experts = [expert_weights] + [from_user(leaving, steps) for steps in others]

    held = [(kept_a, sent_a), (kept_b, sent_b)]
    for at in range(bits):
        arriving = [swapped(sent, 1 << turn[at]) for (_, sent), turn in zip(held, side_turns)]
        if at == 0:
            arriving[0], embed = lax.optimization_barrier((arriving[0], embed))
        pairs = [(kept, come) for (kept, _), come in zip(held, arriving)]
        if at < bits - 1:
            held = [fold([pair]) for pair in pairs]
    return finish(pairs, embed, gating, attn_gain[None], candidate_counts, domain_ids, w_out, experts)


def solution(mesh):
    in_specs = (
        P("hist", None),
        P(("groups", "user"), "hist"),
        P(("groups", "user")),
        P(("groups", "user"), "hist"),
        P(("groups", "user")),
        P(("groups", "user"), "hist", None),
        P(("groups", "user"), "hist", None),
        P(),
        P(),
        P(),
        P(),
        P("user", None, None, None),
    )
    out_specs = P(("groups", "user"), "hist", None)
    return jax.shard_map(
        on_device, mesh=mesh, in_specs=in_specs, out_specs=out_specs, check_vma=False
    )
```
